32 devices in a mesh: group: 2 (over x), seq: 16 (over z, y, core).
Axes of the slice: x: 2, y: 2, z: 4, core: 2. Of those that a mesh axis runs over, the one named last changes fastest.
Arguments:
- queries: bfloat16 [8192, 5120], P(('group', 'seq')), parts along dimension 0, may hold values from -30 to 30
- packed_keys: bfloat16 [8192, 5120], P(('group', 'seq')), parts along dimension 0, may hold values from -30 to 30
- packed_values: bfloat16 [8192, 5120], P(('group', 'seq')), parts along dimension 0, may hold values from -6 to 6
- clip_begin_position: int32 [8192], P(('group', 'seq')), parts along dimension 0, may hold values from 0 to 4095, as said below
- clip_stop_position: int32 [8192], P(('group', 'seq')), parts along dimension 0, may hold values from 1 to 4096
- adapter_down_factor: bfloat16 [5120, 128], P('seq'), may hold values from -6 to 6
- adapter_up_factor: bfloat16 [128, 5120], P(None, 'seq'), may hold values from -0.5 to 0.5
- frozen_projection: bfloat16 [5120, 5120], P('seq'), may hold values from -0.078125 to 0.078125
Outputs:
- attended: bfloat16 [8192, 5120], P(('group', 'seq')), parts along dimension 0
- merged_weight: bfloat16 [10240, 5120], P(('group', 'seq')), parts along dimension 0
The draws below stay inside these ranges and needn't reach their ends.
There are 2 independent parts, one for each index of `group`. The reference program is written for one: setup_inputs(seed, part) draws one part's arguments, and reference() takes and returns one part's arrays. A program takes and returns all parts, laid end to end along the dimension named above; an argument that names none is the same for every part. Nothing has to cross between parts.
Inputs may be any that keep to these rules, and one draw needn't show every extreme that they name: Each token lies in the run of positions [clip_begin_position, clip_stop_position) of its clip; clips are consecutive and cover all 4096 positions; each clip is a whole number of frames of 64 positions, at most 2 frames, except that the last clip may be cut by the end of the pack; one clip holds exactly 128 positions.
All inputs are finite; a program needn't handle non-finite values.
Results may differ from the reference program's by a relative error of at most 0.012.
Values may be sent and summed in bfloat16 or wider, within the bound.
No kernel may reach another device: no remote copies, remote signals or barrier semaphores. Data moves between devices by JAX's collectives and lax.ppermute only.
A program may use at most 192 MiB of HBM per device.

```python
import jax
import jax.numpy as jnp
from jax import lax

MODEL_WIDTH = 5120
HEADS = 40
HD = 128
ADAPTER_RANK = 128
FRAME_TOK = 64
FMAX = 2
TOK_DEV = 256
LMAX = 128
TOKENS = 4096


def draw_queries(key, part):
    key = jax.random.fold_in(key, 11)
    own = jax.random.normal(key, (TOKENS, MODEL_WIDTH), jnp.float32)
    return jnp.clip(own, -30.0, 30.0).astype(jnp.bfloat16)


def draw_packed_keys(key, part):
    key = jax.random.fold_in(key, 13)
    own = jax.random.normal(key, (TOKENS, MODEL_WIDTH), jnp.float32)
    return jnp.clip(own, -30.0, 30.0).astype(jnp.bfloat16)


def clip_bounds(key):
    key = jax.random.fold_in(key, 29)
    length_key, pick_key = jax.random.split(key)
    frames = jax.random.randint(length_key, (TOKENS,), 1, FMAX + 1).astype(jnp.int32)
    chosen = jax.random.randint(pick_key, (), 0, TOKENS // LMAX).astype(jnp.int32)
    places = jnp.arange(TOKENS, dtype=jnp.int32)
    frames = jnp.where(places == chosen, jnp.int32(FMAX), frames)
    lengths = (frames * FRAME_TOK).astype(jnp.int32)
    run_ends = jnp.cumsum(lengths).astype(jnp.int32)
    run_starts = run_ends - lengths
    which = jnp.searchsorted(run_ends, places, side='right').astype(jnp.int32)
    return (run_starts[which].astype(jnp.int32), jnp.minimum(run_ends[which], TOKENS).astype(jnp.int32))


def draw_clip_begin_position(key, part):
    bounds = clip_bounds(key)
    return bounds[0]


def draw_clip_stop_position(key, part):
    bounds = clip_bounds(key)
    return bounds[1]


def shard_levels(own_key, extent, shards, low, high):
    loudness = 1.0
    for dim, parts in shards:
        steps = jax.random.uniform(jax.random.fold_in(jax.random.fold_in(own_key, 6), dim), (parts,), jnp.float32, low / len(shards), high / len(shards))
        loudness = loudness * jnp.repeat(jnp.exp(steps), extent[dim] // parts).reshape((-1,) + (1,) * (len(extent) - 1 - dim))
    return loudness


def scatter_about(stream_key, dims, spread, limit, cuts=(), kind=jnp.bfloat16):
    drawn = spread * jax.random.normal(stream_key, dims, jnp.float32)
    if cuts:
        drawn = drawn * shard_levels(stream_key, dims, cuts, -0.22, 0.18)
    return jnp.clip(drawn, -limit, limit).astype(kind)


def setup_inputs(seed: int = 0, part: int = 0) -> dict:
    key_list = jax.random.split(jax.random.key(seed), 9)
    part_splits = jax.random.split(jax.random.fold_in(key_list[8], part), 9)
    return {
        "queries": draw_queries(jax.random.fold_in(jax.random.fold_in(key_list[8], part), 71), part),
        "packed_keys": draw_packed_keys(jax.random.fold_in(jax.random.fold_in(key_list[8], part), 71), part),
        "packed_values": scatter_about(part_splits[2], (TOKENS, MODEL_WIDTH), 1.0, 6.0, ((0, 16),)),
        "clip_begin_position": draw_clip_begin_position(jax.random.fold_in(jax.random.fold_in(key_list[8], part), 71), part),
        "clip_stop_position": draw_clip_stop_position(jax.random.fold_in(jax.random.fold_in(key_list[8], part), 71), part),
        "adapter_down_factor": scatter_about(key_list[5], (MODEL_WIDTH, ADAPTER_RANK), 1.0, 6.0, ((0, 16),)),
        "adapter_up_factor": scatter_about(key_list[6], (ADAPTER_RANK, MODEL_WIDTH), ADAPTER_RANK ** -0.5, 0.5, ((1, 16),)),
        "frozen_projection": scatter_about(key_list[7], (MODEL_WIDTH, MODEL_WIDTH), MODEL_WIDTH ** -0.5, 0.078125, ((0, 16),)),
    }


def attend(query_block, key_block, value_block, clip_lo, clip_hi, offset):
    query_rows = query_block.shape[0]
    key_count = key_block.shape[0]
    query_heads = query_block.astype(jnp.float32).reshape(query_rows, HEADS, HD)
    key_heads = key_block.astype(jnp.float32).reshape(key_count, HEADS, HD)
    value_heads = value_block.astype(jnp.float32).reshape(key_count, HEADS, HD)
    scores = jnp.einsum("thd,shd->hts", query_heads, key_heads) * (HD ** -0.5)
    position = offset + jnp.arange(key_count, dtype=jnp.int32)
    allowed = (position[None, :] >= clip_lo[:, None]) & (position[None, :] < clip_hi[:, None])
    scores = jnp.where(allowed[None], scores, jnp.float32(-1e30))
    highest = jnp.max(scores, axis=-1, keepdims=True)
    weights = jnp.exp(scores - highest)
    denominator = jnp.sum(weights, axis=-1, keepdims=True)
    weights_bf = (weights / denominator).astype(jnp.bfloat16)
    mixed = jnp.einsum("hts,shd->thd", weights_bf.astype(jnp.float32), value_heads)
    return mixed.reshape(query_rows, HEADS * HD).astype(jnp.bfloat16)


def reference(queries, packed_keys, packed_values, clip_begin_position, clip_stop_position, adapter_down_factor, adapter_up_factor, frozen_projection):
    total_rows = queries.shape[0]
    blocks = total_rows // TOK_DEV
    key_value = jnp.pad(jnp.stack([packed_keys, packed_values]), ((0, 0), (TOK_DEV, TOK_DEV), (0, 0)))

    def one_block(block_index):
        first_row = (block_index * TOK_DEV).astype(jnp.int32)
        query_block = lax.dynamic_slice_in_dim(queries, first_row, TOK_DEV, 0)
        window = lax.dynamic_slice_in_dim(key_value, first_row, 3 * TOK_DEV, 1)
        clip_lo = lax.dynamic_slice_in_dim(clip_begin_position, first_row, TOK_DEV, 0)
        clip_hi = lax.dynamic_slice_in_dim(clip_stop_position, first_row, TOK_DEV, 0)
        return attend(query_block, window[0], window[1], clip_lo, clip_hi, first_row - TOK_DEV)

    gathered_out = lax.map(one_block, jnp.arange(blocks, dtype=jnp.int32))
    clip_attention = gathered_out.reshape(total_rows, HEADS * HD)
    adapter_scale = MODEL_WIDTH ** -0.5
    summed_partial = jnp.dot(clip_attention, adapter_down_factor, preferred_element_type=jnp.float32).astype(jnp.bfloat16)
    weight_delta = jnp.dot(summed_partial, adapter_up_factor, preferred_element_type=jnp.float32)
    attended = (clip_attention.astype(jnp.float32) + adapter_scale * weight_delta).astype(jnp.bfloat16)
    factor_product = jnp.dot(adapter_down_factor, adapter_up_factor, preferred_element_type=jnp.float32)
    merged_weight = (frozen_projection.astype(jnp.float32) + adapter_scale * factor_product).astype(jnp.bfloat16)
    return attended, merged_weight
```

```python
import functools

import jax
import jax.numpy as jnp
from jax import lax
from jax.experimental import pallas as pl
from jax.experimental.pallas import tpu as pltpu
from jax.sharding import PartitionSpec as P

MODEL_WIDTH = 5120
HEADS = 40
HD = 128
FRAME = 64
CHUNK = 512
SCORE_SCALE = HD ** (-0.5) * 1.4426950408889634
ADAPTER_SCALE = MODEL_WIDTH ** (-0.5)
FAR = -1e30
NT = (((1,), (1,)), ((), ()))
NN = (((1,), (0,)), ((), ()))


def dot(a, b, dims):
    return lax.dot_general(a, b, dims, preferred_element_type=jnp.float32)


def softmax_mix(q, k, v, bias):
    scores = dot(q, k, NT) * SCORE_SCALE + bias
    weights = jnp.exp2(scores - jnp.max(scores, axis=-1, keepdims=True))
    total = jnp.sum(weights, axis=-1, keepdims=True)
    mixed = dot(weights.astype(jnp.bfloat16), v, NN)
    return (mixed * (1.0 / total)).astype(jnp.bfloat16)


def frame_bias(lo, hi, first, keys):
    position = first + lax.broadcasted_iota(jnp.int32, (FRAME, keys), 1)
    return jnp.where((position >= lo) & (position < hi), 0.0, FAR).astype(jnp.float32)


def local_kernel(lo_ref, hi_ref, q_ref, k_ref, v_ref, o_ref, bias_ref):
    rows = q_ref.shape[0]
    base = lax.axis_index("seq") * rows

    @pl.when(pl.program_id(0) == 0)
    def _():
        for at in range(0, rows, FRAME):
            bias_ref[at : at + FRAME, :] = frame_bias(lo_ref[at], hi_ref[at], base, rows)

    for col in range(0, CHUNK, HD):
        part = slice(col, col + HD)
        o_ref[:, part] = softmax_mix(q_ref[:, part], k_ref[:, part], v_ref[:, part], bias_ref[...])


def local_attention(lo, hi, q, k, v):
    rows, width = q.shape
    smem = pl.BlockSpec(memory_space=pltpu.SMEM)
    block = pl.BlockSpec((rows, CHUNK), lambda i: (0, i))
    return pl.pallas_call(
        local_kernel,
        grid=(width // CHUNK,),
        out_shape=jax.ShapeDtypeStruct((rows, width), jnp.bfloat16),
        in_specs=[smem, smem, block, block, block],
        out_specs=block,
        scratch_shapes=[pltpu.VMEM((rows, rows), jnp.float32)],
        compiler_params=pltpu.CompilerParams(vmem_limit_bytes=16 << 20),
        cost_estimate=pl.CostEstimate(
            flops=4 * rows * rows * width,
            bytes_accessed=8 * rows * width,
            transcendentals=rows * rows * HEADS,
        ),
        name="local_attention",
    )(lo, hi, q, k, v)


def piece_copies(pieces, half, shard, whole, sems):
    me = lax.axis_index("seq")
    copies = []
    for mask, ref, where in pieces:
        source = ref.at[where] if where is not None else ref
        start = pl.multiple_of((me ^ mask) * shard, shard)
        copies.append(
            pltpu.make_async_copy(
                source.at[pl.ds(half * shard, shard)],
                whole.at[pl.ds(start, shard)],
                sems.at[len(copies)],
            )
        )
    return copies


def merge_kernel(layout, shard, frozen_ref, down_ref, *rest):
    refs = rest[: len(rest) - 3]
    out_ref, up_ref, sems = rest[len(rest) - 3 :]

    @pl.when(pl.program_id(0) == 0)
    def _():
        pieces = [(mask, refs[i], where) for mask, i, where in layout]
        copies = piece_copies(pieces, 1, shard, up_ref, sems)
        for copy in copies:
            copy.start()
        for copy in copies:
            copy.wait()

    first = pl.multiple_of(pl.program_id(0) * CHUNK, CHUNK)
    product = dot(down_ref[...], up_ref[pl.ds(first, CHUNK), :], NT)
    out_ref[...] = (frozen_ref[...].astype(jnp.float32) + ADAPTER_SCALE * product).astype(
        jnp.bfloat16
    )


def merge(frozen, down, layout, pieces):
    shard, width = frozen.shape
    rank = down.shape[1]
    block = pl.BlockSpec((shard, CHUNK), lambda i: (0, i))
    return pl.pallas_call(
        functools.partial(merge_kernel, layout, shard),
        grid=(width // CHUNK,),
        out_shape=jax.ShapeDtypeStruct((shard, width), jnp.bfloat16),
        in_specs=[block, pl.BlockSpec((shard, rank), lambda i: (0, 0))]
        + [pl.BlockSpec(memory_space=pl.ANY)] * len(pieces),
        out_specs=block,
        scratch_shapes=[
            pltpu.VMEM((width, rank), jnp.bfloat16),
            pltpu.SemaphoreType.DMA((len(layout),)),
        ],
        compiler_params=pltpu.CompilerParams(vmem_limit_bytes=16 << 20),
        cost_estimate=pl.CostEstimate(
            flops=2 * shard * width * rank,
            bytes_accessed=4 * shard * width + 2 * width * rank,
            transcendentals=0,
        ),
        name="merge_weight",
    )(frozen, down, *pieces)


def final_kernel(layout, shard, lo_ref, hi_ref, q, k, v, att, k_left, v_left, k_right, v_right, *rest):
    refs = rest[: len(rest) - 11]
    (
        out,
        q_edge,
        k_edge,
        v_edge,
        mixed,
        result,
        down,
        up,
        reduced,
        piece_sems,
        sems,
    ) = rest[len(rest) - 11 :]
    rows, width = q.shape
    near = 2 * FRAME
    base = lax.axis_index("seq") * rows
    pieces = [(mask, refs[i], where) for mask, i, where in layout]

    def local(source, target, i):
        return pltpu.make_async_copy(source, target, sems.at[i])

    head, tail = pl.ds(0, FRAME), pl.ds(rows - FRAME, FRAME)
    front, back = pl.ds(0, near), pl.ds(rows - near, near)
    edges = [
        local(q.at[head], q_edge.at[0], 0),
        local(q.at[tail], q_edge.at[1], 1),
        local(k_left, k_edge.at[0, pl.ds(0, FRAME)], 2),
        local(k.at[front], k_edge.at[0, pl.ds(FRAME, near)], 3),
        local(k.at[back], k_edge.at[1, pl.ds(0, near)], 4),
        local(k_right, k_edge.at[1, pl.ds(near, FRAME)], 5),
        local(v_left, v_edge.at[0, pl.ds(0, FRAME)], 6),
        local(v.at[front], v_edge.at[0, pl.ds(FRAME, near)], 7),
        local(v.at[back], v_edge.at[1, pl.ds(0, near)], 8),
        local(v_right, v_edge.at[1, pl.ds(near, FRAME)], 9),
        local(att.at[pl.ds(FRAME, rows - near)], mixed.at[pl.ds(FRAME, rows - near)], 10),
    ]
    downs = piece_copies(pieces, 0, shard, down, piece_sems.at[0])
    ups = piece_copies(pieces, 1, shard, up, piece_sems.at[1])
    for copy in edges + downs + ups:
        copy.start()
    bias = [
        frame_bias(lo_ref[0], hi_ref[0], base - FRAME, near + FRAME),
        frame_bias(lo_ref[rows - FRAME], hi_ref[rows - FRAME], base + rows - near, near + FRAME),
    ]
    reduced[...] = jnp.zeros_like(reduced)
    for copy in edges + downs:
        copy.wait()

    def attend(step, _):
        for col in range(0, CHUNK, HD):
            part = pl.ds(pl.multiple_of(step * CHUNK + col, HD), HD)
            for e, row in ((0, 0), (1, rows - FRAME)):
                mixed[row : row + FRAME, part] = softmax_mix(
                    q_edge[e, :, part], k_edge[e, :, part], v_edge[e, :, part], bias[e]
                )
        wide = pl.ds(pl.multiple_of(step * CHUNK, CHUNK), CHUNK)
        reduced[...] += dot(mixed[:, wide], down[wide, :], NN)
        return 0

    steps = width // CHUNK
    lax.fori_loop(0, steps, attend, 0)
    for copy in ups:
        copy.wait()
    narrow = reduced[...].astype(jnp.bfloat16)
    stores = []
    for step in range(steps):
        wide = pl.ds(step * CHUNK, CHUNK)
        delta = dot(narrow, up[wide, :], NT)
        result[:, wide] = (mixed[:, wide].astype(jnp.float32) + ADAPTER_SCALE * delta).astype(
            jnp.bfloat16
        )
        store = local(result.at[:, wide], out.at[:, wide], 11 + step)
        store.start()
        stores.append(store)
    for store in stores:
        store.wait()


def final(lo, hi, q, k, v, att, halos, layout, pieces, shard):
    rows, width = q.shape
    rank = pieces[0].shape[-1]
    any_spec = pl.BlockSpec(memory_space=pl.ANY)
    smem = pl.BlockSpec(memory_space=pltpu.SMEM)
    window = 3 * FRAME
    bf16 = jnp.bfloat16
    return pl.pallas_call(
        functools.partial(final_kernel, layout, shard),
        out_shape=jax.ShapeDtypeStruct((rows, width), bf16),
        in_specs=[smem, smem] + [any_spec] * (8 + len(pieces)),
        out_specs=any_spec,
        scratch_shapes=[
            pltpu.VMEM((2, FRAME, width), bf16),
            pltpu.VMEM((2, window, width), bf16),
            pltpu.VMEM((2, window, width), bf16),
            pltpu.VMEM((rows, width), bf16),
            pltpu.VMEM((rows, width), bf16),
            pltpu.VMEM((width, rank), bf16),
            pltpu.VMEM((width, rank), bf16),
            pltpu.VMEM((rows, rank), jnp.float32),
            pltpu.SemaphoreType.DMA((2, len(layout))),
            pltpu.SemaphoreType.DMA((11 + width // CHUNK,)),
        ],
        compiler_params=pltpu.CompilerParams(vmem_limit_bytes=32 << 20),
        cost_estimate=pl.CostEstimate(
            flops=4 * rows * width * rank + 8 * FRAME * window * width,
            bytes_accessed=14 * rows * width,
            transcendentals=2 * FRAME * window * HEADS,
        ),
        name="edge_attention_adapter",
    )(lo, hi, q, k, v, att, *halos, *pieces)


def gather_pieces(own, axis):
    count = lax.axis_size(axis)
    if own.shape[0] % 32:
        full = lax.all_gather(own, axis, axis=0)
        me = lax.axis_index(axis)
        order = jnp.arange(count, dtype=jnp.int32) ^ me
        return [(mask, 0, mask) for mask in range(count)], [full[order]]

    def swap(cells, mask):
        return lax.ppermute(cells, axis, [(i, i ^ mask) for i in range(count)])

    groups = []
    bit = count
    while bit > 4:
        low = max(bit // 4, 4)
        groups.append([low * j for j in range(1, bit // low)])
        bit = low
    while bit > 1:
        bit //= 2
        groups.append([bit])
    cells, masks = own[None], [0]
    for group in groups[:-1]:
        cells = jnp.concatenate([cells] + [swap(cells, mask) for mask in group])
        masks = masks + [have ^ mask for mask in group for have in masks]
    last = groups[-1][0]
    far = swap(cells, last)
    layout = [(mask, 0, i) for i, mask in enumerate(masks)]
    layout += [(mask ^ last, 1, i) for i, mask in enumerate(masks)]
    return layout, [cells, far]


def body(q, k, v, lo, hi, down, up, frozen):
    shard = down.shape[0]
    count = lax.axis_size("seq")
    layout, pieces = gather_pieces(jnp.concatenate([down, up.T]), "seq")
    forward = [(i, i + 1) for i in range(count - 1)]
    backward = [(i + 1, i) for i in range(count - 1)]
    rows = q.shape[0]
    k_left = lax.ppermute(k[rows - FRAME :], "seq", forward)
    v_left = lax.ppermute(v[rows - FRAME :], "seq", forward)
    k_right = lax.ppermute(k[:FRAME], "seq", backward)
    v_right = lax.ppermute(v[:FRAME], "seq", backward)
    att = local_attention(lo, hi, q, k, v)
    merged = merge(frozen, down, layout, pieces)
    attended = final(
        lo, hi, q, k, v, att, (k_left, v_left, k_right, v_right), layout, pieces, shard
    )
    return (attended, merged)


def solution(mesh):
    rows = P(("group", "seq"), None)
    flat = P(("group", "seq"))
    return jax.shard_map(
        body,
        mesh=mesh,
        in_specs=(rows, rows, rows, flat, flat, P("seq", None), P(None, "seq"), P("seq", None)),
        out_specs=(rows, rows),
        check_vma=False,
    )
```

```python
import functools

import jax
import jax.numpy as jnp
from jax import lax
from jax.experimental import pallas as pl
from jax.experimental.pallas import tpu as pltpu
from jax.sharding import PartitionSpec as P

MODEL_WIDTH = 5120
HEADS = 40
HD = 128
FRAME = 64
NEAR = 2 * FRAME
WINDOW = 3 * FRAME
CHUNK = 512
SCORE_SCALE = HD ** (-0.5) * 1.4426950408889634
ADAPTER_SCALE = MODEL_WIDTH ** (-0.5)
FAR = -1e30
NT = (((1,), (1,)), ((), ()))
NN = (((1,), (0,)), ((), ()))
BF16 = jnp.bfloat16
ANY = pl.BlockSpec(memory_space=pl.ANY)
SMEM = pl.BlockSpec(memory_space=pltpu.SMEM)


def dot(a, b, dims):
    return lax.dot_general(a, b, dims, preferred_element_type=jnp.float32)


def clip_bias(lo, hi):
    return jnp.where(
        lax.broadcasted_iota(jnp.int32, (FRAME, NEAR), 1) < hi - lo, 0.0, FAR
    ).astype(jnp.float32)


def attend(blocks):
    scores = [dot(q(), k(), NT) * SCORE_SCALE + bias for q, k, _, bias, _ in blocks]
    peaks = [jnp.max(s, axis=-1, keepdims=True) for s in scores]
    weights = [jnp.exp2(s - m) for s, m in zip(scores, peaks)]
    totals = [jnp.sum(w, axis=-1, keepdims=True) for w in weights]
    mixed = [dot(w.astype(BF16), block[2](), NN) for w, block in zip(weights, blocks)]
    for block, mix, total in zip(blocks, mixed, totals):
        block[4]((mix * (1.0 / total)).astype(BF16))


def local_kernel(lo_ref, hi_ref, q_ref, k_ref, v_ref, o_ref):
    rows = q_ref.shape[0]
    base = lax.axis_index("seq") * rows
    blocks = []
    for row in range(FRAME, rows - FRAME, FRAME):
        lo, hi = lo_ref[row], hi_ref[row]
        keys = pl.ds(pl.multiple_of(lo - base, FRAME), NEAR)
        bias = clip_bias(lo, hi)
        for col in range(0, CHUNK, HD):
            part = slice(col, col + HD)

            def put(value, at=row - FRAME, part=part):
                o_ref[at : at + FRAME, part] = value

            blocks.append(
                (
                    lambda row=row, part=part: q_ref[row : row + FRAME, part],
                    lambda keys=keys, part=part: k_ref[keys, part],
                    lambda keys=keys, part=part: v_ref[keys, part],
                    bias,
                    put,
                )
            )
    attend(blocks)


def local_attention(lo, hi, q, k, v):
    rows, width = q.shape
    inner = rows - NEAR
    block = pl.BlockSpec((rows, CHUNK), lambda i: (0, i))
    return pl.pallas_call(
        local_kernel,
        grid=(width // CHUNK,),
        out_shape=jax.ShapeDtypeStruct((inner, width), BF16),
        in_specs=[SMEM, SMEM, block, block, block],
        out_specs=pl.BlockSpec((inner, CHUNK), lambda i: (0, i)),
        compiler_params=pltpu.CompilerParams(vmem_limit_bytes=16 << 20),
        cost_estimate=pl.CostEstimate(
            flops=4 * inner * NEAR * width,
            bytes_accessed=7 * rows * width,
            transcendentals=inner * NEAR * HEADS,
        ),
        name="local_attention",
    )(lo, hi, q, k, v)


def merge_kernel(layout, frozen, own_down, att, *rest):
    refs, rest = rest[: len(layout)], rest[len(layout) :]
    merged, attended, down, up, w, a, mixed, inner, sems, in_sems, out_sems = rest
    shard, width = frozen.shape
    me = lax.axis_index("seq")
    kind = lax.axis_index("group")
    loads = [
        pltpu.make_async_copy(own_down, a, in_sems.at[0]),
        pltpu.make_async_copy(att, mixed, in_sems.at[1]),
        pltpu.make_async_copy(frozen, w, in_sems.at[2]),
    ]
    pieces = []
    for ref, (swapped, masks) in zip(refs, layout):
        for i, mask in enumerate(masks):
            rows = pl.ds(pl.multiple_of((me ^ mask) * shard, shard), shard)
            pieces.append((swapped, ref.at[i], rows))
    for this, other, up_swapped in ((down, up, 1), (up, down, 0)):
        first_kind = 1 - up_swapped

        @pl.when(kind == first_kind)
        def _(this=this, other=other):
            for n, (swapped, source, rows) in enumerate(pieces):
                target = (other if swapped else this).at[rows]
                pltpu.make_async_copy(source, target, sems.at[n]).start()

    for copy in loads:
        copy.start()
    for n, (_, source, rows) in enumerate(pieces):
        pltpu.make_async_copy(source, down.at[rows], sems.at[n]).wait()
    for copy in loads:
        copy.wait()
    reduced = dot(mixed[...], down[...], NN).astype(BF16)
    stores = []
    for step in range(width // CHUNK):
        part = pl.ds(step * CHUNK, CHUNK)
        factor = up[part, :]
        delta = dot(reduced, factor, NT)
        inner[:, part] = (mixed[:, part].astype(jnp.float32) + ADAPTER_SCALE * delta).astype(BF16)
        product = dot(a[...], factor, NT)
        w[:, part] = (w[:, part].astype(jnp.float32) + ADAPTER_SCALE * product).astype(BF16)
        rows = pl.ds(FRAME, inner.shape[0])
        stores += [
            pltpu.make_async_copy(w.at[:, part], merged.at[:, part], out_sems.at[2 * step]),
            pltpu.make_async_copy(
                inner.at[:, part], attended.at[rows, part], out_sems.at[2 * step + 1]
            ),
        ]
        stores[-1].start()
        stores[-2].start()
    for store in stores:
        store.wait()


def merge(frozen, own_down, att, layout, pieces):
    shard, width = frozen.shape
    rank = own_down.shape[1]
    inner = att.shape[0]
    count = sum(len(masks) for _, masks in layout)
    whole = pl.BlockSpec(memory_space=pltpu.VMEM)
    factor = jax.ShapeDtypeStruct((width, rank), BF16)
    return pl.pallas_call(
        functools.partial(merge_kernel, layout),
        out_shape=(
            jax.ShapeDtypeStruct((shard, width), BF16),
            jax.ShapeDtypeStruct((inner + NEAR, width), BF16),
            factor,
            factor,
        ),
        in_specs=[ANY] * (3 + len(pieces)),
        out_specs=(ANY, ANY, whole, whole),
        scratch_shapes=[
            pltpu.VMEM((shard, width), BF16),
            pltpu.VMEM((shard, rank), BF16),
            pltpu.VMEM((inner, width), BF16),
            pltpu.VMEM((inner, width), BF16),
            pltpu.SemaphoreType.DMA((count,)),
            pltpu.SemaphoreType.DMA((3,)),
            pltpu.SemaphoreType.DMA((2 * (width // CHUNK),)),
        ],
        compiler_params=pltpu.CompilerParams(vmem_limit_bytes=20 << 20),
        cost_estimate=pl.CostEstimate(
            flops=2 * shard * width * rank + 4 * inner * width * rank,
            bytes_accessed=4 * shard * width + 4 * inner * width + 8 * width * rank,
            transcendentals=0,
        ),
        name="merge_and_inner_adapter",
    )(frozen, own_down, att, *pieces)


def edge_kernel(lo_ref, hi_ref, q, k, v, left, right, down, up, _, out, *scratch):
    q_edge, k_edge, v_edge, a, b, mixed, result, reduced, sems, b_sem, out_sems = scratch
    rows, width = q.shape
    span = width // sems.shape[0]
    base = lax.axis_index("seq") * rows
    loads = []
    for n in range(width // span):
        part = pl.ds(n * span, span)
        moves = [
            (q.at[pl.ds(0, FRAME), part], q_edge.at[0, :, part]),
            (q.at[pl.ds(rows - FRAME, FRAME), part], q_edge.at[1, :, part]),
            (left.at[0, :, part], k_edge.at[0, pl.ds(0, FRAME), part]),
            (k.at[pl.ds(0, NEAR), part], k_edge.at[0, pl.ds(FRAME, NEAR), part]),
            (k.at[pl.ds(rows - NEAR, NEAR), part], k_edge.at[1, pl.ds(0, NEAR), part]),
            (right.at[0, :, part], k_edge.at[1, pl.ds(NEAR, FRAME), part]),
            (left.at[1, :, part], v_edge.at[0, pl.ds(0, FRAME), part]),
            (v.at[pl.ds(0, NEAR), part], v_edge.at[0, pl.ds(FRAME, NEAR), part]),
            (v.at[pl.ds(rows - NEAR, NEAR), part], v_edge.at[1, pl.ds(0, NEAR), part]),
            (right.at[1, :, part], v_edge.at[1, pl.ds(NEAR, FRAME), part]),
            (down.at[part], a.at[part]),
        ]
        loads.append(
            [pltpu.make_async_copy(s, t, sems.at[n, i]) for i, (s, t) in enumerate(moves)]
        )
    for group in loads:
        for copy in group:
            copy.start()
    load_up = pltpu.make_async_copy(up, b, b_sem.at[0])
    load_up.start()
    keys, biases = [], []
    for row, first in ((0, base - FRAME), (rows - FRAME, base + rows - NEAR)):
        lo, hi = lo_ref[row], hi_ref[row]
        keys.append(pl.ds(pl.multiple_of(lo - first, FRAME), NEAR))
        biases.append(clip_bias(lo, hi))
    reduced[...] = jnp.zeros_like(reduced)
    for n, group in enumerate(loads):
        for copy in group:
            copy.wait()

        def step(i, _, first=n * span):
            start = first + i * CHUNK
            blocks = []
            for col in range(0, CHUNK, HD):
                part = pl.ds(pl.multiple_of(start + col, HD), HD)
                for e in range(2):

                    def put(value, e=e, part=part):
                        mixed[e * FRAME : (e + 1) * FRAME, part] = value

                    blocks.append(
                        (
                            lambda e=e, part=part: q_edge[e, :, part],
                            lambda e=e, part=part: k_edge[e, keys[e], part],
                            lambda e=e, part=part: v_edge[e, keys[e], part],
                            biases[e],
                            put,
                        )
                    )
            attend(blocks)
            wide = pl.ds(pl.multiple_of(start, CHUNK), CHUNK)
            reduced[...] += dot(mixed[:, wide], a[wide, :], NN)
            return 0

        lax.fori_loop(0, span // CHUNK, step, 0)
    load_up.wait()
    narrow = reduced[...].astype(BF16)
    stores = []
    for n in range(width // CHUNK):
        part = pl.ds(n * CHUNK, CHUNK)
        delta = dot(narrow, b[part, :], NT)
        result[:, part] = (mixed[:, part].astype(jnp.float32) + ADAPTER_SCALE * delta).astype(BF16)
        for e, row in ((0, 0), (1, rows - FRAME)):
            stores.append(
                pltpu.make_async_copy(
                    result.at[pl.ds(e * FRAME, FRAME), part],
                    out.at[pl.ds(row, FRAME), part],
                    out_sems.at[2 * n + e],
                )
            )
            stores[-1].start()
    for store in stores:
        store.wait()


def edge(lo, hi, q, k, v, left, right, down, up, attended):
    rows, width = q.shape
    rank = down.shape[1]
    return pl.pallas_call(
        edge_kernel,
        out_shape=jax.ShapeDtypeStruct((rows, width), BF16),
        in_specs=[SMEM, SMEM] + [ANY] * 8,
        out_specs=ANY,
        input_output_aliases={9: 0},
        scratch_shapes=[
            pltpu.VMEM((2, FRAME, width), BF16),
            pltpu.VMEM((2, WINDOW, width), BF16),
            pltpu.VMEM((2, WINDOW, width), BF16),
            pltpu.VMEM((width, rank), BF16),
            pltpu.VMEM((width, rank), BF16),
            pltpu.VMEM((NEAR, width), BF16),
            pltpu.VMEM((NEAR, width), BF16),
            pltpu.VMEM((NEAR, rank), jnp.float32),
            pltpu.SemaphoreType.DMA((width // (2 * CHUNK), 11)),
            pltpu.SemaphoreType.DMA((1,)),
            pltpu.SemaphoreType.DMA((2 * (width // CHUNK),)),
        ],
        compiler_params=pltpu.CompilerParams(vmem_limit_bytes=24 << 20),
        cost_estimate=pl.CostEstimate(
            flops=4 * NEAR * width * (NEAR + rank),
            bytes_accessed=24 * FRAME * width + 4 * rank * width,
            transcendentals=NEAR * NEAR * HEADS,
        ),
        name="edge_attention_adapter",
    )(lo, hi, q, k, v, left, right, down, up, attended)


def gather_factors(down, up):
    count = lax.axis_size("seq")
    if lax.axis_size("group") != 2 or down.shape[0] % 32:
        both = lax.all_gather(jnp.stack([down, up]), "seq", axis=1)
        kind = lax.axis_index("group")
        order = jnp.arange(count, dtype=jnp.int32) ^ lax.axis_index("seq")
        both = both[:, order]
        masks = list(range(count))
        return [(0, masks), (1, masks)], [both[kind], both[1 - kind]]

    def swap(cells, mask):
        return lax.ppermute(cells, "seq", [(i, i ^ mask) for i in range(count)])

    cells = jnp.where(lax.axis_index("group") == 0, down, up)[None]
    masks = [0]
    low = 2
    while low < count:
        bits = 1 if (count // low).bit_length() % 2 == 0 else 2
        steps = [low * j for j in range(1, 1 << bits)]
        cells = jnp.concatenate([cells] + [swap(cells, mask) for mask in steps])
        masks = masks + [have ^ mask for mask in steps for have in masks]
        low <<= bits
    other = lax.ppermute(cells, "group", [(0, 1), (1, 0)])
    across = [mask ^ 1 for mask in masks]
    return (
        [(0, masks), (0, across), (1, masks), (1, across)],
        [cells, swap(cells, 1), other, swap(other, 1)],
    )


def body(q, k, v, lo, hi, down, up, frozen):
    count = lax.axis_size("seq")
    rows = q.shape[0]
    layout, pieces = gather_factors(down, up.T)
    tails = jnp.stack([k[rows - FRAME :], v[rows - FRAME :]])
    heads = jnp.stack([k[:FRAME], v[:FRAME]])
    left = lax.ppermute(tails, "seq", [(i, i + 1) for i in range(count - 1)])
    right = lax.ppermute(heads, "seq", [(i + 1, i) for i in range(count - 1)])
    att = local_attention(lo, hi, q, k, v)
    merged, attended, down_full, up_full = merge(frozen, down, att, layout, pieces)
    attended = edge(lo, hi, q, k, v, left, right, down_full, up_full, attended)
    return (attended, merged)


def solution(mesh):
    rows = P(("group", "seq"), None)
    flat = P(("group", "seq"))
    return jax.shard_map(
        body,
        mesh=mesh,
        in_specs=(rows, rows, rows, flat, flat, P("seq", None), P(None, "seq"), P("seq", None)),
        out_specs=(rows, rows),
        check_vma=False,
    )
```

```python
import functools

import jax
import jax.numpy as jnp
from jax import lax
from jax.experimental import pallas as pl
from jax.experimental.pallas import tpu as pltpu
from jax.sharding import PartitionSpec as P

MODEL_WIDTH = 5120
HEADS = 40
HD = 128
FRAME = 64
NEAR = 2 * FRAME
CHUNK = 512
SCORE_SCALE = HD ** (-0.5) * 1.4426950408889634
ADAPTER_SCALE = MODEL_WIDTH ** (-0.5)
FAR = -1e30
NT = (((1,), (1,)), ((), ()))
NN = (((1,), (0,)), ((), ()))
BF16 = jnp.bfloat16
F32 = jnp.float32
ANY = pl.BlockSpec(memory_space=pl.ANY)
SMEM = pl.BlockSpec(memory_space=pltpu.SMEM)
VMEM = pl.BlockSpec(memory_space=pltpu.VMEM)


def dot(a, b, dims):
    return lax.dot_general(a, b, dims, preferred_element_type=F32)


def clip_bias(first, second):
    lengths = [hi - lo for lo, hi in (first, second)]
    position = lax.broadcasted_iota(jnp.int32, (FRAME, NEAR), 1)
    return jnp.concatenate([jnp.where(position < n, 0.0, FAR).astype(F32) for n in lengths])


def diagonal(top, bottom):
    zeros = jnp.zeros((FRAME, NEAR), BF16)
    return jnp.concatenate(
        [jnp.concatenate([top, zeros], axis=1), jnp.concatenate([zeros, bottom], axis=1)]
    )


def attend(loads, bias):
    ones = jnp.ones((NEAR, HD), BF16)
    scores = []
    for load_q, load_k, _ in loads:
        keys = jnp.concatenate(load_k(), axis=1)
        scores.append(dot(diagonal(*load_q()), keys, NT) * SCORE_SCALE + bias)
    weights = [jnp.exp2(s - jnp.max(s, axis=-1, keepdims=True)).astype(BF16) for s in scores]
    results = []
    for w, (_, _, load_v) in zip(weights, loads):
        values = jnp.concatenate([jnp.concatenate([v, ones], axis=1) for v in load_v()])
        mixed = dot(diagonal(w[:FRAME], w[FRAME:]), values, NN)
        results.append((mixed[:, :HD] * (1.0 / mixed[:, HD:])).astype(BF16))
    return results


def inner_kernel(lo_ref, hi_ref, q_ref, k_ref, v_ref, o_ref):
    rows = q_ref.shape[0]
    base = lax.axis_index("seq") * rows
    clips = [(lo_ref[row], hi_ref[row]) for row in (FRAME, NEAR)]
    keys = [pl.ds(pl.multiple_of(lo - base, FRAME), NEAR) for lo, _ in clips]
    loads, parts = [], []
    for col in range(0, CHUNK, HD):
        part = slice(col, col + HD)
        parts.append(part)
        loads.append(
            (
                lambda part=part: [q_ref[at : at + FRAME, part] for at in (FRAME, NEAR)],
                lambda part=part: [k_ref[at, part] for at in keys],
                lambda part=part: [v_ref[at, part] for at in keys],
            )
        )
    for part, result in zip(parts, attend(loads, clip_bias(*clips))):
        o_ref[:, part] = result


def inner_attention(lo, hi, q, k, v):
    rows, width = q.shape
    block = pl.BlockSpec((rows, CHUNK), lambda i: (0, i))
    return pl.pallas_call(
        inner_kernel,
        grid=(width // CHUNK,),
        out_shape=jax.ShapeDtypeStruct((NEAR, width), BF16),
        in_specs=[SMEM, SMEM, block, block, block],
        out_specs=pl.BlockSpec((NEAR, CHUNK), lambda i: (0, i)),
        compiler_params=pltpu.CompilerParams(vmem_limit_bytes=16 << 20),
        cost_estimate=pl.CostEstimate(
            flops=16 * NEAR * NEAR * width,
            bytes_accessed=7 * rows * width,
            transcendentals=NEAR * NEAR * HEADS,
        ),
        name="inner_attention",
    )(lo, hi, q, k, v)


def edge_kernel(lo_ref, hi_ref, q, k, v, far, near, out):
    rows, width = q.shape
    me = lax.axis_index("seq")
    base = me * rows
    even = lax.rem(me, 2) == 0
    clips = [(lo_ref[row], hi_ref[row]) for row in (0, rows - FRAME)]
    crosses = [clips[0][0] < base, clips[1][1] > base + rows]
    tail = rows - NEAR

    def window(ref, kind, part):
        away, close = far[kind, :, part], near[kind, :, part]
        first, second = ref[0:FRAME, part], ref[FRAME:NEAR, part]
        third, fourth = ref[tail : tail + FRAME, part], ref[tail + FRAME : rows, part]
        left, right = jnp.where(even, away, close), jnp.where(even, close, away)
        inside = clips[1][0] < base + rows - FRAME
        return [
            jnp.concatenate(
                [jnp.where(crosses[0], left, first), jnp.where(crosses[0], first, second)]
            ),
            jnp.concatenate(
                [jnp.where(inside, third, fourth), jnp.where(inside, fourth, right)]
            ),
        ]

    bias = clip_bias(*clips)

    def step(i, _):
        loads, parts = [], []
        for col in range(0, CHUNK, HD):
            part = pl.ds(pl.multiple_of(i * CHUNK + col, HD), HD)
            parts.append(part)
            loads.append(
                (
                    lambda part=part: [q[0:FRAME, part], q[rows - FRAME : rows, part]],
                    lambda part=part: window(k, 0, part),
                    lambda part=part: window(v, 1, part),
                )
            )
        for part, result in zip(parts, attend(loads, bias)):
            out[:, part] = result
        return 0

    lax.fori_loop(0, width // CHUNK, step, 0)


def edge_attention(lo, hi, q, k, v, far, near):
    rows, width = q.shape
    return pl.pallas_call(
        edge_kernel,
        out_shape=jax.ShapeDtypeStruct((NEAR, width), BF16),
        in_specs=[SMEM, SMEM] + [VMEM] * 5,
        out_specs=VMEM,
        compiler_params=pltpu.CompilerParams(vmem_limit_bytes=20 << 20),
        cost_estimate=pl.CostEstimate(
            flops=16 * NEAR * NEAR * width,
            bytes_accessed=7 * rows * width,
            transcendentals=NEAR * NEAR * HEADS,
        ),
        name="edge_attention",
    )(lo, hi, q, k, v, far, near)


def last_kernel(layout, frozen, own_down, inner, edges, *rest):
    refs, rest = rest[:-6], rest[-6:]
    merged, attended, factors, w, result, sems = rest
    shard, width = frozen.shape
    rows = result.shape[0]
    me = lax.axis_index("seq")
    kind = lax.axis_index("group")
    for ref, (swapped, masks) in zip(refs, layout):
        target = 1 - kind if swapped else kind
        for i, mask in enumerate(masks):
            at = pl.ds(pl.multiple_of((me ^ mask) * shard, shard), shard)
            factors[target, at, :] = ref[i]
    if not layout:
        factors = refs[0]
    down, up = factors.at[0], factors.at[1]
    parts = ((inner, FRAME), (edges, 0))
    reduced = [dot(att[...], down[...], NN).astype(BF16) for att, _ in parts]
    stores = []

    def store(source, target):
        stores.append(pltpu.make_async_copy(source, target, sems.at[len(stores)]))
        stores[-1].start()

    for first in range(0, width, CHUNK):
        part = pl.ds(first, CHUNK)
        factor = up[part, :]
        product = dot(own_down[...], factor, NT)
        w[:, part] = (frozen[:, part].astype(F32) + ADAPTER_SCALE * product).astype(BF16)
        store(w.at[:, part], merged.at[:, part])
        for narrow, (att, _) in zip(reduced, parts):
            value = att[:, part].astype(F32) + ADAPTER_SCALE * dot(narrow, factor, NT)
            value = value.astype(BF16)
            if att is inner:
                result[FRAME : rows - FRAME, part] = value
            else:
                result[0:FRAME, part] = value[:FRAME]
                result[rows - FRAME : rows, part] = value[FRAME:]
        store(result.at[:, part], attended.at[:, part])
    for copy in stores:
        copy.wait()


def last(frozen, own_down, inner, edges, layout, pieces):
    shard, width = frozen.shape
    rank = own_down.shape[1]
    rows = 2 * NEAR
    return pl.pallas_call(
        functools.partial(last_kernel, layout),
        out_shape=(
            jax.ShapeDtypeStruct((shard, width), BF16),
            jax.ShapeDtypeStruct((rows, width), BF16),
        ),
        in_specs=[VMEM] * (4 + len(pieces)),
        out_specs=(ANY, ANY),
        scratch_shapes=[
            pltpu.VMEM((2, width, rank), BF16),
            pltpu.VMEM((shard, width), BF16),
            pltpu.VMEM((rows, width), BF16),
            pltpu.SemaphoreType.DMA((2 * (width // CHUNK),)),
        ],
        compiler_params=pltpu.CompilerParams(vmem_limit_bytes=24 << 20),
        cost_estimate=pl.CostEstimate(
            flops=2 * (shard + 2 * rows) * width * rank,
            bytes_accessed=4 * (shard + rows) * width + 4 * width * rank,
            transcendentals=0,
        ),
        name="adapter_and_merge",
    )(frozen, own_down, inner, edges, *pieces)


def gather_factors(down, up, inner):
    count = lax.axis_size("seq")
    if lax.axis_size("group") != 2 or down.shape[0] % 32:
        both = lax.all_gather(jnp.stack([down, up]), "seq", axis=1, tiled=True)
        return [], [both], inner

    def swap(cells, mask):
        return lax.ppermute(cells, "seq", [(i, i ^ mask) for i in range(count)])

    def cross(cells):
        return lax.ppermute(cells, "group", [(0, 1), (1, 0)])

    cells = jnp.where(lax.axis_index("group") == 0, down, up)[None]
    masks = [0]
    steps = [2] + [count >> j for j in range(1, count.bit_length()) if count >> j > 2]
    for mask in steps[:-1]:
        cells = jnp.concatenate([cells, swap(cells, mask)])
        masks = masks + [have ^ mask for have in masks]
    cells, inner = lax.optimization_barrier((cells, inner))
    early = cross(cells)
    new = swap(cells, steps[-1])
    late = cross(new)
    cells = jnp.concatenate([cells, new])
    masks = masks + [have ^ steps[-1] for have in masks]
    other = jnp.concatenate([early, late])
    across = [mask ^ 1 for mask in masks]
    return (
        [(0, masks), (0, across), (1, masks), (1, across)],
        [cells, swap(cells, 1), other, swap(other, 1)],
        inner,
    )


def exchange_halos(k, v):
    count = lax.axis_size("seq")
    rows = k.shape[0]
    odd = lax.rem(lax.axis_index("seq"), 2)

    def rim(start):
        return jnp.stack([lax.dynamic_slice_in_dim(x, start, FRAME, 0) for x in (k, v)])

    links = [(i, i + 1) for i in range(1, count - 1, 2)]
    far = lax.ppermute(
        rim(odd * (rows - FRAME)), "seq", links + [(b, a) for a, b in links]
    )
    near = lax.ppermute(
        rim((1 - odd) * (rows - FRAME)), "seq", [(i, i ^ 1) for i in range(count)]
    )
    return far, near


def body(q, k, v, lo, hi, down, up, frozen):
    far, near = exchange_halos(k, v)
    inner = inner_attention(lo, hi, q, k, v)
    layout, pieces, inner = gather_factors(down, up.T, inner)
    edges = edge_attention(lo, hi, q, k, v, far, near)
    merged, attended = last(frozen, down, inner, edges, layout, pieces)
    return (attended, merged)


def solution(mesh):
    rows = P(("group", "seq"), None)
    flat = P(("group", "seq"))
    return jax.shard_map(
        body,
        mesh=mesh,
        in_specs=(rows, rows, rows, flat, flat, P("seq", None), P(None, "seq"), P("seq", None)),
        out_specs=(rows, rows),
        check_vma=False,
    )
```

```python
import functools

import jax
import jax.numpy as jnp
from jax import lax
from jax.experimental import pallas as pl
from jax.experimental.pallas import tpu as pltpu
from jax.sharding import PartitionSpec as P

MODEL_WIDTH = 5120
HEADS = 40
HD = 128
FRAME = 64
NEAR = 2 * FRAME
CHUNK = 512
SCORE_SCALE = HD ** (-0.5) * 1.4426950408889634
ADAPTER_SCALE = MODEL_WIDTH ** (-0.5)
FAR = -1e30
NT = (((1,), (1,)), ((), ()))
NN = (((1,), (0,)), ((), ()))
BF16 = jnp.bfloat16
F32 = jnp.float32
ANY = pl.BlockSpec(memory_space=pl.ANY)
SMEM = pl.BlockSpec(memory_space=pltpu.SMEM)
VMEM = pl.BlockSpec(memory_space=pltpu.VMEM)


def dot(a, b, dims):
    return lax.dot_general(a, b, dims, preferred_element_type=F32)


def clip_bias(lo, hi):
    position = lax.broadcasted_iota(jnp.int32, (NEAR, NEAR), 1)
    return jnp.where(position < hi - lo, 0.0, FAR).astype(F32)


def diagonal(top, bottom):
    zeros = jnp.zeros((FRAME, NEAR), BF16)
    return jnp.concatenate(
        [jnp.concatenate([top, zeros], axis=1), jnp.concatenate([zeros, bottom], axis=1)]
    )


def attend(loads):
    ones = jnp.ones((NEAR, HD), BF16)
    scores = []
    for load_q, load_k, _, bias in loads:
        q = load_q()
        scores.append(dot(diagonal(q[:, :HD], q[:, HD:]), load_k(), NT) * SCORE_SCALE + bias)
    weights = [jnp.exp2(s - jnp.max(s, axis=-1, keepdims=True)).astype(BF16) for s in scores]
    results = []
    for w, (_, _, load_v, _) in zip(weights, loads):
        v = load_v()
        values = jnp.concatenate(
            [jnp.concatenate([v[:, at : at + HD], ones], axis=1) for at in (0, HD)]
        )
        mixed = dot(diagonal(w[:FRAME], w[FRAME:]), values, NN)
        mixed = (mixed[:, :HD] * (1.0 / mixed[:, HD:])).astype(BF16)
        results.append(jnp.concatenate([mixed[:FRAME], mixed[FRAME:]], axis=1))
    return results


def inner_kernel(lo_ref, hi_ref, q_ref, k_ref, v_ref, o_ref):
    rows = q_ref.shape[0]
    base = lax.axis_index("seq") * rows
    loads, targets = [], []
    for row in (FRAME, NEAR):
        lo, hi = lo_ref[row], hi_ref[row]
        keys = pl.ds(pl.multiple_of(lo - base, FRAME), NEAR)
        bias = clip_bias(lo, hi)
        for col in range(0, CHUNK, 2 * HD):
            part = slice(col, col + 2 * HD)
            targets.append((slice(row - FRAME, row), part))
            loads.append(
                (
                    lambda row=row, part=part: q_ref[row : row + FRAME, part],
                    lambda keys=keys, part=part: k_ref[keys, part],
                    lambda keys=keys, part=part: v_ref[keys, part],
                    bias,
                )
            )
    for target, result in zip(targets, attend(loads)):
        o_ref[target] = result


def inner_attention(lo, hi, q, k, v):
    rows, width = q.shape
    block = pl.BlockSpec((rows, CHUNK), lambda i: (0, i))
    return pl.pallas_call(
        inner_kernel,
        grid=(width // CHUNK,),
        out_shape=jax.ShapeDtypeStruct((NEAR, width), BF16),
        in_specs=[SMEM, SMEM, block, block, block],
        out_specs=pl.BlockSpec((NEAR, CHUNK), lambda i: (0, i)),
        compiler_params=pltpu.CompilerParams(vmem_limit_bytes=16 << 20),
        cost_estimate=pl.CostEstimate(
            flops=16 * NEAR * NEAR * width,
            bytes_accessed=7 * rows * width,
            transcendentals=NEAR * NEAR * HEADS,
        ),
        name="inner_attention",
    )(lo, hi, q, k, v)


def edge_kernel(is_near, lo_ref, hi_ref, q, k, v, *rest):
    halos, out = rest[:-1], rest[-1]
    rows, width = q.shape
    me = lax.axis_index("seq")
    base = me * rows
    right = lax.rem(me, 2) == (0 if is_near else 1)
    row = pl.multiple_of(jnp.where(right, rows - FRAME, 0), FRAME)
    first = pl.multiple_of(jnp.where(right, rows - NEAR, 0), NEAR)
    second = pl.multiple_of(first + FRAME, FRAME)
    lo, hi = lo_ref[row], hi_ref[row]
    before = lo < base
    after = jnp.logical_and(right, lo == base + rows - FRAME)
    direct = lax.rem(lax.div(me + 1, 2), 2) == 1

    def window(ref, kind, part):
        halo = halos[0][kind, :, part]
        if len(halos) == 2:
            halo = jnp.where(direct, halo, halos[1][kind, :, part])
        one, two = ref[pl.ds(first, FRAME), part], ref[pl.ds(second, FRAME), part]
        return jnp.concatenate(
            [
                jnp.where(before, halo, jnp.where(after, two, one)),
                jnp.where(before, one, jnp.where(after, halo, two)),
            ]
        )

    bias = clip_bias(lo, hi)

    def step(i, _):
        loads, parts = [], []
        for col in range(0, 2 * CHUNK, 2 * HD):
            part = pl.ds(pl.multiple_of(i * 2 * CHUNK + col, 2 * HD), 2 * HD)
            parts.append(part)
            loads.append(
                (
                    lambda part=part: q[pl.ds(row, FRAME), part],
                    lambda part=part: window(k, 0, part),
                    lambda part=part: window(v, 1, part),
                    bias,
                )
            )
        for part, result in zip(parts, attend(loads)):
            out[:, part] = result
        return 0

    lax.fori_loop(0, width // (2 * CHUNK), step, 0)


def edge_attention(lo, hi, q, k, v, *halos):
    rows, width = q.shape
    is_near = len(halos) == 1
    return pl.pallas_call(
        functools.partial(edge_kernel, is_near),
        out_shape=jax.ShapeDtypeStruct((FRAME, width), BF16),
        in_specs=[SMEM, SMEM] + [VMEM] * (3 + len(halos)),
        out_specs=VMEM,
        compiler_params=pltpu.CompilerParams(vmem_limit_bytes=20 << 20),
        cost_estimate=pl.CostEstimate(
            flops=8 * NEAR * NEAR * width,
            bytes_accessed=7 * rows * width,
            transcendentals=FRAME * NEAR * HEADS,
        ),
        name="near_edge_attention" if is_near else "far_edge_attention",
    )(lo, hi, q, k, v, *halos)


def last_kernel(layout, frozen, own_down, inner, near, far, *rest):
    refs, rest = rest[:-6], rest[-6:]
    merged, attended, factors, w, result, sems = rest
    shard, width = frozen.shape
    rows = result.shape[0]
    me = lax.axis_index("seq")
    kind = lax.axis_index("group")
    for ref, (swapped, masks) in zip(refs, layout):
        target = 1 - kind if swapped else kind
        for i, mask in enumerate(masks):
            at = pl.ds(pl.multiple_of((me ^ mask) * shard, shard), shard)
            factors[target, at, :] = ref[i]
    if not layout:
        factors = refs[0]
    down, up = factors.at[0], factors.at[1]
    right = lax.rem(me, 2) == 0
    near_row = pl.multiple_of(jnp.where(right, rows - FRAME, 0), FRAME)
    far_row = pl.multiple_of(jnp.where(right, 0, rows - FRAME), FRAME)
    parts = ((inner, FRAME), (near, near_row), (far, far_row))
    reduced = [dot(att[...], down[...], NN).astype(BF16) for att, _ in parts]
    stores = []

    def store(source, target):
        stores.append(pltpu.make_async_copy(source, target, sems.at[len(stores)]))
        stores[-1].start()

    for first in range(0, width, CHUNK):
        part = pl.ds(first, CHUNK)
        factor = up[part, :]
        product = dot(own_down[...], factor, NT)
        w[:, part] = (frozen[:, part].astype(F32) + ADAPTER_SCALE * product).astype(BF16)
        store(w.at[:, part], merged.at[:, part])
        for narrow, (att, row) in zip(reduced, parts):
            value = att[:, part].astype(F32) + ADAPTER_SCALE * dot(narrow, factor, NT)
            result[pl.ds(row, att.shape[0]), part] = value.astype(BF16)
        store(result.at[:, part], attended.at[:, part])
    for copy in stores:
        copy.wait()


def last(frozen, own_down, inner, near, far, layout, pieces):
    shard, width = frozen.shape
    rank = own_down.shape[1]
    rows = 2 * NEAR
    return pl.pallas_call(
        functools.partial(last_kernel, layout),
        out_shape=(
            jax.ShapeDtypeStruct((shard, width), BF16),
            jax.ShapeDtypeStruct((rows, width), BF16),
        ),
        in_specs=[VMEM] * (5 + len(pieces)),
        out_specs=(ANY, ANY),
        scratch_shapes=[
            pltpu.VMEM((2, width, rank), BF16),
            pltpu.VMEM((shard, width), BF16),
            pltpu.VMEM((rows, width), BF16),
            pltpu.SemaphoreType.DMA((2 * (width // CHUNK),)),
        ],
        compiler_params=pltpu.CompilerParams(vmem_limit_bytes=24 << 20),
        cost_estimate=pl.CostEstimate(
            flops=2 * (shard + 2 * rows) * width * rank,
            bytes_accessed=4 * (shard + rows) * width + 4 * width * rank,
            transcendentals=0,
        ),
        name="adapter_and_merge",
    )(frozen, own_down, inner, near, far, *pieces)


def body(q, k, v, lo, hi, down, up, frozen):
    count = lax.axis_size("seq")
    rows = k.shape[0]
    odd = lax.rem(lax.axis_index("seq"), 2)

    def rim(start):
        return jnp.stack([lax.dynamic_slice_in_dim(x, start, FRAME, 0) for x in (k, v)])

    def send(cells, pairs):
        return lax.ppermute(cells, "seq", pairs + [(b, a) for a, b in pairs])

    def swap(cells, mask):
        return send(cells, [(i, i ^ mask) for i in range(count) if not i & mask])

    def cross(cells):
        return lax.ppermute(cells, "group", [(0, 1), (1, 0)])

    far_rim = rim(odd * (rows - FRAME))
    direct = send(far_rim, [(i, i + 1) for i in range(1, count - 1, 4)])
    near = swap(rim((1 - odd) * (rows - FRAME)), 1)
    distant = [(i, i + 1) for i in range(3, count - 1, 4)]
    up = up.T
    if lax.axis_size("group") != 2 or down.shape[0] % 32:
        both = lax.all_gather(jnp.stack([down, up]), "seq", axis=1, tiled=True)
        layout, pieces = [], [both]
        inner = inner_attention(lo, hi, q, k, v)
        near_edge = edge_attention(lo, hi, q, k, v, near)
        diagonal_halo = send(far_rim, distant)
    else:
        cells = jnp.where(lax.axis_index("group") == 0, down, up)[None]
        masks = [0]
        steps = [2] + [count >> j for j in range(1, count.bit_length()) if count >> j > 2]
        for mask in steps[:-1]:
            cells = jnp.concatenate([cells, swap(cells, mask)])
            masks = masks + [have ^ mask for have in masks]
        cells, far_rim, lo_inner = lax.optimization_barrier((cells, far_rim, lo))
        new = swap(cells, steps[-1])
        diagonal_halo = send(far_rim, distant)
        early = cross(cells)
        inner = inner_attention(lo_inner, hi, q, k, v)
        new, inner, lo_near = lax.optimization_barrier((new, inner, lo))
        late = cross(new)
        cells = jnp.concatenate([cells, new])
        masks = masks + [have ^ steps[-1] for have in masks]
        near_edge = edge_attention(lo_near, hi, q, k, v, near)
        other = jnp.concatenate([early, late])
        other, near_edge = lax.optimization_barrier((other, near_edge))
        across = [mask ^ 1 for mask in masks]
        layout = [(0, masks), (0, across), (1, masks), (1, across)]
        pieces = [cells, swap(cells, 1), other, swap(other, 1)]
    far_edge = edge_attention(lo, hi, q, k, v, direct, diagonal_halo)
    merged, attended = last(frozen, down, inner, near_edge, far_edge, layout, pieces)
    return (attended, merged)


def solution(mesh):
    rows = P(("group", "seq"), None)
    flat = P(("group", "seq"))
    return jax.shard_map(
        body,
        mesh=mesh,
        in_specs=(rows, rows, rows, flat, flat, P("seq", None), P(None, "seq"), P("seq", None)),
        out_specs=(rows, rows),
        check_vma=False,
    )
```

```python
import functools

import jax
import jax.numpy as jnp
from jax import lax
from jax.experimental import pallas as pl
from jax.experimental.pallas import tpu as pltpu
from jax.sharding import PartitionSpec as P

MODEL_WIDTH = 5120
HEADS = 40
HD = 128
FRAME = 64
NEAR = 2 * FRAME
CHUNK = 512
WIDE = 2 * CHUNK
FAR_CUTS = (0, 2048, MODEL_WIDTH)
SCORE_SCALE = HD ** (-0.5) * 1.4426950408889634
ADAPTER_SCALE = MODEL_WIDTH ** (-0.5)
FAR = -1e30
NT = (((1,), (1,)), ((), ()))
NN = (((1,), (0,)), ((), ()))
BF16 = jnp.bfloat16
F32 = jnp.float32
ANY = pl.BlockSpec(memory_space=pl.ANY)
SMEM = pl.BlockSpec(memory_space=pltpu.SMEM)
VMEM = pl.BlockSpec(memory_space=pltpu.VMEM)


def dot(a, b, dims):
    return lax.dot_general(a, b, dims, preferred_element_type=F32)


def clip_bias(lo, hi):
    position = lax.broadcasted_iota(jnp.int32, (NEAR, NEAR), 1)
    return jnp.where(position < hi - lo, 0.0, FAR).astype(F32)


def diagonal(top, bottom):
    zeros = jnp.zeros((FRAME, NEAR), BF16)
    return jnp.concatenate(
        [jnp.concatenate([top, zeros], axis=1), jnp.concatenate([zeros, bottom], axis=1)]
    )


def attend(loads):
    ones = jnp.ones((NEAR, HD), BF16)
    scores = []
    for load_q, load_k, _, bias in loads:
        q = load_q()
        scores.append(dot(diagonal(q[:, :HD], q[:, HD:]), load_k(), NT) * SCORE_SCALE + bias)
    weights = [jnp.exp2(s - jnp.max(s, axis=-1, keepdims=True)).astype(BF16) for s in scores]
    results = []
    for w, (_, _, load_v, _) in zip(weights, loads):
        v = load_v()
        values = jnp.concatenate(
            [jnp.concatenate([v[:, at : at + HD], ones], axis=1) for at in (0, HD)]
        )
        mixed = dot(diagonal(w[:FRAME], w[FRAME:]), values, NN)
        mixed = (mixed[:, :HD] * (1.0 / mixed[:, HD:])).astype(BF16)
        results.append(jnp.concatenate([mixed[:FRAME], mixed[FRAME:]], axis=1))
    return results


def inner_kernel(lo_ref, hi_ref, q_ref, k_ref, v_ref, o_ref):
    rows = q_ref.shape[0]
    base = lax.axis_index("seq") * rows
    loads, targets = [], []
    for row in (FRAME, NEAR):
        lo, hi = lo_ref[row], hi_ref[row]
        keys = pl.ds(pl.multiple_of(lo - base, FRAME), NEAR)
        bias = clip_bias(lo, hi)
        for col in range(0, WIDE, 2 * HD):
            part = slice(col, col + 2 * HD)
            targets.append((slice(row - FRAME, row), part))
            loads.append(
                (
                    lambda row=row, part=part: q_ref[row : row + FRAME, part],
                    lambda keys=keys, part=part: k_ref[keys, part],
                    lambda keys=keys, part=part: v_ref[keys, part],
                    bias,
                )
            )
    for target, result in zip(targets, attend(loads)):
        o_ref[target] = result


def inner_attention(lo, hi, q, k, v):
    rows, width = q.shape
    block = pl.BlockSpec((rows, WIDE), lambda i: (0, i))
    return pl.pallas_call(
        inner_kernel,
        grid=(width // WIDE,),
        out_shape=jax.ShapeDtypeStruct((NEAR, width), BF16),
        in_specs=[SMEM, SMEM, block, block, block],
        out_specs=pl.BlockSpec((NEAR, WIDE), lambda i: (0, i)),
        compiler_params=pltpu.CompilerParams(vmem_limit_bytes=16 << 20),
        cost_estimate=pl.CostEstimate(
            flops=16 * NEAR * NEAR * width,
            bytes_accessed=7 * rows * width,
            transcendentals=NEAR * NEAR * HEADS,
        ),
        name="inner_attention",
    )(lo, hi, q, k, v)


def edge_kernel(is_near, start, lo_ref, hi_ref, q, k, v, *rest):
    halos, out = rest[:-1], rest[-1]
    rows, width = q.shape[0], out.shape[1]
    pairs = width // (2 * HD)
    unroll = next(n for n in (8, 6, 5, 4, 2, 1) if pairs % n == 0)
    me = lax.axis_index("seq")
    base = me * rows
    right = lax.rem(me, 2) == (0 if is_near else 1)
    row = pl.multiple_of(jnp.where(right, rows - FRAME, 0), FRAME)
    first = pl.multiple_of(jnp.where(right, rows - NEAR, 0), NEAR)
    second = pl.multiple_of(first + FRAME, FRAME)
    lo, hi = lo_ref[row], hi_ref[row]
    before = lo < base
    after = jnp.logical_and(right, lo == base + rows - FRAME)
    direct = lax.rem(lax.div(me + 1, 2), 2) == 1

    def window(ref, kind, part, here):
        halo = halos[0][kind, :, here]
        if len(halos) == 2:
            halo = jnp.where(direct, halo, halos[1][kind, :, here])
        one, two = ref[pl.ds(first, FRAME), part], ref[pl.ds(second, FRAME), part]
        return jnp.concatenate(
            [
                jnp.where(before, halo, jnp.where(after, two, one)),
                jnp.where(before, one, jnp.where(after, halo, two)),
            ]
        )

    bias = clip_bias(lo, hi)

    def step(i, _):
        loads, parts = [], []
        for pair in range(unroll):
            col = pl.multiple_of((i * unroll + pair) * 2 * HD, 2 * HD)
            here = pl.ds(col, 2 * HD)
            part = pl.ds(pl.multiple_of(col + start, 2 * HD), 2 * HD)
            parts.append(here)
            loads.append(
                (
                    lambda part=part: q[pl.ds(row, FRAME), part],
                    lambda part=part, here=here: window(k, 0, part, here),
                    lambda part=part, here=here: window(v, 1, part, here),
                    bias,
                )
            )
        for here, result in zip(parts, attend(loads)):
            out[:, here] = result
        return 0

    lax.fori_loop(0, pairs // unroll, step, 0)


def edge_attention(name, start, lo, hi, q, k, v, *halos):
    rows = q.shape[0]
    width = halos[0].shape[2]
    return pl.pallas_call(
        functools.partial(edge_kernel, name == "near_edge", start),
        out_shape=jax.ShapeDtypeStruct((FRAME, width), BF16),
        in_specs=[SMEM, SMEM] + [VMEM] * (3 + len(halos)),
        out_specs=VMEM,
        compiler_params=pltpu.CompilerParams(vmem_limit_bytes=20 << 20),
        cost_estimate=pl.CostEstimate(
            flops=8 * NEAR * NEAR * width,
            bytes_accessed=7 * rows * width,
            transcendentals=FRAME * NEAR * HEADS,
        ),
        name=name,
    )(lo, hi, q, k, v, *halos)


def last_kernel(layout, frozen, own_down, inner, near, *rest):
    fars, rest = rest[: len(FAR_CUTS) - 1], rest[len(FAR_CUTS) - 1 :]
    refs, rest = rest[:-6], rest[-6:]
    merged, attended, factors, w, result, sems = rest
    shard, width = frozen.shape
    rows = result.shape[0]
    me = lax.axis_index("seq")
    kind = lax.axis_index("group")
    for ref, (swapped, masks) in zip(refs, layout):
        target = 1 - kind if swapped else kind
        for i, mask in enumerate(masks):
            at = pl.ds(pl.multiple_of((me ^ mask) * shard, shard), shard)
            factors[target, at, :] = ref[i]
    if not layout:
        factors = refs[0]
    down, up = factors.at[0], factors.at[1]
    right = lax.rem(me, 2) == 0
    near_row = pl.multiple_of(jnp.where(right, rows - FRAME, 0), FRAME)
    far_row = pl.multiple_of(jnp.where(right, 0, rows - FRAME), FRAME)
    parts = ((inner, FRAME), (near, near_row), (None, far_row))
    reduced = [dot(att[...], down[...], NN).astype(BF16) for att in (inner, near)]
    pieces = [
        dot(att[...], down[start : start + att.shape[1]], NN)
        for att, start in zip(fars, FAR_CUTS)
    ]
    reduced.append(sum(pieces[1:], pieces[0]).astype(BF16))
    stores = []

    def store(source, target):
        stores.append(pltpu.make_async_copy(source, target, sems.at[len(stores)]))
        stores[-1].start()

    for first in range(0, width, CHUNK):
        part = pl.ds(first, CHUNK)
        factor = up[part, :]
        product = dot(own_down[...], factor, NT)
        w[:, part] = (frozen[:, part].astype(F32) + ADAPTER_SCALE * product).astype(BF16)
        store(w.at[:, part], merged.at[:, part])
        for narrow, (att, row) in zip(reduced, parts):
            if att is None:
                at = max(i for i, start in enumerate(FAR_CUTS) if start <= first)
                value = fars[at][:, pl.ds(first - FAR_CUTS[at], CHUNK)]
            else:
                value = att[:, part]
            value = value.astype(F32) + ADAPTER_SCALE * dot(narrow, factor, NT)
            result[pl.ds(row, value.shape[0]), part] = value.astype(BF16)
        store(result.at[:, part], attended.at[:, part])
    for copy in stores:
        copy.wait()


def last(frozen, own_down, attention, layout, pieces):
    shard, width = frozen.shape
    rank = own_down.shape[1]
    rows = 2 * NEAR
    return pl.pallas_call(
        functools.partial(last_kernel, layout),
        out_shape=(
            jax.ShapeDtypeStruct((shard, width), BF16),
            jax.ShapeDtypeStruct((rows, width), BF16),
        ),
        in_specs=[VMEM] * (2 + len(attention) + len(pieces)),
        out_specs=(ANY, ANY),
        scratch_shapes=[
            pltpu.VMEM((2, width, rank), BF16),
            pltpu.VMEM((shard, width), BF16),
            pltpu.VMEM((rows, width), BF16),
            pltpu.SemaphoreType.DMA((2 * (width // CHUNK),)),
        ],
        compiler_params=pltpu.CompilerParams(vmem_limit_bytes=24 << 20),
        cost_estimate=pl.CostEstimate(
            flops=2 * (shard + 2 * rows) * width * rank,
            bytes_accessed=4 * (shard + rows) * width + 4 * width * rank,
            transcendentals=0,
        ),
        name="adapter_and_merge",
    )(frozen, own_down, *attention, *pieces)


def body(q, k, v, lo, hi, down, up, frozen):
    count = lax.axis_size("seq")
    rows = k.shape[0]
    odd = lax.rem(lax.axis_index("seq"), 2)

    def rim(start, columns):
        return jnp.stack([lax.dynamic_slice_in_dim(x, start, FRAME, 0)[:, columns] for x in (k, v)])

    def swap(cells, mask):
        return lax.ppermute(cells, "seq", [(i, i ^ mask) for i in range(count)])

    def cross(cells):
        return lax.ppermute(cells, "group", [(0, 1), (1, 0)])

    close, distant = (
        [(i + a, i + 1 - a) for i in range(first, count - 1, 4) for a in (0, 1)]
        for first in (1, 3)
    )

    def far_rim(at):
        return rim(odd * (rows - FRAME), slice(FAR_CUTS[at], FAR_CUTS[at + 1]))

    def near_halo(odd):
        return swap(rim((1 - odd) * (rows - FRAME), slice(None)), 1)

    def far_edge(at, *halos):
        return edge_attention("far_edge", FAR_CUTS[at], lo, hi, q, k, v, *halos)

    up = up.T
    if lax.axis_size("group") != 2 or down.shape[0] % 32:
        both = lax.all_gather(jnp.stack([down, up]), "seq", axis=1, tiled=True)
        layout, pieces = [], [both]
        inner = inner_attention(lo, hi, q, k, v)
        near = edge_attention("near_edge", 0, lo, hi, q, k, v, near_halo(odd))
        fars = [
            far_edge(at, lax.ppermute(far_rim(at), "seq", close + distant)) for at in range(2)
        ]
    else:
        barrier = lax.optimization_barrier
        inner = inner_attention(lo, hi, q, k, v)
        early_halo = lax.ppermute(far_rim(0), "seq", close + distant)
        cells = jnp.where(lax.axis_index("group") == 0, down, up)[None]
        masks = [0]
        steps = [2] + [count >> j for j in range(1, count.bit_length()) if count >> j > 2]
        for mask in steps[:-1]:
            cells = jnp.concatenate([cells, swap(cells, mask)])
            masks = masks + [have ^ mask for have in masks]
            if mask == 2:
                cells, later = barrier((cells, odd))
        near = near_halo(later)
        late_rim = far_rim(1)
        late_halos = [lax.ppermute(late_rim, "seq", close)]
        cells, inner, early_halo, late_rim = barrier((cells, inner, early_halo, late_rim))
        new = swap(cells, steps[-1])
        late_halos.append(lax.ppermute(late_rim, "seq", distant))
        early = cross(cells)
        new, lo_edge = barrier((new, lo))
        late = cross(new)
        cells = jnp.concatenate([cells, new])
        masks = masks + [have ^ steps[-1] for have in masks]
        near = edge_attention("near_edge", 0, lo_edge, hi, q, k, v, near)
        fars = [far_edge(0, early_halo)]
        other = jnp.concatenate([early, late])
        other, near, fars, late_halos = barrier((other, near, fars, late_halos))
        fars.append(far_edge(1, *late_halos))
        across = [mask ^ 1 for mask in masks]
        layout = [(0, masks), (0, across), (1, masks), (1, across)]
        pieces = [cells, swap(cells, 1), other, swap(other, 1)]
    merged, attended = last(frozen, down, (inner, near, *fars), layout, pieces)
    return (attended, merged)


def solution(mesh):
    rows = P(("group", "seq"), None)
    flat = P(("group", "seq"))
    return jax.shard_map(
        body,
        mesh=mesh,
        in_specs=(rows, rows, rows, flat, flat, P("seq", None), P(None, "seq"), P("seq", None)),
        out_specs=(rows, rows),
        check_vma=False,
    )
```

```python
import functools

import jax
import jax.numpy as jnp
from jax import lax
from jax.experimental import pallas as pl
from jax.experimental.pallas import tpu as pltpu
from jax.sharding import PartitionSpec as P

MODEL_WIDTH = 5120
HEADS = 40
HD = 128
FRAME = 64
NEAR = 2 * FRAME
CHUNK = 512
WIDE = 2 * CHUNK
SCORE_SCALE = HD ** (-0.5) * 1.4426950408889634
ADAPTER_SCALE = MODEL_WIDTH ** (-0.5)
FAR = -1e30
NT = (((1,), (1,)), ((), ()))
NN = (((1,), (0,)), ((), ()))
BF16 = jnp.bfloat16
F32 = jnp.float32
ANY = pl.BlockSpec(memory_space=pl.ANY)
SMEM = pl.BlockSpec(memory_space=pltpu.SMEM)
VMEM = pl.BlockSpec(memory_space=pltpu.VMEM)


def dot(a, b, dims):
    return lax.dot_general(a, b, dims, preferred_element_type=F32)


def clip_bias(lo, hi):
    position = lax.broadcasted_iota(jnp.int32, (NEAR, NEAR), 1)
    return jnp.where(position < hi - lo, 0.0, FAR).astype(F32)


def diagonal(top, bottom):
    zeros = jnp.zeros((FRAME, NEAR), BF16)
    return jnp.concatenate(
        [jnp.concatenate([top, zeros], axis=1), jnp.concatenate([zeros, bottom], axis=1)]
    )


def attend(loads):
    ones = jnp.ones((NEAR, HD), BF16)
    scores = []
    for load_q, load_k, _, bias in loads:
        q = load_q()
        scores.append(dot(diagonal(q[:, :HD], q[:, HD:]), load_k(), NT) * SCORE_SCALE + bias)
    weights = [jnp.exp2(s - jnp.max(s, axis=-1, keepdims=True)).astype(BF16) for s in scores]
    results = []
    for w, (_, _, load_v, _) in zip(weights, loads):
        v = load_v()
        values = jnp.concatenate(
            [jnp.concatenate([v[:, at : at + HD], ones], axis=1) for at in (0, HD)]
        )
        mixed = dot(diagonal(w[:FRAME], w[FRAME:]), values, NN)
        mixed = (mixed[:, :HD] * (1.0 / mixed[:, HD:])).astype(BF16)
        results.append(jnp.concatenate([mixed[:FRAME], mixed[FRAME:]], axis=1))
    return results


def inner_kernel(lo_ref, hi_ref, q_ref, k_ref, v_ref, o_ref):
    rows = q_ref.shape[0]
    base = lax.axis_index("seq") * rows
    loads, targets = [], []
    for row in (FRAME, NEAR):
        lo, hi = lo_ref[row], hi_ref[row]
        keys = pl.ds(pl.multiple_of(lo - base, FRAME), NEAR)
        bias = clip_bias(lo, hi)
        for col in range(0, WIDE, 2 * HD):
            part = slice(col, col + 2 * HD)
            targets.append((slice(row - FRAME, row), part))
            loads.append(
                (
                    lambda row=row, part=part: q_ref[row : row + FRAME, part],
                    lambda keys=keys, part=part: k_ref[keys, part],
                    lambda keys=keys, part=part: v_ref[keys, part],
                    bias,
                )
            )
    for target, result in zip(targets, attend(loads)):
        o_ref[target] = result


def inner_attention(lo, hi, q, k, v):
    rows, width = q.shape
    block = pl.BlockSpec((rows, WIDE), lambda i: (0, i))
    return pl.pallas_call(
        inner_kernel,
        grid=(width // WIDE,),
        out_shape=jax.ShapeDtypeStruct((NEAR, width), BF16),
        in_specs=[SMEM, SMEM, block, block, block],
        out_specs=pl.BlockSpec((NEAR, WIDE), lambda i: (0, i)),
        compiler_params=pltpu.CompilerParams(vmem_limit_bytes=16 << 20),
        cost_estimate=pl.CostEstimate(
            flops=16 * NEAR * NEAR * width,
            bytes_accessed=7 * rows * width,
            transcendentals=NEAR * NEAR * HEADS,
        ),
        name="inner_attention",
    )(lo, hi, q, k, v)


def edge_side(is_near, rows):
    right = lax.rem(lax.axis_index("seq"), 2) == (0 if is_near else 1)
    return right, pl.multiple_of(jnp.where(right, rows - FRAME, 0), FRAME)


def attend_edge(is_near, lo_ref, hi_ref, q, k, v, halos, out):
    rows, width = q.shape
    pairs = width // (2 * HD)
    unroll = next(n for n in (10, 8, 6, 5, 4, 2, 1) if pairs % n == 0)
    me = lax.axis_index("seq")
    base = me * rows
    right, row = edge_side(is_near, rows)
    first = pl.multiple_of(jnp.where(right, rows - NEAR, 0), NEAR)
    second = pl.multiple_of(first + FRAME, FRAME)
    lo, hi = lo_ref[row], hi_ref[row]
    before = lo < base
    after = jnp.logical_and(right, lo == base + rows - FRAME)
    direct = lax.rem(lax.div(me + 1, 2), 2) == 1

    def window(ref, kind, part):
        halo = halos[0][kind, :, part]
        if len(halos) == 2:
            halo = jnp.where(direct, halo, halos[1][kind, :, part])
        one, two = ref[pl.ds(first, FRAME), part], ref[pl.ds(second, FRAME), part]
        return jnp.concatenate(
            [
                jnp.where(before, halo, jnp.where(after, two, one)),
                jnp.where(before, one, jnp.where(after, halo, two)),
            ]
        )

    bias = clip_bias(lo, hi)

    def step(i, _):
        loads, parts = [], []
        for pair in range(unroll):
            part = pl.ds(pl.multiple_of((i * unroll + pair) * 2 * HD, 2 * HD), 2 * HD)
            parts.append(part)
            loads.append(
                (
                    lambda part=part: q[pl.ds(row, FRAME), part],
                    lambda part=part: window(k, 0, part),
                    lambda part=part: window(v, 1, part),
                    bias,
                )
            )
        for part, result in zip(parts, attend(loads)):
            out[:, part] = result
        return 0

    lax.fori_loop(0, pairs // unroll, step, 0)


def near_kernel(lo_ref, hi_ref, q, k, v, halo, out):
    attend_edge(True, lo_ref, hi_ref, q, k, v, (halo,), out)


def edge_cost(rows, width):
    return pl.CostEstimate(
        flops=8 * NEAR * NEAR * width,
        bytes_accessed=7 * rows * width,
        transcendentals=FRAME * NEAR * HEADS,
    )


def near_attention(lo, hi, q, k, v, halo):
    rows, width = q.shape
    return pl.pallas_call(
        near_kernel,
        out_shape=jax.ShapeDtypeStruct((FRAME, width), BF16),
        in_specs=[SMEM, SMEM] + [VMEM] * 4,
        out_specs=VMEM,
        compiler_params=pltpu.CompilerParams(vmem_limit_bytes=20 << 20),
        cost_estimate=edge_cost(rows, width),
        name="near_edge_attention",
    )(lo, hi, q, k, v, halo)


def adapt(value, narrow, factor):
    return (value.astype(F32) + ADAPTER_SCALE * dot(narrow, factor, NT)).astype(BF16)


def merge_kernel(layout, frozen, own_down, inner, near, *rest):
    refs, rest = rest[:-6], rest[-6:]
    merged, attended, factors, w, result, sems = rest
    shard, width = frozen.shape
    rows = result.shape[0]
    me = lax.axis_index("seq")
    kind = lax.axis_index("group")
    for ref, (swapped, masks) in zip(refs, layout):
        target = 1 - kind if swapped else kind
        for i, mask in enumerate(masks):
            at = pl.ds(pl.multiple_of((me ^ mask) * shard, shard), shard)
            factors[target, at, :] = ref[i]
    if not layout:
        factors[...] = refs[0][...]
    down, up = factors.at[0], factors.at[1]
    _, near_row = edge_side(True, rows)
    parts = ((inner, FRAME), (near, near_row))
    reduced = [dot(att[...], down[...], NN).astype(BF16) for att, _ in parts]
    stores = []

    def store(source, target):
        stores.append(pltpu.make_async_copy(source, target, sems.at[len(stores)]))
        stores[-1].start()

    for first in range(0, width, CHUNK):
        part = pl.ds(first, CHUNK)
        factor = up[part, :]
        w[:, part] = adapt(frozen[:, part], own_down[...], factor)
        store(w.at[:, part], merged.at[:, part])
        for narrow, (att, row) in zip(reduced, parts):
            result[pl.ds(row, att.shape[0]), part] = adapt(att[:, part], narrow, factor)
            at = (pl.ds(row, att.shape[0]), part)
            store(result.at[at], attended.at[at])
    for copy in stores:
        copy.wait()


def merge(frozen, own_down, inner, near, layout, pieces):
    shard, width = frozen.shape
    rank = own_down.shape[1]
    rows = 2 * NEAR
    return pl.pallas_call(
        functools.partial(merge_kernel, layout),
        out_shape=(
            jax.ShapeDtypeStruct((shard, width), BF16),
            jax.ShapeDtypeStruct((rows, width), BF16),
            jax.ShapeDtypeStruct((2, width, rank), BF16),
        ),
        in_specs=[VMEM] * (4 + len(pieces)),
        out_specs=(ANY, ANY, VMEM),
        scratch_shapes=[
            pltpu.VMEM((shard, width), BF16),
            pltpu.VMEM((rows, width), BF16),
            pltpu.SemaphoreType.DMA((3 * (width // CHUNK),)),
        ],
        compiler_params=pltpu.CompilerParams(vmem_limit_bytes=24 << 20),
        cost_estimate=pl.CostEstimate(
            flops=2 * (shard + 2 * rows) * width * rank,
            bytes_accessed=4 * (shard + rows) * width + 4 * width * rank,
            transcendentals=0,
        ),
        name="merge_and_adapter",
    )(frozen, own_down, inner, near, *pieces)


def far_kernel(lo_ref, hi_ref, q, k, v, direct, distant, factors, _, out, mixed, result, sems):
    rows, width = q.shape
    attend_edge(False, lo_ref, hi_ref, q, k, v, (direct, distant), mixed)
    narrow = dot(mixed[...], factors[0], NN).astype(BF16)
    _, row = edge_side(False, rows)
    stores = []
    for first in range(0, width, WIDE):
        part = pl.ds(first, WIDE)
        result[:, part] = adapt(mixed[:, part], narrow, factors[1, part, :])
        stores.append(
            pltpu.make_async_copy(
                result.at[:, part], out.at[pl.ds(row, FRAME), part], sems.at[len(stores)]
            )
        )
        stores[-1].start()
    for copy in stores:
        copy.wait()


def far_rows(lo, hi, q, k, v, direct, distant, factors, attended):
    rows, width = q.shape
    return pl.pallas_call(
        far_kernel,
        out_shape=jax.ShapeDtypeStruct((rows, width), BF16),
        in_specs=[SMEM, SMEM] + [VMEM] * 6 + [ANY],
        out_specs=ANY,
        input_output_aliases={8: 0},
        scratch_shapes=[
            pltpu.VMEM((FRAME, width), BF16),
            pltpu.VMEM((FRAME, width), BF16),
            pltpu.SemaphoreType.DMA((width // WIDE,)),
        ],
        compiler_params=pltpu.CompilerParams(vmem_limit_bytes=24 << 20),
        cost_estimate=edge_cost(rows, width),
        name="far_edge_rows",
    )(lo, hi, q, k, v, direct, distant, factors, attended)


def body(q, k, v, lo, hi, down, up, frozen):
    count = lax.axis_size("seq")
    rows = k.shape[0]
    odd = lax.rem(lax.axis_index("seq"), 2)

    def rim(start):
        return jnp.stack([lax.dynamic_slice_in_dim(x, start, FRAME, 0) for x in (k, v)])

    def swap(cells, mask):
        return lax.ppermute(cells, "seq", [(i, i ^ mask) for i in range(count)])

    def cross(cells):
        return lax.ppermute(cells, "group", [(0, 1), (1, 0)])

    def near_halo(odd):
        return swap(rim((1 - odd) * (rows - FRAME)), 1)

    direct_pairs, distant_pairs = (
        [(i + a, i + 1 - a) for i in range(first, count - 1, 4) for a in (0, 1)]
        for first in (1, 3)
    )
    far_rim = rim(odd * (rows - FRAME))
    up = up.T
    if lax.axis_size("group") != 2 or down.shape[0] % 32:
        both = lax.all_gather(jnp.stack([down, up]), "seq", axis=1, tiled=True)
        layout, pieces = [], [both]
        direct = lax.ppermute(far_rim, "seq", direct_pairs)
        distant = lax.ppermute(far_rim, "seq", distant_pairs)
        inner = inner_attention(lo, hi, q, k, v)
        near = near_attention(lo, hi, q, k, v, near_halo(odd))
    else:
        barrier = lax.optimization_barrier
        inner = inner_attention(lo, hi, q, k, v)
        cells = jnp.where(lax.axis_index("group") == 0, down, up)[None]
        masks = [0]
        steps = [2] + [count >> j for j in range(1, count.bit_length()) if count >> j > 2]
        for mask in steps[:-1]:
            cells = jnp.concatenate([cells, swap(cells, mask)])
            masks = masks + [have ^ mask for have in masks]
            if mask == 2:
                cells, far_rim = barrier((cells, far_rim))
                direct = lax.ppermute(far_rim, "seq", direct_pairs)
        halo = near_halo(odd)
        cells, inner, far_rim = barrier((cells, inner, far_rim))
        new = swap(cells, steps[-1])
        distant = lax.ppermute(far_rim, "seq", distant_pairs)
        early = cross(cells)
        near = near_attention(lo, hi, q, k, v, halo)
        new, near = barrier((new, near))
        late = cross(new)
        cells = jnp.concatenate([cells, new])
        masks = masks + [have ^ steps[-1] for have in masks]
        other = jnp.concatenate([early, late])
        other, direct = barrier((other, direct))
        across = [mask ^ 1 for mask in masks]
        layout = [(0, masks), (0, across), (1, masks), (1, across)]
        pieces = [cells, swap(cells, 1), other, swap(other, 1)]
    merged, attended, factors = merge(frozen, down, inner, near, layout, pieces)
    attended = far_rows(lo, hi, q, k, v, direct, distant, factors, attended)
    return (attended, merged)


def solution(mesh):
    rows = P(("group", "seq"), None)
    flat = P(("group", "seq"))
    return jax.shard_map(
        body,
        mesh=mesh,
        in_specs=(rows, rows, rows, flat, flat, P("seq", None), P(None, "seq"), P("seq", None)),
        out_specs=(rows, rows),
        check_vma=False,
    )
```

```python
import functools

import jax
import jax.numpy as jnp
from jax import lax
from jax.experimental import pallas as pl
from jax.experimental.pallas import tpu as pltpu
from jax.sharding import PartitionSpec as P

MODEL_WIDTH = 5120
HEADS = 40
HD = 128
FRAME = 64
NEAR = 2 * FRAME
CHUNK = 512
WIDE = 2 * CHUNK
SCORE_SCALE = HD ** (-0.5) * 1.4426950408889634
ADAPTER_SCALE = MODEL_WIDTH ** (-0.5)
FAR = -1e30
NT = (((1,), (1,)), ((), ()))
NN = (((1,), (0,)), ((), ()))
BF16 = jnp.bfloat16
F32 = jnp.float32
ANY = pl.BlockSpec(memory_space=pl.ANY)
SMEM = pl.BlockSpec(memory_space=pltpu.SMEM)
VMEM = pl.BlockSpec(memory_space=pltpu.VMEM)


def dot(a, b, dims):
    return lax.dot_general(a, b, dims, preferred_element_type=F32)


def clip_bias(lo, hi):
    position = lax.broadcasted_iota(jnp.int32, (NEAR, NEAR), 1)
    return jnp.where(position < hi - lo, 0.0, FAR).astype(F32)


def diagonal(top, bottom):
    zeros = jnp.zeros((FRAME, NEAR), BF16)
    return jnp.concatenate(
        [jnp.concatenate([top, zeros], axis=1), jnp.concatenate([zeros, bottom], axis=1)]
    )


def attend(loads):
    ones = jnp.ones((NEAR, HD), BF16)
    scores = []
    for load_q, load_k, _, bias in loads:
        q = load_q()
        scores.append(dot(diagonal(q[:, :HD], q[:, HD:]), load_k(), NT) * SCORE_SCALE + bias)
    weights = [jnp.exp2(s - jnp.max(s, axis=-1, keepdims=True)).astype(BF16) for s in scores]
    results = []
    for w, (_, _, load_v, _) in zip(weights, loads):
        v = load_v()
        values = jnp.concatenate(
            [jnp.concatenate([v[:, at : at + HD], ones], axis=1) for at in (0, HD)]
        )
        mixed = dot(diagonal(w[:FRAME], w[FRAME:]), values, NN)
        mixed = (mixed[:, :HD] * (1.0 / mixed[:, HD:])).astype(BF16)
        results.append(jnp.concatenate([mixed[:FRAME], mixed[FRAME:]], axis=1))
    return results


def inner_kernel(lo_ref, hi_ref, q_ref, k_ref, v_ref, o_ref):
    rows = q_ref.shape[0]
    base = lax.axis_index("seq") * rows
    loads, targets = [], []
    for row in (FRAME, NEAR):
        lo, hi = lo_ref[row], hi_ref[row]
        keys = pl.ds(pl.multiple_of(lo - base, FRAME), NEAR)
        bias = clip_bias(lo, hi)
        for col in range(0, WIDE, 2 * HD):
            part = slice(col, col + 2 * HD)
            targets.append((slice(row - FRAME, row), part))
            loads.append(
                (
                    lambda row=row, part=part: q_ref[row : row + FRAME, part],
                    lambda keys=keys, part=part: k_ref[keys, part],
                    lambda keys=keys, part=part: v_ref[keys, part],
                    bias,
                )
            )
    for target, result in zip(targets, attend(loads)):
        o_ref[target] = result


def inner_attention(lo, hi, q, k, v):
    rows, width = q.shape
    block = pl.BlockSpec((rows, WIDE), lambda i: (0, i))
    return pl.pallas_call(
        inner_kernel,
        grid=(width // WIDE,),
        out_shape=jax.ShapeDtypeStruct((NEAR, width), BF16),
        in_specs=[SMEM, SMEM, block, block, block],
        out_specs=pl.BlockSpec((NEAR, WIDE), lambda i: (0, i)),
        compiler_params=pltpu.CompilerParams(vmem_limit_bytes=16 << 20),
        cost_estimate=pl.CostEstimate(
            flops=16 * NEAR * NEAR * width,
            bytes_accessed=7 * rows * width,
            transcendentals=NEAR * NEAR * HEADS,
        ),
        name="inner_attention",
    )(lo, hi, q, k, v)


def edge_side(is_near, rows):
    right = lax.rem(lax.axis_index("seq"), 2) == (0 if is_near else 1)
    return right, pl.multiple_of(jnp.where(right, rows - FRAME, 0), FRAME)


def attend_edge(is_near, lo_ref, hi_ref, q, k, v, halos, out):
    rows, width = q.shape
    pairs = width // (2 * HD)
    unroll = next(n for n in (10, 8, 6, 5, 4, 2, 1) if pairs % n == 0)
    me = lax.axis_index("seq")
    base = me * rows
    right, row = edge_side(is_near, rows)
    first = pl.multiple_of(jnp.where(right, rows - NEAR, 0), NEAR)
    second = pl.multiple_of(first + FRAME, FRAME)
    lo, hi = lo_ref[row], hi_ref[row]
    before = lo < base
    after = jnp.logical_and(right, lo == base + rows - FRAME)
    direct = lax.rem(lax.div(me + 1, 2), 2) == 1

    def window(ref, kind, part):
        halo = halos[0][kind, :, part]
        if len(halos) == 2:
            halo = jnp.where(direct, halo, halos[1][kind, :, part])
        one, two = ref[pl.ds(first, FRAME), part], ref[pl.ds(second, FRAME), part]
        return jnp.concatenate(
            [
                jnp.where(before, halo, jnp.where(after, two, one)),
                jnp.where(before, one, jnp.where(after, halo, two)),
            ]
        )

    bias = clip_bias(lo, hi)

    def step(i, _):
        loads, parts = [], []
        for pair in range(unroll):
            part = pl.ds(pl.multiple_of((i * unroll + pair) * 2 * HD, 2 * HD), 2 * HD)
            parts.append(part)
            loads.append(
                (
                    lambda part=part: q[pl.ds(row, FRAME), part],
                    lambda part=part: window(k, 0, part),
                    lambda part=part: window(v, 1, part),
                    bias,
                )
            )
        for part, result in zip(parts, attend(loads)):
            out[:, part] = result
        return 0

    lax.fori_loop(0, pairs // unroll, step, 0)


def near_kernel(lo_ref, hi_ref, q, k, v, halo, out):
    attend_edge(True, lo_ref, hi_ref, q, k, v, (halo,), out)


def edge_cost(rows, width):
    return pl.CostEstimate(
        flops=8 * NEAR * NEAR * width,
        bytes_accessed=7 * rows * width,
        transcendentals=FRAME * NEAR * HEADS,
    )


def near_attention(lo, hi, q, k, v, halo):
    rows, width = q.shape
    return pl.pallas_call(
        near_kernel,
        out_shape=jax.ShapeDtypeStruct((FRAME, width), BF16),
        in_specs=[SMEM, SMEM] + [VMEM] * 4,
        out_specs=VMEM,
        compiler_params=pltpu.CompilerParams(vmem_limit_bytes=20 << 20),
        cost_estimate=edge_cost(rows, width),
        name="near_edge_attention",
    )(lo, hi, q, k, v, halo)


def adapt(value, narrow, factor):
    return (value.astype(F32) + ADAPTER_SCALE * dot(narrow, factor, NT)).astype(BF16)


def merge_kernel(layout, frozen, own_down, inner, near, *rest):
    refs, rest = rest[:-6], rest[-6:]
    merged, attended, factors, w, result, sems = rest
    shard, width = frozen.shape
    rows = result.shape[0]
    me = lax.axis_index("seq")
    kind = lax.axis_index("group")
    for ref, (swapped, masks) in zip(refs, layout):
        target = 1 - kind if swapped else kind
        for i, mask in enumerate(masks):
            at = pl.ds(pl.multiple_of((me ^ mask) * shard, shard), shard)
            factors[target, at, :] = ref[i]
    if not layout:
        factors[...] = refs[0][...]
    down, up = factors.at[0], factors.at[1]
    _, near_row = edge_side(True, rows)
    parts = ((inner, FRAME), (near, near_row))
    reduced = [dot(att[...], down[...], NN).astype(BF16) for att, _ in parts]
    stores = []

    def store(source, target):
        stores.append(pltpu.make_async_copy(source, target, sems.at[len(stores)]))
        stores[-1].start()

    for first in range(0, width, CHUNK):
        part = pl.ds(first, CHUNK)
        factor = up[part, :]
        w[:, part] = adapt(frozen[:, part], own_down[...], factor)
        store(w.at[:, part], merged.at[:, part])
        for narrow, (att, row) in zip(reduced, parts):
            result[pl.ds(row, att.shape[0]), part] = adapt(att[:, part], narrow, factor)
            at = (pl.ds(row, att.shape[0]), part)
            store(result.at[at], attended.at[at])
    for copy in stores:
        copy.wait()


def merge(frozen, own_down, inner, near, layout, pieces):
    shard, width = frozen.shape
    rank = own_down.shape[1]
    rows = 2 * NEAR
    return pl.pallas_call(
        functools.partial(merge_kernel, layout),
        out_shape=(
            jax.ShapeDtypeStruct((shard, width), BF16),
            jax.ShapeDtypeStruct((rows, width), BF16),
            jax.ShapeDtypeStruct((2, width, rank), BF16),
        ),
        in_specs=[VMEM] * (4 + len(pieces)),
        out_specs=(ANY, ANY, VMEM),
        scratch_shapes=[
            pltpu.VMEM((shard, width), BF16),
            pltpu.VMEM((rows, width), BF16),
            pltpu.SemaphoreType.DMA((3 * (width // CHUNK),)),
        ],
        compiler_params=pltpu.CompilerParams(vmem_limit_bytes=24 << 20),
        cost_estimate=pl.CostEstimate(
            flops=2 * (shard + 2 * rows) * width * rank,
            bytes_accessed=4 * (shard + rows) * width + 4 * width * rank,
            transcendentals=0,
        ),
        name="merge_and_adapter",
    )(frozen, own_down, inner, near, *pieces)


def far_kernel(lo_ref, hi_ref, q, k, v, direct, distant, factors, _, out, mixed, result, sems):
    rows, width = q.shape
    attend_edge(False, lo_ref, hi_ref, q, k, v, (direct, distant), mixed)
    narrow = dot(mixed[...], factors[0], NN).astype(BF16)
    _, row = edge_side(False, rows)
    stores = []
    for first in range(0, width, WIDE):
        part = pl.ds(first, WIDE)
        result[:, part] = adapt(mixed[:, part], narrow, factors[1, part, :])
        stores.append(
            pltpu.make_async_copy(
                result.at[:, part], out.at[pl.ds(row, FRAME), part], sems.at[len(stores)]
            )
        )
        stores[-1].start()
    for copy in stores:
        copy.wait()


def far_rows(lo, hi, q, k, v, direct, distant, factors, attended):
    rows, width = q.shape
    return pl.pallas_call(
        far_kernel,
        out_shape=jax.ShapeDtypeStruct((rows, width), BF16),
        in_specs=[SMEM, SMEM] + [VMEM] * 6 + [ANY],
        out_specs=ANY,
        input_output_aliases={8: 0},
        scratch_shapes=[
            pltpu.VMEM((FRAME, width), BF16),
            pltpu.VMEM((FRAME, width), BF16),
            pltpu.SemaphoreType.DMA((width // WIDE,)),
        ],
        compiler_params=pltpu.CompilerParams(vmem_limit_bytes=24 << 20),
        cost_estimate=edge_cost(rows, width),
        name="far_edge_rows",
    )(lo, hi, q, k, v, direct, distant, factors, attended)


def body(q, k, v, lo, hi, down, up, frozen):
    count = lax.axis_size("seq")
    rows = k.shape[0]
    odd = lax.rem(lax.axis_index("seq"), 2)

    def rim(start):
        return jnp.stack([lax.dynamic_slice_in_dim(x, start, FRAME, 0) for x in (k, v)])

    def swap(cells, mask):
        return lax.ppermute(cells, "seq", [(i, i ^ mask) for i in range(count)])

    def cross(cells):
        return lax.ppermute(cells, "group", [(0, 1), (1, 0)])

    def near_halo(odd):
        return swap(rim((1 - odd) * (rows - FRAME)), 1)

    direct_pairs, distant_pairs = (
        [(i + a, i + 1 - a) for i in range(first, count - 1, 4) for a in (0, 1)]
        for first in (1, 3)
    )
    far_rim = rim(odd * (rows - FRAME))
    up = up.T
    steps = [1 << bit for bit in range(1, count.bit_length() - 1)]
    if lax.axis_size("group") != 2 or len(steps) != 3 or down.shape[0] % 32:
        both = lax.all_gather(jnp.stack([down, up]), "seq", axis=1, tiled=True)
        layout, pieces = [], [both]
        direct = lax.ppermute(far_rim, "seq", direct_pairs)
        distant = lax.ppermute(far_rim, "seq", distant_pairs)
        inner = inner_attention(lo, hi, q, k, v)
        near = near_attention(lo, hi, q, k, v, near_halo(odd))
    else:
        barrier = lax.optimization_barrier
        join = jnp.concatenate
        inner = inner_attention(lo, hi, q, k, v)
        halo = near_halo(odd)
        side, short, long = steps
        own = jnp.where(lax.axis_index("group") == 0, down, up)[None]
        plane = join([own, swap(own, side)])
        plane, far_rim = barrier((plane, far_rim))
        direct = lax.ppermute(far_rim, "seq", direct_pairs)
        beyond = swap(plane, long)
        beside = swap(plane, short)
        crossed = [cross(plane)]
        beyond, beside, crossed, inner, far_rim = barrier(
            (beyond, beside, crossed, inner, far_rim)
        )
        last = swap(beyond, short)
        distant = lax.ppermute(far_rim, "seq", distant_pairs)
        crossed.append(cross(join([beside, beyond])))
        near = near_attention(lo, hi, q, k, v, halo)
        last, near = barrier((last, near))
        crossed.append(cross(last))
        cells, other = join([plane, beside, beyond, last]), join(crossed)
        masks = [a ^ b for a in (0, short, long, short ^ long) for b in (0, side)]
        across = [mask ^ 1 for mask in masks]
        layout = [(0, masks), (0, across), (1, masks), (1, across)]
        other, direct = barrier((other, direct))
        pieces = [cells, swap(cells, 1), other, swap(other, 1)]
    merged, attended, factors = merge(frozen, down, inner, near, layout, pieces)
    attended = far_rows(lo, hi, q, k, v, direct, distant, factors, attended)
    return (attended, merged)


def solution(mesh):
    rows = P(("group", "seq"), None)
    flat = P(("group", "seq"))
    return jax.shard_map(
        body,
        mesh=mesh,
        in_specs=(rows, rows, rows, flat, flat, P("seq", None), P(None, "seq"), P("seq", None)),
        out_specs=(rows, rows),
        check_vma=False,
    )
```

```python
import functools

import jax
import jax.numpy as jnp
from jax import lax
from jax.experimental import pallas as pl
from jax.experimental.pallas import tpu as pltpu
from jax.sharding import PartitionSpec as P

MODEL_WIDTH = 5120
HEADS = 40
HD = 128
FRAME = 64
NEAR = 2 * FRAME
CHUNK = 512
WIDE = 2 * CHUNK
SCORE_SCALE = HD ** (-0.5) * 1.4426950408889634
ADAPTER_SCALE = MODEL_WIDTH ** (-0.5)
FAR = -1e30
NT = (((1,), (1,)), ((), ()))
NN = (((1,), (0,)), ((), ()))
BF16 = jnp.bfloat16
F32 = jnp.float32
ANY = pl.BlockSpec(memory_space=pl.ANY)
SMEM = pl.BlockSpec(memory_space=pltpu.SMEM)
VMEM = pl.BlockSpec(memory_space=pltpu.VMEM)


def dot(a, b, dims):
    return lax.dot_general(a, b, dims, preferred_element_type=F32)


def clip_bias(lo, hi):
    position = lax.broadcasted_iota(jnp.int32, (NEAR, NEAR), 1)
    return jnp.where(position < hi - lo, 0.0, FAR).astype(F32)


def diagonal(top, bottom):
    zeros = jnp.zeros((FRAME, NEAR), BF16)
    return jnp.concatenate(
        [jnp.concatenate([top, zeros], axis=1), jnp.concatenate([zeros, bottom], axis=1)]
    )


def attend(loads):
    ones = jnp.ones((NEAR, HD), BF16)
    scores = []
    for load_q, load_k, _, bias in loads:
        q = load_q()
        scores.append(dot(diagonal(q[:, :HD], q[:, HD:]), load_k(), NT) * SCORE_SCALE + bias)
    weights = [jnp.exp2(s - jnp.max(s, axis=-1, keepdims=True)).astype(BF16) for s in scores]
    results = []
    for w, (_, _, load_v, _) in zip(weights, loads):
        v = load_v()
        values = jnp.concatenate(
            [jnp.concatenate([v[:, at : at + HD], ones], axis=1) for at in (0, HD)]
        )
        mixed = dot(diagonal(w[:FRAME], w[FRAME:]), values, NN)
        mixed = (mixed[:, :HD] * (1.0 / mixed[:, HD:])).astype(BF16)
        results.append(jnp.concatenate([mixed[:FRAME], mixed[FRAME:]], axis=1))
    return results


def inner_kernel(lo_ref, hi_ref, q_ref, k_ref, v_ref, o_ref):
    rows = q_ref.shape[0]
    base = lax.axis_index("seq") * rows
    loads, targets = [], []
    for row in (FRAME, NEAR):
        lo, hi = lo_ref[row], hi_ref[row]
        keys = pl.ds(pl.multiple_of(lo - base, FRAME), NEAR)
        bias = clip_bias(lo, hi)
        for col in range(0, WIDE, 2 * HD):
            part = slice(col, col + 2 * HD)
            targets.append((slice(row - FRAME, row), part))
            loads.append(
                (
                    lambda row=row, part=part: q_ref[row : row + FRAME, part],
                    lambda keys=keys, part=part: k_ref[keys, part],
                    lambda keys=keys, part=part: v_ref[keys, part],
                    bias,
                )
            )
    for target, result in zip(targets, attend(loads)):
        o_ref[target] = result


def inner_attention(lo, hi, q, k, v):
    rows, width = q.shape
    block = pl.BlockSpec((rows, WIDE), lambda i: (0, i))
    return pl.pallas_call(
        inner_kernel,
        grid=(width // WIDE,),
        out_shape=jax.ShapeDtypeStruct((NEAR, width), BF16),
        in_specs=[SMEM, SMEM, block, block, block],
        out_specs=pl.BlockSpec((NEAR, WIDE), lambda i: (0, i)),
        compiler_params=pltpu.CompilerParams(vmem_limit_bytes=16 << 20),
        cost_estimate=pl.CostEstimate(
            flops=16 * NEAR * NEAR * width,
            bytes_accessed=7 * rows * width,
            transcendentals=NEAR * NEAR * HEADS,
        ),
        name="inner_attention",
    )(lo, hi, q, k, v)


def edge_side(is_near, rows):
    right = lax.rem(lax.axis_index("seq"), 2) == (0 if is_near else 1)
    return right, pl.multiple_of(jnp.where(right, rows - FRAME, 0), FRAME)


def attend_edge(is_near, lo_ref, hi_ref, q, k, v, halos, out):
    rows, width = q.shape
    pairs = width // (2 * HD)
    unroll = next(n for n in (10, 8, 6, 5, 4, 2, 1) if pairs % n == 0)
    me = lax.axis_index("seq")
    base = me * rows
    right, row = edge_side(is_near, rows)
    first = pl.multiple_of(jnp.where(right, rows - NEAR, 0), NEAR)
    second = pl.multiple_of(first + FRAME, FRAME)
    lo, hi = lo_ref[row], hi_ref[row]
    before = lo < base
    after = jnp.logical_and(right, lo == base + rows - FRAME)
    direct = lax.rem(lax.div(me + 1, 2), 2) == 1

    def window(ref, kind, part):
        halo = halos[kind][:, part]
        if len(halos) == 4:
            halo = jnp.where(direct, halo, halos[2 + kind][:, part])
        one, two = ref[pl.ds(first, FRAME), part], ref[pl.ds(second, FRAME), part]
        return jnp.concatenate(
            [
                jnp.where(before, halo, jnp.where(after, two, one)),
                jnp.where(before, one, jnp.where(after, halo, two)),
            ]
        )

    bias = clip_bias(lo, hi)

    def step(i, _):
        loads, parts = [], []
        for pair in range(unroll):
            part = pl.ds(pl.multiple_of((i * unroll + pair) * 2 * HD, 2 * HD), 2 * HD)
            parts.append(part)
            loads.append(
                (
                    lambda part=part: q[pl.ds(row, FRAME), part],
                    lambda part=part: window(k, 0, part),
                    lambda part=part: window(v, 1, part),
                    bias,
                )
            )
        for part, result in zip(parts, attend(loads)):
            out[:, part] = result
        return 0

    lax.fori_loop(0, pairs // unroll, step, 0)


def near_kernel(lo_ref, hi_ref, q, k, v, halo, out):
    attend_edge(True, lo_ref, hi_ref, q, k, v, (halo.at[0], halo.at[1]), out)


def edge_cost(rows, width):
    return pl.CostEstimate(
        flops=8 * NEAR * NEAR * width,
        bytes_accessed=7 * rows * width,
        transcendentals=FRAME * NEAR * HEADS,
    )


def near_attention(lo, hi, q, k, v, halo):
    rows, width = q.shape
    return pl.pallas_call(
        near_kernel,
        out_shape=jax.ShapeDtypeStruct((FRAME, width), BF16),
        in_specs=[SMEM, SMEM] + [VMEM] * 4,
        out_specs=VMEM,
        compiler_params=pltpu.CompilerParams(vmem_limit_bytes=20 << 20),
        cost_estimate=edge_cost(rows, width),
        name="near_edge_attention",
    )(lo, hi, q, k, v, halo)


def adapt(value, narrow, factor):
    return (value.astype(F32) + ADAPTER_SCALE * dot(narrow, factor, NT)).astype(BF16)


def merge_kernel(layout, frozen, own_down, inner, near, *rest):
    refs, rest = rest[:-6], rest[-6:]
    merged, attended, factors, w, result, sems = rest
    shard, width = frozen.shape
    rows = result.shape[0]
    me = lax.axis_index("seq")
    kind = lax.axis_index("group")
    for ref, (swapped, masks) in zip(refs, layout):
        target = 1 - kind if swapped else kind
        for i, mask in enumerate(masks):
            at = pl.ds(pl.multiple_of((me ^ mask) * shard, shard), shard)
            factors[target, at, :] = ref[i]
    if not layout:
        factors[...] = refs[0][...]
    down, up = factors.at[0], factors.at[1]
    _, near_row = edge_side(True, rows)
    parts = ((inner, FRAME), (near, near_row))
    reduced = [dot(att[...], down[...], NN).astype(BF16) for att, _ in parts]
    stores = []

    def store(source, target):
        stores.append(pltpu.make_async_copy(source, target, sems.at[len(stores)]))
        stores[-1].start()

    for first in range(0, width, CHUNK):
        part = pl.ds(first, CHUNK)
        factor = up[part, :]
        w[:, part] = adapt(frozen[:, part], own_down[...], factor)
        store(w.at[:, part], merged.at[:, part])
        for narrow, (att, row) in zip(reduced, parts):
            result[pl.ds(row, att.shape[0]), part] = adapt(att[:, part], narrow, factor)
            at = (pl.ds(row, att.shape[0]), part)
            store(result.at[at], attended.at[at])
    for copy in stores:
        copy.wait()


def merge(frozen, own_down, inner, near, layout, pieces):
    shard, width = frozen.shape
    rank = own_down.shape[1]
    rows = 2 * NEAR
    return pl.pallas_call(
        functools.partial(merge_kernel, layout),
        out_shape=(
            jax.ShapeDtypeStruct((shard, width), BF16),
            jax.ShapeDtypeStruct((rows, width), BF16),
            jax.ShapeDtypeStruct((2, width, rank), BF16),
        ),
        in_specs=[VMEM] * (4 + len(pieces)),
        out_specs=(ANY, ANY, VMEM),
        scratch_shapes=[
            pltpu.VMEM((shard, width), BF16),
            pltpu.VMEM((rows, width), BF16),
            pltpu.SemaphoreType.DMA((3 * (width // CHUNK),)),
        ],
        compiler_params=pltpu.CompilerParams(vmem_limit_bytes=24 << 20),
        cost_estimate=pl.CostEstimate(
            flops=2 * (shard + 2 * rows) * width * rank,
            bytes_accessed=4 * (shard + rows) * width + 4 * width * rank,
            transcendentals=0,
        ),
        name="merge_and_adapter",
    )(frozen, own_down, inner, near, *pieces)


def far_kernel(lo_ref, hi_ref, q, k, v, *rest):
    halos, (factors, _, out, mixed, result, sems) = rest[:3], rest[3:]
    rows, width = q.shape
    halos = (*halos[:2], halos[2].at[0], halos[2].at[1])
    attend_edge(False, lo_ref, hi_ref, q, k, v, halos, mixed)
    narrow = dot(mixed[...], factors[0], NN).astype(BF16)
    _, row = edge_side(False, rows)
    stores = []
    for first in range(0, width, WIDE):
        part = pl.ds(first, WIDE)
        result[:, part] = adapt(mixed[:, part], narrow, factors[1, part, :])
        stores.append(
            pltpu.make_async_copy(
                result.at[:, part], out.at[pl.ds(row, FRAME), part], sems.at[len(stores)]
            )
        )
        stores[-1].start()
    for copy in stores:
        copy.wait()


def far_rows(lo, hi, q, k, v, direct, distant, factors, attended):
    rows, width = q.shape
    return pl.pallas_call(
        far_kernel,
        out_shape=jax.ShapeDtypeStruct((rows, width), BF16),
        in_specs=[SMEM, SMEM] + [VMEM] * 7 + [ANY],
        out_specs=ANY,
        input_output_aliases={9: 0},
        scratch_shapes=[
            pltpu.VMEM((FRAME, width), BF16),
            pltpu.VMEM((FRAME, width), BF16),
            pltpu.SemaphoreType.DMA((width // WIDE,)),
        ],
        compiler_params=pltpu.CompilerParams(vmem_limit_bytes=24 << 20),
        cost_estimate=edge_cost(rows, width),
        name="far_edge_rows",
    )(lo, hi, q, k, v, *direct, distant, factors, attended)


def body(q, k, v, lo, hi, down, up, frozen):
    count = lax.axis_size("seq")
    rows = k.shape[0]
    odd = lax.rem(lax.axis_index("seq"), 2)

    def rim(start):
        return [lax.dynamic_slice_in_dim(x, start, FRAME, 0) for x in (k, v)]

    def send(cells, pairs):
        return [lax.ppermute(x, "seq", pairs) for x in cells]

    def swap(cells, mask):
        return lax.ppermute(cells, "seq", [(i, i ^ mask) for i in range(count)])

    def cross(cells):
        return lax.ppermute(cells, "group", [(0, 1), (1, 0)])

    direct_pairs, distant_pairs = (
        [(i + a, i + 1 - a) for i in range(first, count - 1, 4) for a in (0, 1)]
        for first in (1, 3)
    )
    far_rim = rim(odd * (rows - FRAME))
    near_rim = jnp.stack(rim((1 - odd) * (rows - FRAME)))
    up = up.T
    steps = [1 << bit for bit in range(1, count.bit_length() - 1)]
    if lax.axis_size("group") != 2 or len(steps) != 3 or down.shape[0] % 32:
        both = lax.all_gather(jnp.stack([down, up]), "seq", axis=1, tiled=True)
        layout, pieces = [], [both]
        direct = send(far_rim, direct_pairs)
        distant = lax.ppermute(jnp.stack(far_rim), "seq", distant_pairs)
        inner = inner_attention(lo, hi, q, k, v)
        near = near_attention(lo, hi, q, k, v, swap(near_rim, 1))
    else:
        barrier = lax.optimization_barrier
        join = jnp.concatenate
        side, short, long = steps
        own = jnp.where(lax.axis_index("group") == 0, down, up)[None]
        plane = join([own, swap(own, side)])
        plane, far_rim, near_rim = barrier((plane, far_rim, near_rim))
        halo = swap(near_rim, 1)
        direct = send(far_rim, direct_pairs)
        beyond = swap(plane, long)
        beside = swap(plane, short)
        crossed = [cross(plane)]
        beyond, beside, crossed, far_rim = barrier(
            (beyond, beside, crossed, far_rim)
        )
        last = swap(beyond, short)
        distant = lax.ppermute(jnp.stack(far_rim), "seq", distant_pairs)
        crossed.append(cross(join([beside, beyond])))
        last, direct, crossed[1], lo_later = barrier((last, direct, crossed[1], lo))
        inner = inner_attention(lo_later, hi, q, k, v)
        near = near_attention(lo_later, hi, q, k, v, halo)
        crossed.append(cross(last))
        cells, other = join([plane, beside, beyond, last]), join(crossed)
        other, inner = barrier((other, inner))
        masks = [a ^ b for a in (0, short, long, short ^ long) for b in (0, side)]
        across = [mask ^ 1 for mask in masks]
        layout = [(0, masks), (0, across), (1, masks), (1, across)]
        pieces = [cells, swap(cells, 1), other, swap(other, 1)]
    merged, attended, factors = merge(frozen, down, inner, near, layout, pieces)
    attended = far_rows(lo, hi, q, k, v, direct, distant, factors, attended)
    return (attended, merged)


def solution(mesh):
    rows = P(("group", "seq"), None)
    flat = P(("group", "seq"))
    return jax.shard_map(
        body,
        mesh=mesh,
        in_specs=(rows, rows, rows, flat, flat, P("seq", None), P(None, "seq"), P("seq", None)),
        out_specs=(rows, rows),
        check_vma=False,
    )
```

```python
import functools

import jax
import jax.numpy as jnp
from jax import lax
from jax.experimental import pallas as pl
from jax.experimental.pallas import tpu as pltpu
from jax.sharding import PartitionSpec as P

MODEL_WIDTH = 5120
HEADS = 40
HD = 128
FRAME = 64
NEAR = 2 * FRAME
CHUNK = 512
WIDE = 2 * CHUNK
SCORE_SCALE = HD ** (-0.5) * 1.4426950408889634
ADAPTER_SCALE = MODEL_WIDTH ** (-0.5)
FAR = -1e30
NT = (((1,), (1,)), ((), ()))
NN = (((1,), (0,)), ((), ()))
BF16 = jnp.bfloat16
F32 = jnp.float32
ANY = pl.BlockSpec(memory_space=pl.ANY)
SMEM = pl.BlockSpec(memory_space=pltpu.SMEM)
VMEM = pl.BlockSpec(memory_space=pltpu.VMEM)


def dot(a, b, dims):
    return lax.dot_general(a, b, dims, preferred_element_type=F32)


def clip_bias(lo, hi):
    position = lax.broadcasted_iota(jnp.int32, (NEAR, NEAR), 1)
    return jnp.where(position < hi - lo, 0.0, FAR).astype(F32)


def diagonal(top, bottom):
    zeros = jnp.zeros((FRAME, NEAR), BF16)
    return jnp.concatenate(
        [jnp.concatenate([top, zeros], axis=1), jnp.concatenate([zeros, bottom], axis=1)]
    )


def attend(loads):
    ones = jnp.ones((NEAR, HD), BF16)
    scores = []
    for load_q, load_k, _, bias in loads:
        q = load_q()
        scores.append(dot(diagonal(q[:, :HD], q[:, HD:]), load_k(), NT) * SCORE_SCALE + bias)
    weights = [jnp.exp2(s - jnp.max(s, axis=-1, keepdims=True)).astype(BF16) for s in scores]
    results = []
    for w, (_, _, load_v, _) in zip(weights, loads):
        v = load_v()
        values = jnp.concatenate(
            [jnp.concatenate([v[:, at : at + HD], ones], axis=1) for at in (0, HD)]
        )
        mixed = dot(diagonal(w[:FRAME], w[FRAME:]), values, NN)
        mixed = (mixed[:, :HD] * (1.0 / mixed[:, HD:])).astype(BF16)
        results.append(jnp.concatenate([mixed[:FRAME], mixed[FRAME:]], axis=1))
    return results


def inner_kernel(lo_ref, hi_ref, q_ref, k_ref, v_ref, o_ref):
    rows = q_ref.shape[0]
    base = lax.axis_index("seq") * rows
    loads, targets = [], []
    for row in (FRAME, NEAR):
        lo, hi = lo_ref[row], hi_ref[row]
        keys = pl.ds(pl.multiple_of(lo - base, FRAME), NEAR)
        bias = clip_bias(lo, hi)
        for col in range(0, WIDE, 2 * HD):
            part = slice(col, col + 2 * HD)
            targets.append((slice(row - FRAME, row), part))
            loads.append(
                (
                    lambda row=row, part=part: q_ref[row : row + FRAME, part],
                    lambda keys=keys, part=part: k_ref[keys, part],
                    lambda keys=keys, part=part: v_ref[keys, part],
                    bias,
                )
            )
    for target, result in zip(targets, attend(loads)):
        o_ref[target] = result


def inner_attention(lo, hi, q, k, v):
    rows, width = q.shape
    block = pl.BlockSpec((rows, WIDE), lambda i: (0, i))
    return pl.pallas_call(
        inner_kernel,
        grid=(width // WIDE,),
        out_shape=jax.ShapeDtypeStruct((NEAR, width), BF16),
        in_specs=[SMEM, SMEM, block, block, block],
        out_specs=pl.BlockSpec((NEAR, WIDE), lambda i: (0, i)),
        compiler_params=pltpu.CompilerParams(vmem_limit_bytes=16 << 20),
        cost_estimate=pl.CostEstimate(
            flops=16 * NEAR * NEAR * width,
            bytes_accessed=7 * rows * width,
            transcendentals=NEAR * NEAR * HEADS,
        ),
        name="inner_attention",
    )(lo, hi, q, k, v)


def edge_side(is_near, rows):
    right = lax.rem(lax.axis_index("seq"), 2) == (0 if is_near else 1)
    return right, pl.multiple_of(jnp.where(right, rows - FRAME, 0), FRAME)


def attend_edge(is_near, lo_ref, hi_ref, q, k, v, halos, out):
    rows, width = q.shape
    pairs = width // (2 * HD)
    unroll = next(n for n in (10, 8, 6, 5, 4, 2, 1) if pairs % n == 0)
    me = lax.axis_index("seq")
    base = me * rows
    right, row = edge_side(is_near, rows)
    first = pl.multiple_of(jnp.where(right, rows - NEAR, 0), NEAR)
    second = pl.multiple_of(first + FRAME, FRAME)
    lo, hi = lo_ref[row], hi_ref[row]
    before = lo < base
    after = jnp.logical_and(right, lo == base + rows - FRAME)
    direct = lax.rem(lax.div(me + 1, 2), 2) == 1

    def window(ref, kind, part):
        halo = halos[kind][:, part]
        if len(halos) == 4:
            halo = jnp.where(direct, halo, halos[2 + kind][:, part])
        one, two = ref[pl.ds(first, FRAME), part], ref[pl.ds(second, FRAME), part]
        return jnp.concatenate(
            [
                jnp.where(before, halo, jnp.where(after, two, one)),
                jnp.where(before, one, jnp.where(after, halo, two)),
            ]
        )

    bias = clip_bias(lo, hi)

    def step(i, _):
        loads, parts = [], []
        for pair in range(unroll):
            part = pl.ds(pl.multiple_of((i * unroll + pair) * 2 * HD, 2 * HD), 2 * HD)
            parts.append(part)
            loads.append(
                (
                    lambda part=part: q[pl.ds(row, FRAME), part],
                    lambda part=part: window(k, 0, part),
                    lambda part=part: window(v, 1, part),
                    bias,
                )
            )
        for part, result in zip(parts, attend(loads)):
            out[:, part] = result
        return 0

    lax.fori_loop(0, pairs // unroll, step, 0)


def near_kernel(lo_ref, hi_ref, q, k, v, halo, out):
    attend_edge(True, lo_ref, hi_ref, q, k, v, (halo.at[0], halo.at[1]), out)


def edge_cost(rows, width):
    return pl.CostEstimate(
        flops=8 * NEAR * NEAR * width,
        bytes_accessed=7 * rows * width,
        transcendentals=FRAME * NEAR * HEADS,
    )


def near_attention(lo, hi, q, k, v, halo):
    rows, width = q.shape
    return pl.pallas_call(
        near_kernel,
        out_shape=jax.ShapeDtypeStruct((FRAME, width), BF16),
        in_specs=[SMEM, SMEM] + [VMEM] * 4,
        out_specs=VMEM,
        compiler_params=pltpu.CompilerParams(vmem_limit_bytes=20 << 20),
        cost_estimate=edge_cost(rows, width),
        name="near_edge_attention",
    )(lo, hi, q, k, v, halo)


def adapt(value, narrow, factor):
    return (value.astype(F32) + ADAPTER_SCALE * dot(narrow, factor, NT)).astype(BF16)


def merge_kernel(layout, frozen, own_down, inner, near, *rest):
    refs, rest = rest[:-6], rest[-6:]
    merged, attended, factors, w, result, sems = rest
    shard, width = frozen.shape
    rows = result.shape[0]
    me = lax.axis_index("seq")
    kind = lax.axis_index("group")
    for ref, (swapped, masks) in zip(refs, layout):
        target = 1 - kind if swapped else kind
        for i, mask in enumerate(masks):
            at = pl.ds(pl.multiple_of((me ^ mask) * shard, shard), shard)
            factors[target, at, :] = ref[i]
    if not layout:
        factors[...] = refs[0][...]
    down, up = factors.at[0], factors.at[1]
    _, near_row = edge_side(True, rows)
    parts = ((inner, FRAME), (near, near_row))
    reduced = [dot(att[...], down[...], NN).astype(BF16) for att, _ in parts]
    stores = []

    def store(source, target):
        stores.append(pltpu.make_async_copy(source, target, sems.at[len(stores)]))
        stores[-1].start()

    for first in range(0, width, CHUNK):
        part = pl.ds(first, CHUNK)
        factor = up[part, :]
        w[:, part] = adapt(frozen[:, part], own_down[...], factor)
        store(w.at[:, part], merged.at[:, part])
        for narrow, (att, row) in zip(reduced, parts):
            result[pl.ds(row, att.shape[0]), part] = adapt(att[:, part], narrow, factor)
            at = (pl.ds(row, att.shape[0]), part)
            store(result.at[at], attended.at[at])
    for copy in stores:
        copy.wait()


def merge(frozen, own_down, inner, near, layout, pieces):
    shard, width = frozen.shape
    rank = own_down.shape[1]
    rows = 2 * NEAR
    return pl.pallas_call(
        functools.partial(merge_kernel, layout),
        out_shape=(
            jax.ShapeDtypeStruct((shard, width), BF16),
            jax.ShapeDtypeStruct((rows, width), BF16),
            jax.ShapeDtypeStruct((2, width, rank), BF16),
        ),
        in_specs=[VMEM] * (4 + len(pieces)),
        out_specs=(ANY, ANY, VMEM),
        scratch_shapes=[
            pltpu.VMEM((shard, width), BF16),
            pltpu.VMEM((rows, width), BF16),
            pltpu.SemaphoreType.DMA((3 * (width // CHUNK),)),
        ],
        compiler_params=pltpu.CompilerParams(vmem_limit_bytes=24 << 20),
        cost_estimate=pl.CostEstimate(
            flops=2 * (shard + 2 * rows) * width * rank,
            bytes_accessed=4 * (shard + rows) * width + 4 * width * rank,
            transcendentals=0,
        ),
        name="merge_and_adapter",
    )(frozen, own_down, inner, near, *pieces)


def far_kernel(lo_ref, hi_ref, q, k, v, *rest):
    halos, (factors, _, out, mixed, result, sems) = rest[:3], rest[3:]
    rows, width = q.shape
    halos = (*halos[:2], halos[2].at[0], halos[2].at[1])
    attend_edge(False, lo_ref, hi_ref, q, k, v, halos, mixed)
    narrow = dot(mixed[...], factors[0], NN).astype(BF16)
    _, row = edge_side(False, rows)
    stores = []
    for first in range(0, width, WIDE):
        part = pl.ds(first, WIDE)
        result[:, part] = adapt(mixed[:, part], narrow, factors[1, part, :])
        stores.append(
            pltpu.make_async_copy(
                result.at[:, part], out.at[pl.ds(row, FRAME), part], sems.at[len(stores)]
            )
        )
        stores[-1].start()
    for copy in stores:
        copy.wait()


def far_rows(lo, hi, q, k, v, direct, distant, factors, attended):
    rows, width = q.shape
    return pl.pallas_call(
        far_kernel,
        out_shape=jax.ShapeDtypeStruct((rows, width), BF16),
        in_specs=[SMEM, SMEM] + [VMEM] * 7 + [ANY],
        out_specs=ANY,
        input_output_aliases={9: 0},
        scratch_shapes=[
            pltpu.VMEM((FRAME, width), BF16),
            pltpu.VMEM((FRAME, width), BF16),
            pltpu.SemaphoreType.DMA((width // WIDE,)),
        ],
        compiler_params=pltpu.CompilerParams(vmem_limit_bytes=24 << 20),
        cost_estimate=edge_cost(rows, width),
        name="far_edge_rows",
    )(lo, hi, q, k, v, *direct, distant, factors, attended)


def body(q, k, v, lo, hi, down, up, frozen):
    count = lax.axis_size("seq")
    rows = k.shape[0]
    odd = lax.rem(lax.axis_index("seq"), 2)

    def rim(start):
        return [lax.dynamic_slice_in_dim(x, start, FRAME, 0) for x in (k, v)]

    def send(cells, pairs):
        return [lax.ppermute(x, "seq", pairs) for x in cells]

    def swap(cells, mask):
        return lax.ppermute(cells, "seq", [(i, i ^ mask) for i in range(count)])

    def cross(cells):
        return lax.ppermute(cells, "group", [(0, 1), (1, 0)])

    direct_pairs, distant_pairs = (
        [(i + a, i + 1 - a) for i in range(first, count - 1, 4) for a in (0, 1)]
        for first in (1, 3)
    )
    far_rim = rim(odd * (rows - FRAME))
    near_rim = jnp.stack(rim((1 - odd) * (rows - FRAME)))
    up = up.T
    steps = [1 << bit for bit in range(1, count.bit_length() - 1)]
    if lax.axis_size("group") != 2 or len(steps) != 3 or down.shape[0] % 32:
        both = lax.all_gather(jnp.stack([down, up]), "seq", axis=1, tiled=True)
        layout, pieces = [], [both]
        direct = send(far_rim, direct_pairs)
        distant = lax.ppermute(jnp.stack(far_rim), "seq", distant_pairs)
        inner = inner_attention(lo, hi, q, k, v)
        near = near_attention(lo, hi, q, k, v, swap(near_rim, 1))
    else:
        barrier = lax.optimization_barrier
        join = jnp.concatenate
        side, short, long = steps
        own = jnp.where(lax.axis_index("group") == 0, down, up)[None]
        plane = join([own, swap(own, side)])
        direct = send(far_rim, direct_pairs)
        plane, near_rim = barrier((plane, near_rim))
        halo = swap(near_rim, 1)
        beyond = swap(plane, long)
        beside = swap(plane, short)
        crossed = [cross(plane)]
        beyond, beside, crossed = barrier((beyond, beside, crossed))
        far_rim, direct = barrier((far_rim, direct))
        last = swap(beyond, short)
        distant = lax.ppermute(jnp.stack(far_rim), "seq", distant_pairs)
        crossed.append(cross(join([beside, beyond])))
        last, crossed[1], lo_later = barrier((last, crossed[1], lo))
        inner = inner_attention(lo_later, hi, q, k, v)
        near = near_attention(lo_later, hi, q, k, v, halo)
        crossed.append(cross(last))
        cells, other = join([plane, beside, beyond, last]), join(crossed)
        other, inner = barrier((other, inner))
        masks = [a ^ b for a in (0, short, long, short ^ long) for b in (0, side)]
        across = [mask ^ 1 for mask in masks]
        layout = [(0, masks), (0, across), (1, masks), (1, across)]
        pieces = [cells, swap(cells, 1), other, swap(other, 1)]
    merged, attended, factors = merge(frozen, down, inner, near, layout, pieces)
    attended = far_rows(lo, hi, q, k, v, direct, distant, factors, attended)
    return (attended, merged)


def solution(mesh):
    rows = P(("group", "seq"), None)
    flat = P(("group", "seq"))
    return jax.shard_map(
        body,
        mesh=mesh,
        in_specs=(rows, rows, rows, flat, flat, P("seq", None), P(None, "seq"), P("seq", None)),
        out_specs=(rows, rows),
        check_vma=False,
    )
```

```python
import functools

import jax
import jax.numpy as jnp
from jax import lax
from jax.experimental import pallas as pl
from jax.experimental.pallas import tpu as pltpu
from jax.sharding import PartitionSpec as P

MODEL_WIDTH = 5120
HEADS = 40
HD = 128
FRAME = 64
NEAR = 2 * FRAME
CHUNK = 512
WIDE = 2 * CHUNK
SCORE_SCALE = HD ** (-0.5) * 1.4426950408889634
ADAPTER_SCALE = MODEL_WIDTH ** (-0.5)
FAR = -1e30
NT = (((1,), (1,)), ((), ()))
NN = (((1,), (0,)), ((), ()))
BF16 = jnp.bfloat16
F32 = jnp.float32
ANY = pl.BlockSpec(memory_space=pl.ANY)
SMEM = pl.BlockSpec(memory_space=pltpu.SMEM)
VMEM = pl.BlockSpec(memory_space=pltpu.VMEM)


def dot(a, b, dims):
    return lax.dot_general(a, b, dims, preferred_element_type=F32)


def clip_bias(lo, hi):
    position = lax.broadcasted_iota(jnp.int32, (NEAR, NEAR), 1)
    return jnp.where(position < hi - lo, 0.0, FAR).astype(F32)


def diagonal(top, bottom):
    zeros = jnp.zeros((FRAME, NEAR), BF16)
    return jnp.concatenate(
        [jnp.concatenate([top, zeros], axis=1), jnp.concatenate([zeros, bottom], axis=1)]
    )


def attend(loads):
    ones = jnp.ones((NEAR, HD), BF16)
    scores = []
    for load_q, load_k, _, bias in loads:
        q = load_q()
        scores.append(dot(diagonal(q[:, :HD], q[:, HD:]), load_k(), NT) * SCORE_SCALE + bias)
    weights = [jnp.exp2(s - jnp.max(s, axis=-1, keepdims=True)).astype(BF16) for s in scores]
    results = []
    for w, (_, _, load_v, _) in zip(weights, loads):
        v = load_v()
        values = jnp.concatenate(
            [jnp.concatenate([v[:, at : at + HD], ones], axis=1) for at in (0, HD)]
        )
        mixed = dot(diagonal(w[:FRAME], w[FRAME:]), values, NN)
        mixed = (mixed[:, :HD] * (1.0 / mixed[:, HD:])).astype(BF16)
        results.append(jnp.concatenate([mixed[:FRAME], mixed[FRAME:]], axis=1))
    return results


def inner_kernel(lo_ref, hi_ref, q_ref, k_ref, v_ref, o_ref):
    rows = q_ref.shape[0]
    base = lax.axis_index("seq") * rows
    loads, targets = [], []
    for row in (FRAME, NEAR):
        lo, hi = lo_ref[row], hi_ref[row]
        keys = pl.ds(pl.multiple_of(lo - base, FRAME), NEAR)
        bias = clip_bias(lo, hi)
        for col in range(0, WIDE, 2 * HD):
            part = slice(col, col + 2 * HD)
            targets.append((slice(row - FRAME, row), part))
            loads.append(
                (
                    lambda row=row, part=part: q_ref[row : row + FRAME, part],
                    lambda keys=keys, part=part: k_ref[keys, part],
                    lambda keys=keys, part=part: v_ref[keys, part],
                    bias,
                )
            )
    for target, result in zip(targets, attend(loads)):
        o_ref[target] = result


def inner_attention(lo, hi, q, k, v):
    rows, width = q.shape
    block = pl.BlockSpec((rows, WIDE), lambda i: (0, i))
    return pl.pallas_call(
        inner_kernel,
        grid=(width // WIDE,),
        out_shape=jax.ShapeDtypeStruct((NEAR, width), BF16),
        in_specs=[SMEM, SMEM, block, block, block],
        out_specs=pl.BlockSpec((NEAR, WIDE), lambda i: (0, i)),
        compiler_params=pltpu.CompilerParams(vmem_limit_bytes=16 << 20),
        cost_estimate=pl.CostEstimate(
            flops=16 * NEAR * NEAR * width,
            bytes_accessed=7 * rows * width,
            transcendentals=NEAR * NEAR * HEADS,
        ),
        name="inner_attention",
    )(lo, hi, q, k, v)


def edge_side(is_near, rows):
    right = lax.rem(lax.axis_index("seq"), 2) == (0 if is_near else 1)
    return right, pl.multiple_of(jnp.where(right, rows - FRAME, 0), FRAME)


def attend_edge(is_near, lo_ref, hi_ref, q, k, v, halos, out):
    rows, width = q.shape
    pairs = width // (2 * HD)
    unroll = next(n for n in (10, 8, 6, 5, 4, 2, 1) if pairs % n == 0)
    me = lax.axis_index("seq")
    base = me * rows
    right, row = edge_side(is_near, rows)
    first = pl.multiple_of(jnp.where(right, rows - NEAR, 0), NEAR)
    second = pl.multiple_of(first + FRAME, FRAME)
    lo, hi = lo_ref[row], hi_ref[row]
    before = lo < base
    after = jnp.logical_and(right, lo == base + rows - FRAME)
    direct = lax.rem(lax.div(me + 1, 2), 2) == 1

    def window(ref, kind, part):
        halo = halos[kind][:, part]
        if len(halos) == 4:
            halo = jnp.where(direct, halo, halos[2 + kind][:, part])
        one, two = ref[pl.ds(first, FRAME), part], ref[pl.ds(second, FRAME), part]
        return jnp.concatenate(
            [
                jnp.where(before, halo, jnp.where(after, two, one)),
                jnp.where(before, one, jnp.where(after, halo, two)),
            ]
        )

    bias = clip_bias(lo, hi)

    def step(i, _):
        loads, parts = [], []
        for pair in range(unroll):
            part = pl.ds(pl.multiple_of((i * unroll + pair) * 2 * HD, 2 * HD), 2 * HD)
            parts.append(part)
            loads.append(
                (
                    lambda part=part: q[pl.ds(row, FRAME), part],
                    lambda part=part: window(k, 0, part),
                    lambda part=part: window(v, 1, part),
                    bias,
                )
            )
        for part, result in zip(parts, attend(loads)):
            out[:, part] = result
        return 0

    lax.fori_loop(0, pairs // unroll, step, 0)


def near_kernel(lo_ref, hi_ref, q, k, v, halo, out):
    attend_edge(True, lo_ref, hi_ref, q, k, v, (halo.at[0], halo.at[1]), out)


def edge_cost(rows, width):
    return pl.CostEstimate(
        flops=8 * NEAR * NEAR * width,
        bytes_accessed=7 * rows * width,
        transcendentals=FRAME * NEAR * HEADS,
    )


def near_attention(lo, hi, q, k, v, halo):
    rows, width = q.shape
    return pl.pallas_call(
        near_kernel,
        out_shape=jax.ShapeDtypeStruct((FRAME, width), BF16),
        in_specs=[SMEM, SMEM] + [VMEM] * 4,
        out_specs=VMEM,
        compiler_params=pltpu.CompilerParams(vmem_limit_bytes=20 << 20),
        cost_estimate=edge_cost(rows, width),
        name="near_edge_attention",
    )(lo, hi, q, k, v, halo)


def adapt(value, narrow, factor):
    return (value.astype(F32) + ADAPTER_SCALE * dot(narrow, factor, NT)).astype(BF16)


def merge_kernel(layout, frozen, own_down, inner, near, *rest):
    refs, rest = rest[:-6], rest[-6:]
    merged, attended, factors, w, result, sems = rest
    shard, width = frozen.shape
    rows = result.shape[0]
    me = lax.axis_index("seq")
    kind = lax.axis_index("group")
    for ref, (swapped, masks) in zip(refs, layout):
        target = 1 - kind if swapped else kind
        for i, mask in enumerate(masks):
            at = pl.ds(pl.multiple_of((me ^ mask) * shard, shard), shard)
            factors[target, at, :] = ref[i]
    if not layout:
        factors[...] = refs[0][...]
    down, up = factors.at[0], factors.at[1]
    _, near_row = edge_side(True, rows)
    parts = ((inner, FRAME), (near, near_row))
    reduced = [dot(att[...], down[...], NN).astype(BF16) for att, _ in parts]
    stores = []

    def store(source, target):
        stores.append(pltpu.make_async_copy(source, target, sems.at[len(stores)]))
        stores[-1].start()

    for first in range(0, width, CHUNK):
        part = pl.ds(first, CHUNK)
        factor = up[part, :]
        w[:, part] = adapt(frozen[:, part], own_down[...], factor)
        store(w.at[:, part], merged.at[:, part])
        for narrow, (att, row) in zip(reduced, parts):
            result[pl.ds(row, att.shape[0]), part] = adapt(att[:, part], narrow, factor)
            at = (pl.ds(row, att.shape[0]), part)
            store(result.at[at], attended.at[at])
    for copy in stores:
        copy.wait()


def merge(frozen, own_down, inner, near, layout, pieces):
    shard, width = frozen.shape
    rank = own_down.shape[1]
    rows = 2 * NEAR
    return pl.pallas_call(
        functools.partial(merge_kernel, layout),
        out_shape=(
            jax.ShapeDtypeStruct((shard, width), BF16),
            jax.ShapeDtypeStruct((rows, width), BF16),
            jax.ShapeDtypeStruct((2, width, rank), BF16),
        ),
        in_specs=[VMEM] * (4 + len(pieces)),
        out_specs=(ANY, ANY, VMEM),
        scratch_shapes=[
            pltpu.VMEM((shard, width), BF16),
            pltpu.VMEM((rows, width), BF16),
            pltpu.SemaphoreType.DMA((3 * (width // CHUNK),)),
        ],
        compiler_params=pltpu.CompilerParams(vmem_limit_bytes=24 << 20),
        cost_estimate=pl.CostEstimate(
            flops=2 * (shard + 2 * rows) * width * rank,
            bytes_accessed=4 * (shard + rows) * width + 4 * width * rank,
            transcendentals=0,
        ),
        name="merge_and_adapter",
    )(frozen, own_down, inner, near, *pieces)


def far_kernel(lo_ref, hi_ref, q, k, v, *rest):
    halos, (factors, _, out, mixed, result, sems) = rest[:3], rest[3:]
    rows, width = q.shape
    halos = (*halos[:2], halos[2].at[0], halos[2].at[1])
    attend_edge(False, lo_ref, hi_ref, q, k, v, halos, mixed)
    narrow = dot(mixed[...], factors[0], NN).astype(BF16)
    _, row = edge_side(False, rows)
    stores = []
    for first in range(0, width, WIDE):
        part = pl.ds(first, WIDE)
        result[:, part] = adapt(mixed[:, part], narrow, factors[1, part, :])
        stores.append(
            pltpu.make_async_copy(
                result.at[:, part], out.at[pl.ds(row, FRAME), part], sems.at[len(stores)]
            )
        )
        stores[-1].start()
    for copy in stores:
        copy.wait()


def far_rows(lo, hi, q, k, v, direct, distant, factors, attended):
    rows, width = q.shape
    return pl.pallas_call(
        far_kernel,
        out_shape=jax.ShapeDtypeStruct((rows, width), BF16),
        in_specs=[SMEM, SMEM] + [VMEM] * 7 + [ANY],
        out_specs=ANY,
        input_output_aliases={9: 0},
        scratch_shapes=[
            pltpu.VMEM((FRAME, width), BF16),
            pltpu.VMEM((FRAME, width), BF16),
            pltpu.SemaphoreType.DMA((width // WIDE,)),
        ],
        compiler_params=pltpu.CompilerParams(vmem_limit_bytes=24 << 20),
        cost_estimate=edge_cost(rows, width),
        name="far_edge_rows",
    )(lo, hi, q, k, v, *direct, distant, factors, attended)


def body(q, k, v, lo, hi, down, up, frozen):
    count = lax.axis_size("seq")
    rows = k.shape[0]
    odd = lax.rem(lax.axis_index("seq"), 2)

    def rim(start):
        return [lax.dynamic_slice_in_dim(x, start, FRAME, 0) for x in (k, v)]

    def send(cells, pairs):
        return [lax.ppermute(x, "seq", pairs) for x in cells]

    def swap(cells, mask):
        return lax.ppermute(cells, "seq", [(i, i ^ mask) for i in range(count)])

    def cross(cells):
        return lax.ppermute(cells, "group", [(0, 1), (1, 0)])

    direct_pairs, distant_pairs = (
        [(i + a, i + 1 - a) for i in range(first, count - 1, 4) for a in (0, 1)]
        for first in (1, 3)
    )
    far_rim = rim(odd * (rows - FRAME))
    near_rim = jnp.stack(rim((1 - odd) * (rows - FRAME)))
    up = up.T
    steps = [1 << bit for bit in range(1, count.bit_length() - 1)]
    if lax.axis_size("group") != 2 or len(steps) != 3 or down.shape[0] % 32:
        both = lax.all_gather(jnp.stack([down, up]), "seq", axis=1, tiled=True)
        layout, pieces = [], [both]
        direct = send(far_rim, direct_pairs)
        distant = lax.ppermute(jnp.stack(far_rim), "seq", distant_pairs)
        inner = inner_attention(lo, hi, q, k, v)
        near = near_attention(lo, hi, q, k, v, swap(near_rim, 1))
    else:
        barrier = lax.optimization_barrier
        join = jnp.concatenate
        side, short, long = steps
        own = jnp.where(lax.axis_index("group") == 0, down, up)[None]
        plane = join([own, swap(own, side)])
        direct = send(far_rim, direct_pairs)
        plane, near_rim = barrier((plane, near_rim))
        halo = swap(near_rim, 1)
        beyond = swap(plane, long)
        beside = swap(plane, short)
        crossed = [cross(plane)]
        beyond, beside, crossed = barrier((beyond, beside, crossed))
        far_rim, direct, lo_later = barrier((far_rim, direct, lo))
        last = swap(beyond, short)
        distant = lax.ppermute(jnp.stack(far_rim), "seq", distant_pairs)
        crossed.append(cross(join([beside, beyond])))
        inner = inner_attention(lo_later, hi, q, k, v)
        near = near_attention(lo_later, hi, q, k, v, halo)
        last, inner, near = barrier((last, inner, near))
        crossed.append(cross(last))
        cells, other = join([plane, beside, beyond, last]), join(crossed)
        masks = [a ^ b for a in (0, short, long, short ^ long) for b in (0, side)]
        across = [mask ^ 1 for mask in masks]
        layout = [(0, masks), (0, across), (1, masks), (1, across)]
        pieces = [cells, swap(cells, 1), other, swap(other, 1)]
    merged, attended, factors = merge(frozen, down, inner, near, layout, pieces)
    attended = far_rows(lo, hi, q, k, v, direct, distant, factors, attended)
    return (attended, merged)


def solution(mesh):
    rows = P(("group", "seq"), None)
    flat = P(("group", "seq"))
    return jax.shard_map(
        body,
        mesh=mesh,
        in_specs=(rows, rows, rows, flat, flat, P("seq", None), P(None, "seq"), P("seq", None)),
        out_specs=(rows, rows),
        check_vma=False,
    )
```

```python
import functools

import jax
import jax.numpy as jnp
from jax import lax
from jax.experimental import pallas as pl
from jax.experimental.pallas import tpu as pltpu
from jax.sharding import PartitionSpec as P

MODEL_WIDTH = 5120
HEADS = 40
HD = 128
FRAME = 64
NEAR = 2 * FRAME
CHUNK = 512
WIDE = 2 * CHUNK
SCORE_SCALE = HD ** (-0.5) * 1.4426950408889634
ADAPTER_SCALE = MODEL_WIDTH ** (-0.5)
FAR = -1e30
NT = (((1,), (1,)), ((), ()))
NN = (((1,), (0,)), ((), ()))
BF16 = jnp.bfloat16
F32 = jnp.float32
ANY = pl.BlockSpec(memory_space=pl.ANY)
SMEM = pl.BlockSpec(memory_space=pltpu.SMEM)
VMEM = pl.BlockSpec(memory_space=pltpu.VMEM)


def dot(a, b, dims):
    return lax.dot_general(a, b, dims, preferred_element_type=F32)


def clip_bias(lo, hi):
    position = lax.broadcasted_iota(jnp.int32, (NEAR, NEAR), 1)
    return jnp.where(position < hi - lo, 0.0, FAR).astype(F32)


def diagonal(top, bottom):
    zeros = jnp.zeros((FRAME, NEAR), BF16)
    return jnp.concatenate(
        [jnp.concatenate([top, zeros], axis=1), jnp.concatenate([zeros, bottom], axis=1)]
    )


def attend(loads):
    ones = jnp.ones((NEAR, HD), BF16)
    scores = []
    for load_q, load_k, _, bias in loads:
        q = load_q()
        scores.append(dot(diagonal(q[:, :HD], q[:, HD:]), load_k(), NT) * SCORE_SCALE + bias)
    weights = [jnp.exp2(s - jnp.max(s, axis=-1, keepdims=True)).astype(BF16) for s in scores]
    results = []
    for w, (_, _, load_v, _) in zip(weights, loads):
        v = load_v()
        values = jnp.concatenate(
            [jnp.concatenate([v[:, at : at + HD], ones], axis=1) for at in (0, HD)]
        )
        mixed = dot(diagonal(w[:FRAME], w[FRAME:]), values, NN)
        mixed = (mixed[:, :HD] * (1.0 / mixed[:, HD:])).astype(BF16)
        results.append(jnp.concatenate([mixed[:FRAME], mixed[FRAME:]], axis=1))
    return results


def inner_kernel(lo_ref, hi_ref, q_ref, k_ref, v_ref, o_ref):
    rows = q_ref.shape[0]
    base = lax.axis_index("seq") * rows
    loads, targets = [], []
    for row in (FRAME, NEAR):
        lo, hi = lo_ref[row], hi_ref[row]
        keys = pl.ds(pl.multiple_of(lo - base, FRAME), NEAR)
        bias = clip_bias(lo, hi)
        for col in range(0, WIDE, 2 * HD):
            part = slice(col, col + 2 * HD)
            targets.append((slice(row - FRAME, row), part))
            loads.append(
                (
                    lambda row=row, part=part: q_ref[row : row + FRAME, part],
                    lambda keys=keys, part=part: k_ref[keys, part],
                    lambda keys=keys, part=part: v_ref[keys, part],
                    bias,
                )
            )
    for target, result in zip(targets, attend(loads)):
        o_ref[target] = result


def inner_attention(lo, hi, q, k, v):
    rows, width = q.shape
    block = pl.BlockSpec((rows, WIDE), lambda i: (0, i))
    return pl.pallas_call(
        inner_kernel,
        grid=(width // WIDE,),
        out_shape=jax.ShapeDtypeStruct((NEAR, width), BF16),
        in_specs=[SMEM, SMEM, block, block, block],
        out_specs=pl.BlockSpec((NEAR, WIDE), lambda i: (0, i)),
        compiler_params=pltpu.CompilerParams(vmem_limit_bytes=16 << 20),
        cost_estimate=pl.CostEstimate(
            flops=16 * NEAR * NEAR * width,
            bytes_accessed=7 * rows * width,
            transcendentals=NEAR * NEAR * HEADS,
        ),
        name="inner_attention",
    )(lo, hi, q, k, v)


def edge_side(is_near, rows):
    right = lax.rem(lax.axis_index("seq"), 2) == (0 if is_near else 1)
    return right, pl.multiple_of(jnp.where(right, rows - FRAME, 0), FRAME)


def attend_edge(is_near, lo_ref, hi_ref, q, k, v, halos, out):
    rows, width = q.shape
    pairs = width // (2 * HD)
    unroll = next(n for n in (10, 8, 6, 5, 4, 2, 1) if pairs % n == 0)
    me = lax.axis_index("seq")
    base = me * rows
    right, row = edge_side(is_near, rows)
    first = pl.multiple_of(jnp.where(right, rows - NEAR, 0), NEAR)
    second = pl.multiple_of(first + FRAME, FRAME)
    lo, hi = lo_ref[row], hi_ref[row]
    before = lo < base
    after = jnp.logical_and(right, lo == base + rows - FRAME)
    direct = lax.rem(lax.div(me + 1, 2), 2) == 1

    def window(ref, kind, part):
        halo = halos[kind][:, part]
        if len(halos) == 4:
            halo = jnp.where(direct, halo, halos[2 + kind][:, part])
        one, two = ref[pl.ds(first, FRAME), part], ref[pl.ds(second, FRAME), part]
        return jnp.concatenate(
            [
                jnp.where(before, halo, jnp.where(after, two, one)),
                jnp.where(before, one, jnp.where(after, halo, two)),
            ]
        )

    bias = clip_bias(lo, hi)

    def step(i, _):
        loads, parts = [], []
        for pair in range(unroll):
            part = pl.ds(pl.multiple_of((i * unroll + pair) * 2 * HD, 2 * HD), 2 * HD)
            parts.append(part)
            loads.append(
                (
                    lambda part=part: q[pl.ds(row, FRAME), part],
                    lambda part=part: window(k, 0, part),
                    lambda part=part: window(v, 1, part),
                    bias,
                )
            )
        for part, result in zip(parts, attend(loads)):
            out[:, part] = result
        return 0

    lax.fori_loop(0, pairs // unroll, step, 0)


def near_kernel(lo_ref, hi_ref, q, k, v, halo, out):
    attend_edge(True, lo_ref, hi_ref, q, k, v, (halo.at[0], halo.at[1]), out)


def edge_cost(rows, width):
    return pl.CostEstimate(
        flops=8 * NEAR * NEAR * width,
        bytes_accessed=7 * rows * width,
        transcendentals=FRAME * NEAR * HEADS,
    )


def near_attention(lo, hi, q, k, v, halo):
    rows, width = q.shape
    return pl.pallas_call(
        near_kernel,
        out_shape=jax.ShapeDtypeStruct((FRAME, width), BF16),
        in_specs=[SMEM, SMEM] + [VMEM] * 4,
        out_specs=VMEM,
        compiler_params=pltpu.CompilerParams(vmem_limit_bytes=20 << 20),
        cost_estimate=edge_cost(rows, width),
        name="near_edge_attention",
    )(lo, hi, q, k, v, halo)


def adapt(value, narrow, factor):
    return (value.astype(F32) + ADAPTER_SCALE * dot(narrow, factor, NT)).astype(BF16)


def merge_kernel(layout, frozen, own_down, inner, near, *rest):
    refs, rest = rest[:-6], rest[-6:]
    merged, attended, factors, w, result, sems = rest
    shard, width = frozen.shape
    rows = result.shape[0]
    me = lax.axis_index("seq")
    kind = lax.axis_index("group")
    for ref, cells in zip(refs, layout):
        for i, (swapped, mask) in enumerate(cells):
            at = pl.ds(pl.multiple_of((me ^ mask) * shard, shard), shard)
            factors[1 - kind if swapped else kind, at, :] = ref[i]
    if not layout:
        factors[...] = refs[0][...]
    down, up = factors.at[0], factors.at[1]
    _, near_row = edge_side(True, rows)
    parts = ((inner, FRAME), (near, near_row))
    reduced = [dot(att[...], down[...], NN).astype(BF16) for att, _ in parts]
    stores = []

    def store(source, target):
        stores.append(pltpu.make_async_copy(source, target, sems.at[len(stores)]))
        stores[-1].start()

    for first in range(0, width, CHUNK):
        part = pl.ds(first, CHUNK)
        factor = up[part, :]
        w[:, part] = adapt(frozen[:, part], own_down[...], factor)
        store(w.at[:, part], merged.at[:, part])
        for narrow, (att, row) in zip(reduced, parts):
            result[pl.ds(row, att.shape[0]), part] = adapt(att[:, part], narrow, factor)
            at = (pl.ds(row, att.shape[0]), part)
            store(result.at[at], attended.at[at])
    for copy in stores:
        copy.wait()


def merge(frozen, own_down, inner, near, layout, pieces):
    shard, width = frozen.shape
    rank = own_down.shape[1]
    rows = 2 * NEAR
    return pl.pallas_call(
        functools.partial(merge_kernel, layout),
        out_shape=(
            jax.ShapeDtypeStruct((shard, width), BF16),
            jax.ShapeDtypeStruct((rows, width), BF16),
            jax.ShapeDtypeStruct((2, width, rank), BF16),
        ),
        in_specs=[VMEM] * (4 + len(pieces)),
        out_specs=(ANY, ANY, VMEM),
        scratch_shapes=[
            pltpu.VMEM((shard, width), BF16),
            pltpu.VMEM((rows, width), BF16),
            pltpu.SemaphoreType.DMA((3 * (width // CHUNK),)),
        ],
        compiler_params=pltpu.CompilerParams(vmem_limit_bytes=24 << 20),
        cost_estimate=pl.CostEstimate(
            flops=2 * (shard + 2 * rows) * width * rank,
            bytes_accessed=4 * (shard + rows) * width + 4 * width * rank,
            transcendentals=0,
        ),
        name="merge_and_adapter",
    )(frozen, own_down, inner, near, *pieces)


def far_kernel(lo_ref, hi_ref, q, k, v, *rest):
    halos, (factors, _, out, mixed, result, sems) = rest[:3], rest[3:]
    rows, width = q.shape
    halos = (*halos[:2], halos[2].at[0], halos[2].at[1])
    attend_edge(False, lo_ref, hi_ref, q, k, v, halos, mixed)
    narrow = dot(mixed[...], factors[0], NN).astype(BF16)
    _, row = edge_side(False, rows)
    stores = []
    for first in range(0, width, WIDE):
        part = pl.ds(first, WIDE)
        result[:, part] = adapt(mixed[:, part], narrow, factors[1, part, :])
        stores.append(
            pltpu.make_async_copy(
                result.at[:, part], out.at[pl.ds(row, FRAME), part], sems.at[len(stores)]
            )
        )
        stores[-1].start()
    for copy in stores:
        copy.wait()


def far_rows(lo, hi, q, k, v, direct, distant, factors, attended):
    rows, width = q.shape
    return pl.pallas_call(
        far_kernel,
        out_shape=jax.ShapeDtypeStruct((rows, width), BF16),
        in_specs=[SMEM, SMEM] + [VMEM] * 7 + [ANY],
        out_specs=ANY,
        input_output_aliases={9: 0},
        scratch_shapes=[
            pltpu.VMEM((FRAME, width), BF16),
            pltpu.VMEM((FRAME, width), BF16),
            pltpu.SemaphoreType.DMA((width // WIDE,)),
        ],
        compiler_params=pltpu.CompilerParams(vmem_limit_bytes=24 << 20),
        cost_estimate=edge_cost(rows, width),
        name="far_edge_rows",
    )(lo, hi, q, k, v, *direct, distant, factors, attended)


def body(q, k, v, lo, hi, down, up, frozen):
    count = lax.axis_size("seq")
    rows = k.shape[0]
    odd = lax.rem(lax.axis_index("seq"), 2)

    def rim(start):
        return [lax.dynamic_slice_in_dim(x, start, FRAME, 0) for x in (k, v)]

    def send(cells, pairs):
        return [lax.ppermute(x, "seq", pairs) for x in cells]

    def swap(cells, mask):
        return lax.ppermute(cells, "seq", [(i, i ^ mask) for i in range(count)])

    def cross(cells):
        return lax.ppermute(cells, "group", [(0, 1), (1, 0)])

    direct_pairs, distant_pairs = (
        [(i + a, i + 1 - a) for i in range(first, count - 1, 4) for a in (0, 1)]
        for first in (1, 3)
    )
    far_rim = rim(odd * (rows - FRAME))
    near_rim = jnp.stack(rim((1 - odd) * (rows - FRAME)))
    up = up.T
    steps = [1 << bit for bit in range(1, count.bit_length() - 1)]
    if lax.axis_size("group") != 2 or len(steps) != 3 or down.shape[0] % 32:
        both = lax.all_gather(jnp.stack([down, up]), "seq", axis=1, tiled=True)
        layout, pieces = [], [both]
        direct = send(far_rim, direct_pairs)
        distant = lax.ppermute(jnp.stack(far_rim), "seq", distant_pairs)
        inner = inner_attention(lo, hi, q, k, v)
        near = near_attention(lo, hi, q, k, v, swap(near_rim, 1))
    else:
        barrier = lax.optimization_barrier
        join = jnp.concatenate
        side, short, long = steps
        own = join([down, up])[None]
        first = lax.axis_index("group") == 0
        shard = down.shape[0]
        direct = send(far_rim, direct_pairs)
        plane = join([own, swap(own, side)])
        plane, near_rim = barrier((plane, near_rim))
        halo = swap(near_rim, 1)
        halves = plane[:, :shard], plane[:, shard:]
        plane = jnp.where(first, *halves)
        crossed = [jnp.where(first, *halves[::-1])]
        beyond = swap(plane, long)
        beside = swap(plane, short)
        inner = inner_attention(lo, hi, q, k, v)
        beyond, beside, inner = barrier((beyond, beside, inner))
        far_rim, direct, lo_near = barrier((far_rim, direct, lo))
        last = swap(beyond, short)
        distant = lax.ppermute(jnp.stack(far_rim), "seq", distant_pairs)
        crossed.append(cross(join([beside, beyond])))
        near = near_attention(lo, hi, q, k, v, halo)
        last, crossed[1], near = barrier((last, crossed[1], near))
        crossed.append(cross(last))
        masks = [a ^ b for a in (0, short, long) for b in (0, side)]
        late_masks = [short ^ long ^ b for b in (0, side)]
        early = join([plane, beside, beyond, *crossed[:2]])
        late = join([last, crossed[2]])
        pieces = [early, swap(early, 1), late, swap(late, 1)]
        layout = [
            [(kind, mask ^ core) for kind in (0, 1) for mask in group]
            for group in (masks, late_masks)
            for core in (0, 1)
        ]
    merged, attended, factors = merge(frozen, down, inner, near, layout, pieces)
    attended = far_rows(lo, hi, q, k, v, direct, distant, factors, attended)
    return (attended, merged)


def solution(mesh):
    rows = P(("group", "seq"), None)
    flat = P(("group", "seq"))
    return jax.shard_map(
        body,
        mesh=mesh,
        in_specs=(rows, rows, rows, flat, flat, P("seq", None), P(None, "seq"), P("seq", None)),
        out_specs=(rows, rows),
        check_vma=False,
    )
```

```python
import functools

import jax
import jax.numpy as jnp
from jax import lax
from jax.experimental import pallas as pl
from jax.experimental.pallas import tpu as pltpu
from jax.sharding import PartitionSpec as P

MODEL_WIDTH = 5120
HEADS = 40
HD = 128
FRAME = 64
NEAR = 2 * FRAME
CHUNK = 512
WIDE = 2 * CHUNK
SCORE_SCALE = HD ** (-0.5) * 1.4426950408889634
ADAPTER_SCALE = MODEL_WIDTH ** (-0.5)
FAR = -1e30
NT = (((1,), (1,)), ((), ()))
NN = (((1,), (0,)), ((), ()))
BF16 = jnp.bfloat16
F32 = jnp.float32
ANY = pl.BlockSpec(memory_space=pl.ANY)
SMEM = pl.BlockSpec(memory_space=pltpu.SMEM)
VMEM = pl.BlockSpec(memory_space=pltpu.VMEM)


def dot(a, b, dims):
    return lax.dot_general(a, b, dims, preferred_element_type=F32)


def clip_bias(lo, hi):
    position = lax.broadcasted_iota(jnp.int32, (NEAR, NEAR), 1)
    return jnp.where(position < hi - lo, 0.0, FAR).astype(F32)


def diagonal(top, bottom):
    zeros = jnp.zeros((FRAME, NEAR), BF16)
    return jnp.concatenate(
        [jnp.concatenate([top, zeros], axis=1), jnp.concatenate([zeros, bottom], axis=1)]
    )


def attend(loads):
    ones = jnp.ones((NEAR, HD), BF16)
    scores = []
    for load_q, load_k, _, bias in loads:
        q = load_q()
        scores.append(dot(diagonal(q[:, :HD], q[:, HD:]), load_k(), NT) * SCORE_SCALE + bias)
    weights = [jnp.exp2(s - jnp.max(s, axis=-1, keepdims=True)).astype(BF16) for s in scores]
    results = []
    for w, (_, _, load_v, _) in zip(weights, loads):
        v = load_v()
        values = jnp.concatenate(
            [jnp.concatenate([v[:, at : at + HD], ones], axis=1) for at in (0, HD)]
        )
        mixed = dot(diagonal(w[:FRAME], w[FRAME:]), values, NN)
        mixed = (mixed[:, :HD] * (1.0 / mixed[:, HD:])).astype(BF16)
        results.append(jnp.concatenate([mixed[:FRAME], mixed[FRAME:]], axis=1))
    return results


def inner_kernel(lo_ref, hi_ref, q_ref, k_ref, v_ref, o_ref):
    rows = q_ref.shape[0]
    base = lax.axis_index("seq") * rows
    loads, targets = [], []
    for row in (FRAME, NEAR):
        lo, hi = lo_ref[row], hi_ref[row]
        keys = pl.ds(pl.multiple_of(lo - base, FRAME), NEAR)
        bias = clip_bias(lo, hi)
        for col in range(0, WIDE, 2 * HD):
            part = slice(col, col + 2 * HD)
            targets.append((slice(row - FRAME, row), part))
            loads.append(
                (
                    lambda row=row, part=part: q_ref[row : row + FRAME, part],
                    lambda keys=keys, part=part: k_ref[keys, part],
                    lambda keys=keys, part=part: v_ref[keys, part],
                    bias,
                )
            )
    for target, result in zip(targets, attend(loads)):
        o_ref[target] = result


def inner_attention(lo, hi, q, k, v):
    rows, width = q.shape
    block = pl.BlockSpec((rows, WIDE), lambda i: (0, i))
    return pl.pallas_call(
        inner_kernel,
        grid=(width // WIDE,),
        out_shape=jax.ShapeDtypeStruct((NEAR, width), BF16),
        in_specs=[SMEM, SMEM, block, block, block],
        out_specs=pl.BlockSpec((NEAR, WIDE), lambda i: (0, i)),
        compiler_params=pltpu.CompilerParams(vmem_limit_bytes=6 << 20),
        cost_estimate=pl.CostEstimate(
            flops=16 * NEAR * NEAR * width,
            bytes_accessed=7 * rows * width,
            transcendentals=NEAR * NEAR * HEADS,
        ),
        name="inner_attention",
    )(lo, hi, q, k, v)


def edge_side(is_near, rows):
    right = lax.rem(lax.axis_index("seq"), 2) == (0 if is_near else 1)
    return right, pl.multiple_of(jnp.where(right, rows - FRAME, 0), FRAME)


def attend_edge(is_near, lo_ref, hi_ref, q, k, v, halos, out):
    rows, width = q.shape
    pairs = width // (2 * HD)
    unroll = next(n for n in (10, 8, 6, 5, 4, 2, 1) if pairs % n == 0)
    me = lax.axis_index("seq")
    base = me * rows
    right, row = edge_side(is_near, rows)
    first = pl.multiple_of(jnp.where(right, rows - NEAR, 0), NEAR)
    second = pl.multiple_of(first + FRAME, FRAME)
    lo, hi = lo_ref[row], hi_ref[row]
    before = lo < base
    after = jnp.logical_and(right, lo == base + rows - FRAME)
    direct = lax.rem(lax.div(me + 1, 2), 2) == 1

    def window(ref, kind, part):
        halo = halos[kind][:, part]
        if len(halos) == 4:
            halo = jnp.where(direct, halo, halos[2 + kind][:, part])
        one, two = ref[pl.ds(first, FRAME), part], ref[pl.ds(second, FRAME), part]
        return jnp.concatenate(
            [
                jnp.where(before, halo, jnp.where(after, two, one)),
                jnp.where(before, one, jnp.where(after, halo, two)),
            ]
        )

    bias = clip_bias(lo, hi)

    def step(i, _):
        loads, parts = [], []
        for pair in range(unroll):
            part = pl.ds(pl.multiple_of((i * unroll + pair) * 2 * HD, 2 * HD), 2 * HD)
            parts.append(part)
            loads.append(
                (
                    lambda part=part: q[pl.ds(row, FRAME), part],
                    lambda part=part: window(k, 0, part),
                    lambda part=part: window(v, 1, part),
                    bias,
                )
            )
        for part, result in zip(parts, attend(loads)):
            out[:, part] = result
        return 0

    lax.fori_loop(0, pairs // unroll, step, 0)


def near_kernel(lo_ref, hi_ref, q, k, v, halo, out):
    attend_edge(True, lo_ref, hi_ref, q, k, v, (halo.at[0], halo.at[1]), out)


def edge_cost(rows, width):
    return pl.CostEstimate(
        flops=8 * NEAR * NEAR * width,
        bytes_accessed=7 * rows * width,
        transcendentals=FRAME * NEAR * HEADS,
    )


def near_attention(lo, hi, q, k, v, halo):
    rows, width = q.shape
    return pl.pallas_call(
        near_kernel,
        out_shape=jax.ShapeDtypeStruct((FRAME, width), BF16),
        in_specs=[SMEM, SMEM] + [VMEM] * 4,
        out_specs=VMEM,
        compiler_params=pltpu.CompilerParams(vmem_limit_bytes=13 << 20),
        cost_estimate=edge_cost(rows, width),
        name="near_edge_attention",
    )(lo, hi, q, k, v, halo)


def adapt(value, narrow, factor):
    return (value.astype(F32) + ADAPTER_SCALE * dot(narrow, factor, NT)).astype(BF16)


def merge_kernel(layout, frozen, own_down, inner, near, *rest):
    refs, rest = rest[:-6], rest[-6:]
    merged, attended, factors, w, result, sems = rest
    shard, width = frozen.shape
    rows = result.shape[0]
    me = lax.axis_index("seq")
    kind = lax.axis_index("group")
    for ref, cells in zip(refs, layout):
        for i, (swapped, mask) in enumerate(cells):
            at = pl.ds(pl.multiple_of((me ^ mask) * shard, shard), shard)
            factors[1 - kind if swapped else kind, at, :] = ref[i]
    if not layout:
        factors[...] = refs[0][...]
    down, up = factors.at[0], factors.at[1]
    _, near_row = edge_side(True, rows)
    parts = ((inner, FRAME), (near, near_row))
    reduced = [dot(att[...], down[...], NN).astype(BF16) for att, _ in parts]
    stores = []

    def store(source, target):
        stores.append(pltpu.make_async_copy(source, target, sems.at[len(stores)]))
        stores[-1].start()

    for first in range(0, width, CHUNK):
        part = pl.ds(first, CHUNK)
        factor = up[part, :]
        w[:, part] = adapt(frozen[:, part], own_down[...], factor)
        store(w.at[:, part], merged.at[:, part])
        for narrow, (att, row) in zip(reduced, parts):
            result[pl.ds(row, att.shape[0]), part] = adapt(att[:, part], narrow, factor)
            at = (pl.ds(row, att.shape[0]), part)
            store(result.at[at], attended.at[at])
    for copy in stores:
        copy.wait()


def merge(frozen, own_down, inner, near, layout, pieces):
    shard, width = frozen.shape
    rank = own_down.shape[1]
    rows = 2 * NEAR
    return pl.pallas_call(
        functools.partial(merge_kernel, layout),
        out_shape=(
            jax.ShapeDtypeStruct((shard, width), BF16),
            jax.ShapeDtypeStruct((rows, width), BF16),
            jax.ShapeDtypeStruct((2, width, rank), BF16),
        ),
        in_specs=[VMEM] * (4 + len(pieces)),
        out_specs=(ANY, ANY, VMEM),
        scratch_shapes=[
            pltpu.VMEM((shard, width), BF16),
            pltpu.VMEM((rows, width), BF16),
            pltpu.SemaphoreType.DMA((3 * (width // CHUNK),)),
        ],
        compiler_params=pltpu.CompilerParams(vmem_limit_bytes=18 << 20),
        cost_estimate=pl.CostEstimate(
            flops=2 * (shard + 2 * rows) * width * rank,
            bytes_accessed=4 * (shard + rows) * width + 4 * width * rank,
            transcendentals=0,
        ),
        name="merge_and_adapter",
    )(frozen, own_down, inner, near, *pieces)


def far_kernel(lo_ref, hi_ref, q, k, v, *rest):
    halos, (factors, _, out, mixed, result, sems) = rest[:3], rest[3:]
    rows, width = q.shape
    halos = (*halos[:2], halos[2].at[0], halos[2].at[1])
    attend_edge(False, lo_ref, hi_ref, q, k, v, halos, mixed)
    narrow = dot(mixed[...], factors[0], NN).astype(BF16)
    _, row = edge_side(False, rows)
    stores = []
    for first in range(0, width, WIDE):
        part = pl.ds(first, WIDE)
        result[:, part] = adapt(mixed[:, part], narrow, factors[1, part, :])
        stores.append(
            pltpu.make_async_copy(
                result.at[:, part], out.at[pl.ds(row, FRAME), part], sems.at[len(stores)]
            )
        )
        stores[-1].start()
    for copy in stores:
        copy.wait()


def far_rows(lo, hi, q, k, v, direct, distant, factors, attended):
    rows, width = q.shape
    return pl.pallas_call(
        far_kernel,
        out_shape=jax.ShapeDtypeStruct((rows, width), BF16),
        in_specs=[SMEM, SMEM] + [VMEM] * 7 + [ANY],
        out_specs=ANY,
        input_output_aliases={9: 0},
        scratch_shapes=[
            pltpu.VMEM((FRAME, width), BF16),
            pltpu.VMEM((FRAME, width), BF16),
            pltpu.SemaphoreType.DMA((width // WIDE,)),
        ],
        compiler_params=pltpu.CompilerParams(vmem_limit_bytes=18 << 20),
        cost_estimate=edge_cost(rows, width),
        name="far_edge_rows",
    )(lo, hi, q, k, v, *direct, distant, factors, attended)


def body(q, k, v, lo, hi, down, up, frozen):
    count = lax.axis_size("seq")
    rows = k.shape[0]
    odd = lax.rem(lax.axis_index("seq"), 2)

    def rim(start):
        return [lax.dynamic_slice_in_dim(x, start, FRAME, 0) for x in (k, v)]

    def send(cells, pairs):
        return [lax.ppermute(x, "seq", pairs) for x in cells]

    def swap(cells, mask):
        return lax.ppermute(cells, "seq", [(i, i ^ mask) for i in range(count)])

    def cross(cells):
        return lax.ppermute(cells, "group", [(0, 1), (1, 0)])

    direct_pairs, distant_pairs = (
        [(i + a, i + 1 - a) for i in range(first, count - 1, 4) for a in (0, 1)]
        for first in (1, 3)
    )
    far_rim = rim(odd * (rows - FRAME))
    near_rim = jnp.stack(rim((1 - odd) * (rows - FRAME)))
    up = up.T
    steps = [1 << bit for bit in range(1, count.bit_length() - 1)]
    if lax.axis_size("group") != 2 or len(steps) != 3 or down.shape[0] % 32:
        both = lax.all_gather(jnp.stack([down, up]), "seq", axis=1, tiled=True)
        layout, pieces = [], [both]
        direct = send(far_rim, direct_pairs)
        distant = lax.ppermute(jnp.stack(far_rim), "seq", distant_pairs)
        inner = inner_attention(lo, hi, q, k, v)
        near = near_attention(lo, hi, q, k, v, swap(near_rim, 1))
    else:
        barrier = lax.optimization_barrier
        join = jnp.concatenate
        side, short, long = steps
        own = join([down, up])[None]
        first = lax.axis_index("group") == 0
        shard = down.shape[0]
        direct = send(far_rim, direct_pairs)
        plane = join([own, swap(own, side)])
        plane, near_rim = barrier((plane, near_rim))
        halo = swap(near_rim, 1)
        halves = plane[:, :shard], plane[:, shard:]
        plane = jnp.where(first, *halves)
        crossed = [jnp.where(first, *halves[::-1])]
        beyond = swap(plane, long)
        beside = swap(plane, short)
        inner = inner_attention(lo, hi, q, k, v)
        beyond, beside, inner = barrier((beyond, beside, inner))
        far_rim, direct, lo_near = barrier((far_rim, direct, lo))
        last = swap(beyond, short)
        distant = lax.ppermute(jnp.stack(far_rim), "seq", distant_pairs)
        crossed.append(cross(join([beside, beyond])))
        near = near_attention(lo, hi, q, k, v, halo)
        last, crossed[1], near = barrier((last, crossed[1], near))
        crossed.append(cross(last))
        masks = [a ^ b for a in (0, short, long) for b in (0, side)]
        late_masks = [short ^ long ^ b for b in (0, side)]
        early = join([plane, beside, beyond, *crossed[:2]])
        late = join([last, crossed[2]])
        pieces = [early, swap(early, 1), late, swap(late, 1)]
        layout = [
            [(kind, mask ^ core) for kind in (0, 1) for mask in group]
            for group in (masks, late_masks)
            for core in (0, 1)
        ]
    merged, attended, factors = merge(frozen, down, inner, near, layout, pieces)
    attended = far_rows(lo, hi, q, k, v, direct, distant, factors, attended)
    return (attended, merged)


def solution(mesh):
    rows = P(("group", "seq"), None)
    flat = P(("group", "seq"))
    return jax.shard_map(
        body,
        mesh=mesh,
        in_specs=(rows, rows, rows, flat, flat, P("seq", None), P(None, "seq"), P("seq", None)),
        out_specs=(rows, rows),
        check_vma=False,
    )
```

```python
import functools

import jax
import jax.numpy as jnp
from jax import lax
from jax.experimental import pallas as pl
from jax.experimental.pallas import tpu as pltpu
from jax.sharding import PartitionSpec as P

MODEL_WIDTH = 5120
HEADS = 40
HD = 128
FRAME = 64
NEAR = 2 * FRAME
CHUNK = 512
WIDE = 2 * CHUNK
SCORE_SCALE = HD ** (-0.5) * 1.4426950408889634
ADAPTER_SCALE = MODEL_WIDTH ** (-0.5)
FAR = -1e30
NT = (((1,), (1,)), ((), ()))
NN = (((1,), (0,)), ((), ()))
BF16 = jnp.bfloat16
F32 = jnp.float32
ANY = pl.BlockSpec(memory_space=pl.ANY)
SMEM = pl.BlockSpec(memory_space=pltpu.SMEM)
VMEM = pl.BlockSpec(memory_space=pltpu.VMEM)


def dot(a, b, dims):
    return lax.dot_general(a, b, dims, preferred_element_type=F32)


def clip_bias(lo, hi):
    position = lax.broadcasted_iota(jnp.int32, (NEAR, NEAR), 1)
    return jnp.where(position < hi - lo, 0.0, FAR).astype(F32)


def diagonal(top, bottom):
    zeros = jnp.zeros((FRAME, NEAR), BF16)
    return jnp.concatenate(
        [jnp.concatenate([top, zeros], axis=1), jnp.concatenate([zeros, bottom], axis=1)]
    )


def attend(loads):
    ones = jnp.ones((NEAR, HD), BF16)
    scores = []
    for load_q, load_k, _, bias in loads:
        q = load_q()
        scores.append(dot(diagonal(q[:, :HD], q[:, HD:]), load_k(), NT) * SCORE_SCALE + bias)
    weights = [jnp.exp2(s - jnp.max(s, axis=-1, keepdims=True)).astype(BF16) for s in scores]
    results = []
    for w, (_, _, load_v, _) in zip(weights, loads):
        v = load_v()
        values = jnp.concatenate(
            [jnp.concatenate([v[:, at : at + HD], ones], axis=1) for at in (0, HD)]
        )
        mixed = dot(diagonal(w[:FRAME], w[FRAME:]), values, NN)
        mixed = (mixed[:, :HD] * (1.0 / mixed[:, HD:])).astype(BF16)
        results.append(jnp.concatenate([mixed[:FRAME], mixed[FRAME:]], axis=1))
    return results


def inner_kernel(lo_ref, hi_ref, q_ref, k_ref, v_ref, o_ref):
    rows = q_ref.shape[0]
    base = lax.axis_index("seq") * rows
    loads, targets = [], []
    for row in (FRAME, NEAR):
        lo, hi = lo_ref[row], hi_ref[row]
        keys = pl.ds(pl.multiple_of(lo - base, FRAME), NEAR)
        bias = clip_bias(lo, hi)
        for col in range(0, WIDE, 2 * HD):
            part = slice(col, col + 2 * HD)
            targets.append((slice(row - FRAME, row), part))
            loads.append(
                (
                    lambda row=row, part=part: q_ref[row : row + FRAME, part],
                    lambda keys=keys, part=part: k_ref[keys, part],
                    lambda keys=keys, part=part: v_ref[keys, part],
                    bias,
                )
            )
    for target, result in zip(targets, attend(loads)):
        o_ref[target] = result


def inner_attention(lo, hi, q, k, v):
    rows, width = q.shape
    block = pl.BlockSpec((rows, WIDE), lambda i: (0, i))
    return pl.pallas_call(
        inner_kernel,
        grid=(width // WIDE,),
        out_shape=jax.ShapeDtypeStruct((NEAR, width), BF16),
        in_specs=[SMEM, SMEM, block, block, block],
        out_specs=pl.BlockSpec((NEAR, WIDE), lambda i: (0, i)),
        compiler_params=pltpu.CompilerParams(vmem_limit_bytes=16 << 20),
        cost_estimate=pl.CostEstimate(
            flops=16 * NEAR * NEAR * width,
            bytes_accessed=7 * rows * width,
            transcendentals=NEAR * NEAR * HEADS,
        ),
        name="inner_attention",
    )(lo, hi, q, k, v)


def edge_side(is_near, rows):
    right = lax.rem(lax.axis_index("seq"), 2) == (0 if is_near else 1)
    return right, pl.multiple_of(jnp.where(right, rows - FRAME, 0), FRAME)


def attend_edge(is_near, lo_ref, hi_ref, q, k, v, halos, out):
    rows, width = q.shape
    pairs = width // (2 * HD)
    unroll = next(n for n in (10, 8, 6, 5, 4, 2, 1) if pairs % n == 0)
    me = lax.axis_index("seq")
    base = me * rows
    right, row = edge_side(is_near, rows)
    first = pl.multiple_of(jnp.where(right, rows - NEAR, 0), NEAR)
    second = pl.multiple_of(first + FRAME, FRAME)
    lo, hi = lo_ref[row], hi_ref[row]
    before = lo < base
    after = jnp.logical_and(right, lo == base + rows - FRAME)
    direct = lax.rem(lax.div(me + 1, 2), 2) == 1

    def window(ref, kind, part):
        halo = halos[kind][:, part]
        if len(halos) == 4:
            halo = jnp.where(direct, halo, halos[2 + kind][:, part])
        one, two = ref[pl.ds(first, FRAME), part], ref[pl.ds(second, FRAME), part]
        return jnp.concatenate(
            [
                jnp.where(before, halo, jnp.where(after, two, one)),
                jnp.where(before, one, jnp.where(after, halo, two)),
            ]
        )

    bias = clip_bias(lo, hi)

    def step(i, _):
        loads, parts = [], []
        for pair in range(unroll):
            part = pl.ds(pl.multiple_of((i * unroll + pair) * 2 * HD, 2 * HD), 2 * HD)
            parts.append(part)
            loads.append(
                (
                    lambda part=part: q[pl.ds(row, FRAME), part],
                    lambda part=part: window(k, 0, part),
                    lambda part=part: window(v, 1, part),
                    bias,
                )
            )
        for part, result in zip(parts, attend(loads)):
            out[:, part] = result
        return 0

    lax.fori_loop(0, pairs // unroll, step, 0)


def near_kernel(lo_ref, hi_ref, q, k, v, halo, out):
    attend_edge(True, lo_ref, hi_ref, q, k, v, (halo.at[0], halo.at[1]), out)


def edge_cost(rows, width):
    return pl.CostEstimate(
        flops=8 * NEAR * NEAR * width,
        bytes_accessed=7 * rows * width,
        transcendentals=FRAME * NEAR * HEADS,
    )


def near_attention(lo, hi, q, k, v, halo):
    rows, width = q.shape
    return pl.pallas_call(
        near_kernel,
        out_shape=jax.ShapeDtypeStruct((FRAME, width), BF16),
        in_specs=[SMEM, SMEM] + [VMEM] * 4,
        out_specs=VMEM,
        compiler_params=pltpu.CompilerParams(vmem_limit_bytes=20 << 20),
        cost_estimate=edge_cost(rows, width),
        name="near_edge_attention",
    )(lo, hi, q, k, v, halo)


def adapt(value, narrow, factor):
    return (value.astype(F32) + ADAPTER_SCALE * dot(narrow, factor, NT)).astype(BF16)


def merge_kernel(layout, frozen, own_down, inner, near, *rest):
    refs, rest = rest[:-6], rest[-6:]
    merged, attended, factors, w, result, sems = rest
    shard, width = frozen.shape
    rows = result.shape[0]
    me = lax.axis_index("seq")
    kind = lax.axis_index("group")
    for ref, cells in zip(refs, layout):
        for i, (swapped, mask) in enumerate(cells):
            at = pl.ds(pl.multiple_of((me ^ mask) * shard, shard), shard)
            factors[1 - kind if swapped else kind, at, :] = ref[i]
    if not layout:
        factors[...] = refs[0][...]
    down, up = factors.at[0], factors.at[1]
    _, near_row = edge_side(True, rows)
    parts = ((inner, FRAME), (near, near_row))
    reduced = [dot(att[...], down[...], NN).astype(BF16) for att, _ in parts]
    stores = []

    def store(source, target):
        stores.append(pltpu.make_async_copy(source, target, sems.at[len(stores)]))
        stores[-1].start()

    for first in range(0, width, CHUNK):
        part = pl.ds(first, CHUNK)
        factor = up[part, :]
        w[:, part] = adapt(frozen[:, part], own_down[...], factor)
        store(w.at[:, part], merged.at[:, part])
        for narrow, (att, row) in zip(reduced, parts):
            result[pl.ds(row, att.shape[0]), part] = adapt(att[:, part], narrow, factor)
            at = (pl.ds(row, att.shape[0]), part)
            store(result.at[at], attended.at[at])
    for copy in stores:
        copy.wait()


def merge(frozen, own_down, inner, near, layout, pieces):
    shard, width = frozen.shape
    rank = own_down.shape[1]
    rows = 2 * NEAR
    return pl.pallas_call(
        functools.partial(merge_kernel, layout),
        out_shape=(
            jax.ShapeDtypeStruct((shard, width), BF16),
            jax.ShapeDtypeStruct((rows, width), BF16),
            jax.ShapeDtypeStruct((2, width, rank), BF16),
        ),
        in_specs=[VMEM] * (4 + len(pieces)),
        out_specs=(ANY, ANY, VMEM),
        scratch_shapes=[
            pltpu.VMEM((shard, width), BF16),
            pltpu.VMEM((rows, width), BF16),
            pltpu.SemaphoreType.DMA((3 * (width // CHUNK),)),
        ],
        compiler_params=pltpu.CompilerParams(vmem_limit_bytes=24 << 20),
        cost_estimate=pl.CostEstimate(
            flops=2 * (shard + 2 * rows) * width * rank,
            bytes_accessed=4 * (shard + rows) * width + 4 * width * rank,
            transcendentals=0,
        ),
        name="merge_and_adapter",
    )(frozen, own_down, inner, near, *pieces)


def far_kernel(lo_ref, hi_ref, q, k, v, *rest):
    halos, (factors, _, out, mixed, result, sems) = rest[:3], rest[3:]
    rows, width = q.shape
    halos = (*halos[:2], halos[2].at[0], halos[2].at[1])
    attend_edge(False, lo_ref, hi_ref, q, k, v, halos, mixed)
    narrow = dot(mixed[...], factors[0], NN).astype(BF16)
    _, row = edge_side(False, rows)
    stores = []
    for first in range(0, width, WIDE):
        part = pl.ds(first, WIDE)
        result[:, part] = adapt(mixed[:, part], narrow, factors[1, part, :])
        stores.append(
            pltpu.make_async_copy(
                result.at[:, part], out.at[pl.ds(row, FRAME), part], sems.at[len(stores)]
            )
        )
        stores[-1].start()
    for copy in stores:
        copy.wait()


def far_rows(lo, hi, q, k, v, direct, distant, factors, attended):
    rows, width = q.shape
    return pl.pallas_call(
        far_kernel,
        out_shape=jax.ShapeDtypeStruct((rows, width), BF16),
        in_specs=[SMEM, SMEM] + [VMEM] * 7 + [ANY],
        out_specs=ANY,
        input_output_aliases={9: 0},
        scratch_shapes=[
            pltpu.VMEM((FRAME, width), BF16),
            pltpu.VMEM((FRAME, width), BF16),
            pltpu.SemaphoreType.DMA((width // WIDE,)),
        ],
        compiler_params=pltpu.CompilerParams(vmem_limit_bytes=24 << 20),
        cost_estimate=edge_cost(rows, width),
        name="far_edge_rows",
    )(lo, hi, q, k, v, *direct, distant, factors, attended)


def body(q, k, v, lo, hi, down, up, frozen):
    count = lax.axis_size("seq")
    rows = k.shape[0]
    odd = lax.rem(lax.axis_index("seq"), 2)

    def rim(start):
        return [lax.dynamic_slice_in_dim(x, start, FRAME, 0) for x in (k, v)]

    def send(cells, pairs):
        return [lax.ppermute(x, "seq", pairs) for x in cells]

    def swap(cells, mask):
        return lax.ppermute(cells, "seq", [(i, i ^ mask) for i in range(count)])

    def cross(cells):
        return lax.ppermute(cells, "group", [(0, 1), (1, 0)])

    direct_pairs, distant_pairs = (
        [(i + a, i + 1 - a) for i in range(first, count - 1, 4) for a in (0, 1)]
        for first in (1, 3)
    )
    far_rim = rim(odd * (rows - FRAME))
    near_rim = jnp.stack(rim((1 - odd) * (rows - FRAME)))
    up = up.T
    steps = [1 << bit for bit in range(1, count.bit_length() - 1)]
    if lax.axis_size("group") != 2 or len(steps) != 3 or down.shape[0] % 32:
        both = lax.all_gather(jnp.stack([down, up]), "seq", axis=1, tiled=True)
        layout, pieces = [], [both]
        direct = send(far_rim, direct_pairs)
        distant = lax.ppermute(jnp.stack(far_rim), "seq", distant_pairs)
        inner = inner_attention(lo, hi, q, k, v)
        near = near_attention(lo, hi, q, k, v, swap(near_rim, 1))
    else:
        barrier = lax.optimization_barrier
        join = jnp.concatenate
        side, short, long = steps
        own = join([down, up])[None]
        first = lax.axis_index("group") == 0
        shard = down.shape[0]
        direct = send(far_rim, direct_pairs)
        plane = join([own, swap(own, side)])
        plane, near_rim = barrier((plane, near_rim))
        halo = swap(near_rim, 1)
        halves = plane[:, :shard], plane[:, shard:]
        plane = jnp.where(first, *halves)
        crossed = [jnp.where(first, *halves[::-1])]
        beyond = swap(plane, long)
        beside = swap(plane, short)
        beyond, beside = barrier((beyond, beside))
        last = swap(beyond, short)
        far_rim, direct, last, lo_near = barrier((far_rim, direct, last, lo))
        distant = lax.ppermute(jnp.stack(far_rim), "seq", distant_pairs)
        crossed.append(cross(join([beside, beyond])))
        inner = inner_attention(lo_near, hi, q, k, v)
        near = near_attention(lo_near, hi, q, k, v, halo)
        crossed.append(cross(last))
        masks = [a ^ b for a in (0, short, long) for b in (0, side)]
        late_masks = [short ^ long ^ b for b in (0, side)]
        early = join([plane, beside, beyond, *crossed[:2]])
        late, inner, near = barrier((join([last, crossed[2]]), inner, near))
        pieces = [early, swap(early, 1), late, swap(late, 1)]
        layout = [
            [(kind, mask ^ core) for kind in (0, 1) for mask in group]
            for group in (masks, late_masks)
            for core in (0, 1)
        ]
    merged, attended, factors = merge(frozen, down, inner, near, layout, pieces)
    attended = far_rows(lo, hi, q, k, v, direct, distant, factors, attended)
    return (attended, merged)


def solution(mesh):
    rows = P(("group", "seq"), None)
    flat = P(("group", "seq"))
    return jax.shard_map(
        body,
        mesh=mesh,
        in_specs=(rows, rows, rows, flat, flat, P("seq", None), P(None, "seq"), P("seq", None)),
        out_specs=(rows, rows),
        check_vma=False,
    )
```

```python
import functools

import jax
import jax.numpy as jnp
from jax import lax
from jax.experimental import pallas as pl
from jax.experimental.pallas import tpu as pltpu
from jax.sharding import PartitionSpec as P

MODEL_WIDTH = 5120
HEADS = 40
HD = 128
FRAME = 64
NEAR = 2 * FRAME
CHUNK = 512
WIDE = 2 * CHUNK
SCORE_SCALE = HD ** (-0.5) * 1.4426950408889634
ADAPTER_SCALE = MODEL_WIDTH ** (-0.5)
FAR = -1e30
NT = (((1,), (1,)), ((), ()))
NN = (((1,), (0,)), ((), ()))
BF16 = jnp.bfloat16
F32 = jnp.float32
ANY = pl.BlockSpec(memory_space=pl.ANY)
SMEM = pl.BlockSpec(memory_space=pltpu.SMEM)
VMEM = pl.BlockSpec(memory_space=pltpu.VMEM)


def dot(a, b, dims):
    return lax.dot_general(a, b, dims, preferred_element_type=F32)


def clip_bias(lo, hi):
    position = lax.broadcasted_iota(jnp.int32, (NEAR, NEAR), 1)
    return jnp.where(position < hi - lo, 0.0, FAR).astype(F32)


def diagonal(top, bottom):
    zeros = jnp.zeros((FRAME, NEAR), BF16)
    return jnp.concatenate(
        [jnp.concatenate([top, zeros], axis=1), jnp.concatenate([zeros, bottom], axis=1)]
    )


def attend(loads):
    ones = jnp.ones((NEAR, HD), BF16)
    scores = []
    for load_q, load_k, _, bias in loads:
        q = load_q()
        scores.append(dot(diagonal(q[:, :HD], q[:, HD:]), load_k(), NT) * SCORE_SCALE + bias)
    weights = [jnp.exp2(s - jnp.max(s, axis=-1, keepdims=True)).astype(BF16) for s in scores]
    results = []
    for w, (_, _, load_v, _) in zip(weights, loads):
        v = load_v()
        values = jnp.concatenate(
            [jnp.concatenate([v[:, at : at + HD], ones], axis=1) for at in (0, HD)]
        )
        mixed = dot(diagonal(w[:FRAME], w[FRAME:]), values, NN)
        mixed = (mixed[:, :HD] * (1.0 / mixed[:, HD:])).astype(BF16)
        results.append(jnp.concatenate([mixed[:FRAME], mixed[FRAME:]], axis=1))
    return results


def inner_kernel(lo_ref, hi_ref, q_ref, k_ref, v_ref, o_ref):
    rows = q_ref.shape[0]
    base = lax.axis_index("seq") * rows
    loads, targets = [], []
    for row in (FRAME, NEAR):
        lo, hi = lo_ref[row], hi_ref[row]
        keys = pl.ds(pl.multiple_of(lo - base, FRAME), NEAR)
        bias = clip_bias(lo, hi)
        for col in range(0, WIDE, 2 * HD):
            part = slice(col, col + 2 * HD)
            targets.append((slice(row - FRAME, row), part))
            loads.append(
                (
                    lambda row=row, part=part: q_ref[row : row + FRAME, part],
                    lambda keys=keys, part=part: k_ref[keys, part],
                    lambda keys=keys, part=part: v_ref[keys, part],
                    bias,
                )
            )
    for target, result in zip(targets, attend(loads)):
        o_ref[target] = result


def inner_attention(lo, hi, q, k, v):
    rows, width = q.shape
    block = pl.BlockSpec((rows, WIDE), lambda i: (0, i))
    return pl.pallas_call(
        inner_kernel,
        grid=(width // WIDE,),
        out_shape=jax.ShapeDtypeStruct((NEAR, width), BF16),
        in_specs=[SMEM, SMEM, block, block, block],
        out_specs=pl.BlockSpec((NEAR, WIDE), lambda i: (0, i)),
        compiler_params=pltpu.CompilerParams(vmem_limit_bytes=16 << 20),
        cost_estimate=pl.CostEstimate(
            flops=16 * NEAR * NEAR * width,
            bytes_accessed=7 * rows * width,
            transcendentals=NEAR * NEAR * HEADS,
        ),
        name="inner_attention",
    )(lo, hi, q, k, v)


def edge_side(is_near, rows):
    right = lax.rem(lax.axis_index("seq"), 2) == (0 if is_near else 1)
    return right, pl.multiple_of(jnp.where(right, rows - FRAME, 0), FRAME)


def attend_edge(is_near, lo_ref, hi_ref, q, k, v, halos, out):
    rows, width = q.shape
    pairs = width // (2 * HD)
    unroll = next(n for n in (10, 8, 6, 5, 4, 2, 1) if pairs % n == 0)
    me = lax.axis_index("seq")
    base = me * rows
    right, row = edge_side(is_near, rows)
    first = pl.multiple_of(jnp.where(right, rows - NEAR, 0), NEAR)
    second = pl.multiple_of(first + FRAME, FRAME)
    lo, hi = lo_ref[row], hi_ref[row]
    before = lo < base
    after = jnp.logical_and(right, lo == base + rows - FRAME)
    direct = lax.rem(lax.div(me + 1, 2), 2) == 1

    def window(ref, kind, part):
        halo = halos[kind][:, part]
        if len(halos) == 4:
            halo = jnp.where(direct, halo, halos[2 + kind][:, part])
        one, two = ref[pl.ds(first, FRAME), part], ref[pl.ds(second, FRAME), part]
        return jnp.concatenate(
            [
                jnp.where(before, halo, jnp.where(after, two, one)),
                jnp.where(before, one, jnp.where(after, halo, two)),
            ]
        )

    bias = clip_bias(lo, hi)

    for i in range(pairs // unroll):
        loads, parts = [], []
        for pair in range(unroll):
            part = pl.ds((i * unroll + pair) * 2 * HD, 2 * HD)
            parts.append(part)
            loads.append(
                (
                    lambda part=part: q[pl.ds(row, FRAME), part],
                    lambda part=part: window(k, 0, part),
                    lambda part=part: window(v, 1, part),
                    bias,
                )
            )
        for part, result in zip(parts, attend(loads)):
            out[:, part] = result


def near_kernel(lo_ref, hi_ref, q, k, v, halo, out):
    attend_edge(True, lo_ref, hi_ref, q, k, v, (halo.at[0], halo.at[1]), out)


def edge_cost(rows, width):
    return pl.CostEstimate(
        flops=8 * NEAR * NEAR * width,
        bytes_accessed=7 * rows * width,
        transcendentals=FRAME * NEAR * HEADS,
    )


def near_attention(lo, hi, q, k, v, halo):
    rows, width = q.shape
    return pl.pallas_call(
        near_kernel,
        out_shape=jax.ShapeDtypeStruct((FRAME, width), BF16),
        in_specs=[SMEM, SMEM] + [VMEM] * 4,
        out_specs=VMEM,
        compiler_params=pltpu.CompilerParams(vmem_limit_bytes=20 << 20),
        cost_estimate=edge_cost(rows, width),
        name="near_edge_attention",
    )(lo, hi, q, k, v, halo)


def adapt(value, narrow, factor):
    return (value.astype(F32) + ADAPTER_SCALE * dot(narrow, factor, NT)).astype(BF16)


def merge_kernel(layout, frozen, own_down, inner, near, *rest):
    refs, rest = rest[:-6], rest[-6:]
    merged, attended, factors, w, result, sems = rest
    shard, width = frozen.shape
    rows = result.shape[0]
    me = lax.axis_index("seq")
    kind = lax.axis_index("group")
    for ref, (swapped, masks) in zip(refs, layout):
        target = 1 - kind if swapped else kind
        for i, mask in enumerate(masks):
            at = pl.ds(pl.multiple_of((me ^ mask) * shard, shard), shard)
            factors[target, at, :] = ref[i]
    if not layout:
        factors[...] = refs[0][...]
    down, up = factors.at[0], factors.at[1]
    _, near_row = edge_side(True, rows)
    parts = ((inner, FRAME), (near, near_row))
    reduced = [dot(att[...], down[...], NN).astype(BF16) for att, _ in parts]
    stores = []

    def store(source, target):
        stores.append(pltpu.make_async_copy(source, target, sems.at[len(stores)]))
        stores[-1].start()

    for first in range(0, width, WIDE):
        part = pl.ds(first, WIDE)
        factor = up[part, :]
        w[:, part] = adapt(frozen[:, part], own_down[...], factor)
        store(w.at[:, part], merged.at[:, part])
        for narrow, (att, row) in zip(reduced, parts):
            result[pl.ds(row, att.shape[0]), part] = adapt(att[:, part], narrow, factor)
            at = (pl.ds(row, att.shape[0]), part)
            store(result.at[at], attended.at[at])
    for copy in stores:
        copy.wait()


def merge(frozen, own_down, inner, near, layout, pieces):
    shard, width = frozen.shape
    rank = own_down.shape[1]
    rows = 2 * NEAR
    return pl.pallas_call(
        functools.partial(merge_kernel, layout),
        out_shape=(
            jax.ShapeDtypeStruct((shard, width), BF16),
            jax.ShapeDtypeStruct((rows, width), BF16),
            jax.ShapeDtypeStruct((2, width, rank), BF16),
        ),
        in_specs=[VMEM] * (4 + len(pieces)),
        out_specs=(ANY, ANY, VMEM),
        scratch_shapes=[
            pltpu.VMEM((shard, width), BF16),
            pltpu.VMEM((rows, width), BF16),
            pltpu.SemaphoreType.DMA((3 * (width // CHUNK),)),
        ],
        compiler_params=pltpu.CompilerParams(vmem_limit_bytes=24 << 20),
        cost_estimate=pl.CostEstimate(
            flops=2 * (shard + 2 * rows) * width * rank,
            bytes_accessed=4 * (shard + rows) * width + 4 * width * rank,
            transcendentals=0,
        ),
        name="merge_and_adapter",
    )(frozen, own_down, inner, near, *pieces)


def far_kernel(lo_ref, hi_ref, q, k, v, *rest):
    halos, (factors, _, out, mixed, result, sems) = rest[:3], rest[3:]
    rows, width = q.shape
    halos = (*halos[:2], halos[2].at[0], halos[2].at[1])
    attend_edge(False, lo_ref, hi_ref, q, k, v, halos, mixed)
    narrow = dot(mixed[...], factors[0], NN).astype(BF16)
    _, row = edge_side(False, rows)
    stores = []
    for first in range(0, width, WIDE):
        part = pl.ds(first, WIDE)
        result[:, part] = adapt(mixed[:, part], narrow, factors[1, part, :])
        stores.append(
            pltpu.make_async_copy(
                result.at[:, part], out.at[pl.ds(row, FRAME), part], sems.at[len(stores)]
            )
        )
        stores[-1].start()
    for copy in stores:
        copy.wait()


def far_rows(lo, hi, q, k, v, direct, distant, factors, attended):
    rows, width = q.shape
    return pl.pallas_call(
        far_kernel,
        out_shape=jax.ShapeDtypeStruct((rows, width), BF16),
        in_specs=[SMEM, SMEM] + [VMEM] * 7 + [ANY],
        out_specs=ANY,
        input_output_aliases={9: 0},
        scratch_shapes=[
            pltpu.VMEM((FRAME, width), BF16),
            pltpu.VMEM((FRAME, width), BF16),
            pltpu.SemaphoreType.DMA((width // WIDE,)),
        ],
        compiler_params=pltpu.CompilerParams(vmem_limit_bytes=24 << 20),
        cost_estimate=edge_cost(rows, width),
        name="far_edge_rows",
    )(lo, hi, q, k, v, *direct, distant, factors, attended)


def body(q, k, v, lo, hi, down, up, frozen):
    count = lax.axis_size("seq")
    rows = k.shape[0]
    odd = lax.rem(lax.axis_index("seq"), 2)

    def rim(start):
        return [lax.dynamic_slice_in_dim(x, start, FRAME, 0) for x in (k, v)]

    def send(cells, pairs):
        return [lax.ppermute(x, "seq", pairs) for x in cells]

    def swap(cells, mask):
        return lax.ppermute(cells, "seq", [(i, i ^ mask) for i in range(count)])

    def cross(cells):
        return lax.ppermute(cells, "group", [(0, 1), (1, 0)])

    direct_pairs, distant_pairs = (
        [(i + a, i + 1 - a) for i in range(first, count - 1, 4) for a in (0, 1)]
        for first in (1, 3)
    )
    far_rim = rim(odd * (rows - FRAME))
    near_rim = jnp.stack(rim((1 - odd) * (rows - FRAME)))
    up = up.T
    steps = [1 << bit for bit in range(1, count.bit_length() - 1)]
    if lax.axis_size("group") != 2 or len(steps) != 3 or down.shape[0] % 32:
        both = lax.all_gather(jnp.stack([down, up]), "seq", axis=1, tiled=True)
        layout, pieces = [], [both]
        direct = send(far_rim, direct_pairs)
        distant = lax.ppermute(jnp.stack(far_rim), "seq", distant_pairs)
        inner = inner_attention(lo, hi, q, k, v)
        near = near_attention(lo, hi, q, k, v, swap(near_rim, 1))
    else:
        barrier = lax.optimization_barrier
        join = jnp.concatenate
        side, short, long = steps
        own = jnp.where(lax.axis_index("group") == 0, down, up)[None]
        plane = join([own, swap(own, side)])
        direct = send(far_rim, direct_pairs)
        plane, near_rim = barrier((plane, near_rim))
        halo = swap(near_rim, 1)
        beyond = swap(plane, long)
        beside = swap(plane, short)
        crossed = [cross(plane)]
        beyond, beside, crossed = barrier((beyond, beside, crossed))
        far_rim, direct, lo_later = barrier((far_rim, direct, lo))
        last = swap(beyond, short)
        distant = lax.ppermute(jnp.stack(far_rim), "seq", distant_pairs)
        crossed.append(cross(join([beside, beyond])))
        inner = inner_attention(lo_later, hi, q, k, v)
        near = near_attention(lo_later, hi, q, k, v, halo)
        last, inner, near = barrier((last, inner, near))
        crossed.append(cross(last))
        cells, other = join([plane, beside, beyond, last]), join(crossed)
        masks = [a ^ b for a in (0, short, long, short ^ long) for b in (0, side)]
        across = [mask ^ 1 for mask in masks]
        layout = [(0, masks), (0, across), (1, masks), (1, across)]
        pieces = [cells, swap(cells, 1), other, swap(other, 1)]
    merged, attended, factors = merge(frozen, down, inner, near, layout, pieces)
    attended = far_rows(lo, hi, q, k, v, direct, distant, factors, attended)
    return (attended, merged)


def solution(mesh):
    rows = P(("group", "seq"), None)
    flat = P(("group", "seq"))
    return jax.shard_map(
        body,
        mesh=mesh,
        in_specs=(rows, rows, rows, flat, flat, P("seq", None), P(None, "seq"), P("seq", None)),
        out_specs=(rows, rows),
        check_vma=False,
    )
```

```python
import functools

import jax
import jax.numpy as jnp
from jax import lax
from jax.experimental import pallas as pl
from jax.experimental.pallas import tpu as pltpu
from jax.sharding import PartitionSpec as P

MODEL_WIDTH = 5120
HEADS = 40
HD = 128
FRAME = 64
NEAR = 2 * FRAME
CHUNK = 512
WIDE = 2 * CHUNK
SCORE_SCALE = HD ** (-0.5) * 1.4426950408889634
ADAPTER_SCALE = MODEL_WIDTH ** (-0.5)
FAR = -1e30
NT = (((1,), (1,)), ((), ()))
NN = (((1,), (0,)), ((), ()))
BF16 = jnp.bfloat16
F32 = jnp.float32
ANY = pl.BlockSpec(memory_space=pl.ANY)
SMEM = pl.BlockSpec(memory_space=pltpu.SMEM)
VMEM = pl.BlockSpec(memory_space=pltpu.VMEM)


def dot(a, b, dims):
    return lax.dot_general(a, b, dims, preferred_element_type=F32)


def clip_bias(lo, hi):
    position = lax.broadcasted_iota(jnp.int32, (NEAR, NEAR), 1)
    return jnp.where(position < hi - lo, 0.0, FAR).astype(F32)


def diagonal(top, bottom):
    zeros = jnp.zeros((FRAME, NEAR), BF16)
    return jnp.concatenate(
        [jnp.concatenate([top, zeros], axis=1), jnp.concatenate([zeros, bottom], axis=1)]
    )


def attend(loads):
    ones = jnp.ones((NEAR, HD), BF16)
    scores = []
    for load_q, load_k, _, bias in loads:
        q = load_q()
        scores.append(dot(diagonal(q[:, :HD], q[:, HD:]), load_k(), NT) * SCORE_SCALE + bias)
    weights = [jnp.exp2(s - jnp.max(s, axis=-1, keepdims=True)).astype(BF16) for s in scores]
    results = []
    for w, (_, _, load_v, _) in zip(weights, loads):
        v = load_v()
        values = jnp.concatenate(
            [jnp.concatenate([v[:, at : at + HD], ones], axis=1) for at in (0, HD)]
        )
        mixed = dot(diagonal(w[:FRAME], w[FRAME:]), values, NN)
        mixed = (mixed[:, :HD] * (1.0 / mixed[:, HD:])).astype(BF16)
        results.append(jnp.concatenate([mixed[:FRAME], mixed[FRAME:]], axis=1))
    return results


def inner_kernel(lo_ref, hi_ref, q_ref, k_ref, v_ref, o_ref):
    rows, width = q_ref.shape
    base = lax.axis_index("seq") * rows
    for row in (FRAME, NEAR):
        lo, hi = lo_ref[row], hi_ref[row]
        keys = pl.ds(pl.multiple_of(lo - base, FRAME), NEAR)
        bias = clip_bias(lo, hi)
        for first in range(0, width, width // 2):
            loads, parts = [], []
            for col in range(first, first + width // 2, 2 * HD):
                part = slice(col, col + 2 * HD)
                parts.append(part)
                loads.append(
                    (
                        lambda row=row, part=part: q_ref[row : row + FRAME, part],
                        lambda keys=keys, part=part: k_ref[keys, part],
                        lambda keys=keys, part=part: v_ref[keys, part],
                        bias,
                    )
                )
            for part, result in zip(parts, attend(loads)):
                o_ref[row - FRAME : row, part] = result


def inner_attention(lo, hi, q, k, v):
    rows, width = q.shape
    return pl.pallas_call(
        inner_kernel,
        out_shape=jax.ShapeDtypeStruct((NEAR, width), BF16),
        in_specs=[SMEM, SMEM] + [VMEM] * 3,
        out_specs=VMEM,
        compiler_params=pltpu.CompilerParams(vmem_limit_bytes=20 << 20),
        cost_estimate=pl.CostEstimate(
            flops=16 * NEAR * NEAR * width,
            bytes_accessed=7 * rows * width,
            transcendentals=NEAR * NEAR * HEADS,
        ),
        name="inner_attention",
    )(lo, hi, q, k, v)


def edge_side(is_near, rows):
    right = lax.rem(lax.axis_index("seq"), 2) == (0 if is_near else 1)
    return right, pl.multiple_of(jnp.where(right, rows - FRAME, 0), FRAME)


def attend_edge(is_near, lo_ref, hi_ref, q, k, v, halos, out):
    rows, width = q.shape
    pairs = width // (2 * HD)
    unroll = next(n for n in (10, 8, 6, 5, 4, 2, 1) if pairs % n == 0)
    me = lax.axis_index("seq")
    base = me * rows
    right, row = edge_side(is_near, rows)
    first = pl.multiple_of(jnp.where(right, rows - NEAR, 0), NEAR)
    second = pl.multiple_of(first + FRAME, FRAME)
    lo, hi = lo_ref[row], hi_ref[row]
    before = lo < base
    after = jnp.logical_and(right, lo == base + rows - FRAME)
    direct = lax.rem(lax.div(me + 1, 2), 2) == 1

    def window(ref, kind, part):
        halo = halos[kind][:, part]
        if len(halos) == 4:
            halo = jnp.where(direct, halo, halos[2 + kind][:, part])
        one, two = ref[pl.ds(first, FRAME), part], ref[pl.ds(second, FRAME), part]
        return jnp.concatenate(
            [
                jnp.where(before, halo, jnp.where(after, two, one)),
                jnp.where(before, one, jnp.where(after, halo, two)),
            ]
        )

    bias = clip_bias(lo, hi)

    for i in range(pairs // unroll):
        loads, parts = [], []
        for pair in range(unroll):
            part = pl.ds((i * unroll + pair) * 2 * HD, 2 * HD)
            parts.append(part)
            loads.append(
                (
                    lambda part=part: q[pl.ds(row, FRAME), part],
                    lambda part=part: window(k, 0, part),
                    lambda part=part: window(v, 1, part),
                    bias,
                )
            )
        for part, result in zip(parts, attend(loads)):
            out[:, part] = result


def near_kernel(lo_ref, hi_ref, q, k, v, halo, out):
    attend_edge(True, lo_ref, hi_ref, q, k, v, (halo.at[0], halo.at[1]), out)


def edge_cost(rows, width):
    return pl.CostEstimate(
        flops=8 * NEAR * NEAR * width,
        bytes_accessed=7 * rows * width,
        transcendentals=FRAME * NEAR * HEADS,
    )


def near_attention(lo, hi, q, k, v, halo):
    rows, width = q.shape
    return pl.pallas_call(
        near_kernel,
        out_shape=jax.ShapeDtypeStruct((FRAME, width), BF16),
        in_specs=[SMEM, SMEM] + [VMEM] * 4,
        out_specs=VMEM,
        compiler_params=pltpu.CompilerParams(vmem_limit_bytes=20 << 20),
        cost_estimate=edge_cost(rows, width),
        name="near_edge_attention",
    )(lo, hi, q, k, v, halo)


def adapt(value, narrow, factor):
    return (value.astype(F32) + ADAPTER_SCALE * dot(narrow, factor, NT)).astype(BF16)


def merge_kernel(layout, frozen, own_down, inner, near, *rest):
    refs, rest = rest[:-6], rest[-6:]
    merged, attended, factors, w, result, sems = rest
    shard, width = frozen.shape
    rows = result.shape[0]
    me = lax.axis_index("seq")
    kind = lax.axis_index("group")
    for ref, (swapped, masks) in zip(refs, layout):
        target = 1 - kind if swapped else kind
        for i, mask in enumerate(masks):
            at = pl.ds(pl.multiple_of((me ^ mask) * shard, shard), shard)
            factors[target, at, :] = ref[i]
    if not layout:
        factors[...] = refs[0][...]
    down, up = factors.at[0], factors.at[1]
    _, near_row = edge_side(True, rows)
    parts = ((inner, FRAME), (near, near_row))
    reduced = [dot(att[...], down[...], NN).astype(BF16) for att, _ in parts]
    stores = []

    def store(source, target):
        stores.append(pltpu.make_async_copy(source, target, sems.at[len(stores)]))
        stores[-1].start()

    for first in range(0, width, WIDE):
        part = pl.ds(first, WIDE)
        factor = up[part, :]
        w[:, part] = adapt(frozen[:, part], own_down[...], factor)
        store(w.at[:, part], merged.at[:, part])
        for narrow, (att, row) in zip(reduced, parts):
            result[pl.ds(row, att.shape[0]), part] = adapt(att[:, part], narrow, factor)
            at = (pl.ds(row, att.shape[0]), part)
            store(result.at[at], attended.at[at])
    for copy in stores:
        copy.wait()


def merge(frozen, own_down, inner, near, layout, pieces):
    shard, width = frozen.shape
    rank = own_down.shape[1]
    rows = 2 * NEAR
    return pl.pallas_call(
        functools.partial(merge_kernel, layout),
        out_shape=(
            jax.ShapeDtypeStruct((shard, width), BF16),
            jax.ShapeDtypeStruct((rows, width), BF16),
            jax.ShapeDtypeStruct((2, width, rank), BF16),
        ),
        in_specs=[VMEM] * (4 + len(pieces)),
        out_specs=(ANY, ANY, VMEM),
        scratch_shapes=[
            pltpu.VMEM((shard, width), BF16),
            pltpu.VMEM((rows, width), BF16),
            pltpu.SemaphoreType.DMA((3 * (width // CHUNK),)),
        ],
        compiler_params=pltpu.CompilerParams(vmem_limit_bytes=24 << 20),
        cost_estimate=pl.CostEstimate(
            flops=2 * (shard + 2 * rows) * width * rank,
            bytes_accessed=4 * (shard + rows) * width + 4 * width * rank,
            transcendentals=0,
        ),
        name="merge_and_adapter",
    )(frozen, own_down, inner, near, *pieces)


def far_kernel(lo_ref, hi_ref, q, k, v, *rest):
    halos, (factors, _, out, mixed, result, sems) = rest[:3], rest[3:]
    rows, width = q.shape
    halos = (*halos[:2], halos[2].at[0], halos[2].at[1])
    attend_edge(False, lo_ref, hi_ref, q, k, v, halos, mixed)
    narrow = dot(mixed[...], factors[0], NN).astype(BF16)
    _, row = edge_side(False, rows)
    stores = []
    for first in range(0, width, WIDE):
        part = pl.ds(first, WIDE)
        result[:, part] = adapt(mixed[:, part], narrow, factors[1, part, :])
        stores.append(
            pltpu.make_async_copy(
                result.at[:, part], out.at[pl.ds(row, FRAME), part], sems.at[len(stores)]
            )
        )
        stores[-1].start()
    for copy in stores:
        copy.wait()


def far_rows(lo, hi, q, k, v, direct, distant, factors, attended):
    rows, width = q.shape
    return pl.pallas_call(
        far_kernel,
        out_shape=jax.ShapeDtypeStruct((rows, width), BF16),
        in_specs=[SMEM, SMEM] + [VMEM] * 7 + [ANY],
        out_specs=ANY,
        input_output_aliases={9: 0},
        scratch_shapes=[
            pltpu.VMEM((FRAME, width), BF16),
            pltpu.VMEM((FRAME, width), BF16),
            pltpu.SemaphoreType.DMA((width // WIDE,)),
        ],
        compiler_params=pltpu.CompilerParams(vmem_limit_bytes=24 << 20),
        cost_estimate=edge_cost(rows, width),
        name="far_edge_rows",
    )(lo, hi, q, k, v, *direct, distant, factors, attended)


def body(q, k, v, lo, hi, down, up, frozen):
    count = lax.axis_size("seq")
    rows = k.shape[0]
    odd = lax.rem(lax.axis_index("seq"), 2)

    def rim(start):
        return [lax.dynamic_slice_in_dim(x, start, FRAME, 0) for x in (k, v)]

    def send(cells, pairs):
        return [lax.ppermute(x, "seq", pairs) for x in cells]

    def swap(cells, mask):
        return lax.ppermute(cells, "seq", [(i, i ^ mask) for i in range(count)])

    def cross(cells):
        return lax.ppermute(cells, "group", [(0, 1), (1, 0)])

    direct_pairs, distant_pairs = (
        [(i + a, i + 1 - a) for i in range(first, count - 1, 4) for a in (0, 1)]
        for first in (1, 3)
    )
    far_rim = rim(odd * (rows - FRAME))
    near_rim = jnp.stack(rim((1 - odd) * (rows - FRAME)))
    up = up.T
    steps = [1 << bit for bit in range(1, count.bit_length() - 1)]
    if lax.axis_size("group") != 2 or len(steps) != 3 or down.shape[0] % 32:
        both = lax.all_gather(jnp.stack([down, up]), "seq", axis=1, tiled=True)
        layout, pieces = [], [both]
        direct = send(far_rim, direct_pairs)
        distant = lax.ppermute(jnp.stack(far_rim), "seq", distant_pairs)
        inner = inner_attention(lo, hi, q, k, v)
        near = near_attention(lo, hi, q, k, v, swap(near_rim, 1))
    else:
        barrier = lax.optimization_barrier
        join = jnp.concatenate
        side, short, long = steps
        own = jnp.where(lax.axis_index("group") == 0, down, up)[None]
        plane = join([own, swap(own, side)])
        direct = send(far_rim, direct_pairs)
        plane, near_rim = barrier((plane, near_rim))
        halo = swap(near_rim, 1)
        beyond = swap(plane, long)
        beside = swap(plane, short)
        crossed = [cross(plane)]
        beyond, beside, crossed = barrier((beyond, beside, crossed))
        far_rim, direct, lo_later = barrier((far_rim, direct, lo))
        last = swap(beyond, short)
        distant = lax.ppermute(jnp.stack(far_rim), "seq", distant_pairs)
        crossed.append(cross(join([beside, beyond])))
        inner = inner_attention(lo_later, hi, q, k, v)
        near = near_attention(lo_later, hi, q, k, v, halo)
        last, inner, near = barrier((last, inner, near))
        crossed.append(cross(last))
        cells, other = join([plane, beside, beyond, last]), join(crossed)
        masks = [a ^ b for a in (0, short, long, short ^ long) for b in (0, side)]
        across = [mask ^ 1 for mask in masks]
        layout = [(0, masks), (0, across), (1, masks), (1, across)]
        pieces = [cells, swap(cells, 1), other, swap(other, 1)]
    merged, attended, factors = merge(frozen, down, inner, near, layout, pieces)
    attended = far_rows(lo, hi, q, k, v, direct, distant, factors, attended)
    return (attended, merged)


def solution(mesh):
    rows = P(("group", "seq"), None)
    flat = P(("group", "seq"))
    return jax.shard_map(
        body,
        mesh=mesh,
        in_specs=(rows, rows, rows, flat, flat, P("seq", None), P(None, "seq"), P("seq", None)),
        out_specs=(rows, rows),
        check_vma=False,
    )
```
